128 devices in a mesh: tm: 16 (over z_hi, x, core), height: 8 (over z_lo, y).
Axes of the slice: x: 4, y: 4, z: 4 (z_hi: 2, z_lo: 2; z = z_hi * 2 + z_lo), core: 2. Of those that a mesh axis runs over, the one named last changes fastest.
Arguments:
- coarse: bfloat16 [8, 32, 128, 256], P('height', 'tm'), may hold values from -360 to 360
- gain: float32 [256], replicated, may hold values from 0.1 to 1.9
- bias: float32 [256], replicated, may hold values from -3 to 3
- weight: bfloat16 [256, 3, 3, 3, 128], replicated, may hold values from -0.078125 to 0.078125
- cotangent: bfloat16 [8, 64, 256, 128], P(None, 'tm', 'height'), may hold values from -0.0390625 to 0.0390625
Outputs:
- decoded: bfloat16 [8, 64, 256, 128], P(None, 'tm', 'height')
- grad_weight: float32 [256, 3, 3, 3, 128], P('tm')
- grad_affine: float32 [2, 256], replicated
The draws below stay inside these ranges and needn't reach their ends.
All inputs are finite; a program needn't handle non-finite values.
Results may differ from the reference program's by a relative error of at most 0.0051.
Values may be sent and summed in bfloat16 or wider, within the bound.
A program may use at most 64 MiB of HBM per device.

```python
import math
import jax
import jax.numpy as jnp
from jax import lax

CIN = 256
COUT = 128
GROUPS = 32
FRAMES = 8
ROWS = 64
COLS = 256


def draw_coarse(key, part):
    key = jax.random.fold_in(key, 11)
    key_base, key_chan = jax.random.split(key, 2)
    shape = (FRAMES, ROWS // 2, COLS // 2, CIN)
    base = jnp.clip(jax.random.normal(key_base, shape, jnp.float32), -4.0, 4.0)
    frame_ramp = 3.0 ** (jnp.arange(FRAMES, dtype=jnp.float32) / max(FRAMES - 1, 1))
    row_ramp = 3.0 ** (jnp.arange(ROWS // 2, dtype=jnp.float32) / max(ROWS // 2 - 1, 1))
    scales = jnp.exp(jax.random.uniform(key_chan, (CIN,), jnp.float32, 0.0, math.log(10.0)))
    return (base * frame_ramp[:, None, None, None] * row_ramp[None, :, None, None] * scales).astype(jnp.bfloat16)


def level_of(own_key, extent, pieces, low, largest):
    level, own = 1.0, jax.random.fold_in(own_key, 6)
    for axis_at, blocks in pieces:
        steps = jnp.exp(jax.random.uniform(jax.random.fold_in(own, axis_at), (blocks,), jnp.float32, low / len(pieces), largest / len(pieces)))
        level = level * jnp.repeat(steps, extent[axis_at] // blocks).reshape([-1 if axis == axis_at else 1 for axis in range(len(extent))])
    return level


def scatter_about(rng, shape, width, bound, shards=(), held_as=jnp.bfloat16):
    level = level_of(rng, shape, shards, -0.22, 0.18) if shards else 1.0
    values = jax.random.normal(rng, shape, jnp.float32) * width * level
    return jnp.minimum(jnp.maximum(values, -bound), bound).astype(held_as)


def setup_inputs(seed: int = 0) -> dict:
    key_list = jax.random.split(jax.random.key(seed), 6)
    coarse = draw_coarse(jax.random.fold_in(key_list[5], 71), 0)
    gain = jnp.clip(1.0 + 0.18 * jax.random.normal(key_list[1], (CIN,), jnp.float32), 0.1, 1.9)
    bias = scatter_about(key_list[2], (CIN,), 0.5, 3.0, (), jnp.float32)
    weight = scatter_about(key_list[3], (CIN, 3, 3, 3, COUT), (27 * CIN) ** -0.5, 0.078125)
    cotangent = scatter_about(key_list[4], (FRAMES, ROWS, COLS, COUT), ((FRAMES * ROWS * COLS) ** -0.5), 0.0390625, ((1, 16), (2, 8)))
    return {"coarse": coarse, "gain": gain, "bias": bias, "weight": weight, "cotangent": cotangent}


EPSILON = 1e-06

def upsample(activation):
    return jnp.repeat(jnp.repeat(activation, 2, axis=1), 2, axis=2)

def reference(coarse, gain, bias, weight, cotangent):
    widened = coarse.astype(jnp.float32)
    grouped = widened.reshape(widened.shape[:3] + (GROUPS, CIN // GROUPS))
    numbers = grouped.shape[0] * grouped.shape[1] * grouped.shape[2] * grouped.shape[4]
    average = lax.optimization_barrier(jnp.sum(grouped, axis=(0, 1, 2, 4))) / numbers
    variance = lax.optimization_barrier(jnp.sum(grouped * grouped, axis=(0, 1, 2, 4))) / numbers - average * average
    inverse = lax.rsqrt(variance + EPSILON)
    normed = ((grouped - average[:, None]) * inverse[:, None]).reshape(widened.shape)
    shifted = normed * gain + bias
    activation = jax.nn.silu(shifted).astype(jnp.bfloat16)
    padded = jnp.pad(upsample(activation), ((2, 0), (1, 1), (1, 1), (0, 0)))
    frames_all, rows_all, cols_all = cotangent.shape[:3]
    flat_cot = cotangent.reshape(-1, COUT)
    cot_padded = jnp.pad(cotangent, ((0, 2), (1, 1), (1, 1), (0, 0)))
    product = jnp.zeros((frames_all * rows_all * cols_all, COUT), jnp.float32)
    grad_up = jnp.zeros((frames_all * rows_all * cols_all, CIN), jnp.float32)
    kernel_terms = []
    for tap_t in range(3):
        for tap_r in range(3):
            for tap_c in range(3):
                window = padded[tap_t:tap_t + frames_all, tap_r:tap_r + rows_all, tap_c:tap_c + cols_all].reshape(-1, CIN)
                kernel = weight[:, tap_t, tap_r, tap_c, :]
                product = product + jnp.dot(window, kernel, preferred_element_type=jnp.float32)
                kernel_terms.append(lax.dot_general(window, flat_cot, (((0,), (0,)), ((), ())), preferred_element_type=jnp.float32))
                cot_window = cot_padded[2 - tap_t:2 - tap_t + frames_all, 2 - tap_r:2 - tap_r + rows_all, 2 - tap_c:2 - tap_c + cols_all].reshape(-1, COUT)
                grad_up = grad_up + lax.dot_general(cot_window, kernel, (((1,), (1,)), ((), ())), preferred_element_type=jnp.float32)
    decoded = product.reshape(cotangent.shape).astype(jnp.bfloat16)
    grad_weight = jnp.stack(kernel_terms, axis=1).reshape(CIN, 3, 3, 3, COUT)
    grad_act = grad_up.reshape(frames_all, rows_all // 2, 2, cols_all // 2, 2, CIN).sum(axis=(2, 4))
    sigmoid_z = jax.nn.sigmoid(shifted)
    grad_shifted = grad_act * sigmoid_z * (1.0 + shifted * (1.0 - sigmoid_z))
    grad_affine = jnp.stack([lax.optimization_barrier(jnp.sum(grad_shifted * normed, axis=(0, 1, 2))), lax.optimization_barrier(jnp.sum(grad_shifted, axis=(0, 1, 2)))])
    return (decoded, grad_weight, grad_affine)
```

```python
import functools

import jax
import jax.numpy as jnp
from jax import lax
from jax.experimental import pallas as pl
from jax.experimental.pallas import tpu as pltpu
from jax.sharding import PartitionSpec as P

MESH = pl.DeviceIdType.MESH
F32, BF16 = jnp.float32, jnp.bfloat16
EPSILON = 1e-06
NUMBERS = 8 * 32 * 128 * 8
CHIPS, HEIGHT = 8, 8

(STATS1, STATS2, BLOCKS, COT_PAIR, COT_ROWS, COT_COLS, X_PAIR, X_ROWS, X_COLS, REDUCE, GATHER, AFF1, AFF2) = range(13)


def group_totals(tile):
    lane = lax.broadcasted_iota(jnp.int32, tile.shape, 1)
    for step in (1, 2, 4):
        other = jnp.where(
            (lane & step) == 0, pltpu.roll(tile, 128 - step, 1), pltpu.roll(tile, step, 1)
        )
        tile = tile + other
    return tile


def kernel(
    coarse, gain, bias, w_hbm, cot, dec, gw, aff,
    w, wsem, wc, st, st1, st2, at, at1, at2,
    xraw, xf, xe, hc, acts, pad0, pad1, a_t,
    cpart, cedge, ce, ch, cf, s_buf, g_buf, r_buf, ag_s, ag_r, d_buf, ssem, rsem,
):
    tm, h = lax.axis_index("tm"), lax.axis_index("height")
    core = lax.rem(tm, 2)
    t = tm // 2
    left, right = lax.rem(h + 7, 8), lax.rem(h + 1, 8)
    t_off = lax.rem(t + 7 + 2 * core, 8)
    pair = tm + 1 - 2 * core

    def send(src, dst, kind, to_tm, to_h):
        pltpu.make_async_remote_copy(
            src_ref=src, dst_ref=dst, send_sem=ssem.at[kind], recv_sem=rsem.at[kind],
            device_id=(to_tm, to_h), device_id_type=MESH,
        ).start()

    def arrived(kind, like):
        pltpu.make_async_copy(like, like, rsem.at[kind]).wait()

    def sent(kind, like):
        pltpu.make_async_copy(like, like, ssem.at[kind]).wait()

    fetch_w = pltpu.make_async_copy(w_hbm, w, wsem)
    fetch_w.start()

    barrier = pltpu.get_barrier_semaphore()

    def greet(to_tm, to_h):
        pl.semaphore_signal(barrier, inc=1, device_id=(to_tm, to_h), device_id_type=MESH)

    @pl.loop(1, 8)
    def _(k):
        greet(tm, lax.rem(h + k, 8))

    @pl.loop(1, 16)
    def _(k):
        greet(lax.rem(tm + k, 16), h)

    greet(pair, left)
    greet(pair, right)

    @pl.loop(0, 4)
    def _(k):
        to_tm = lax.rem(t + 7 + 2 * (k // 2), 8) * 2 + lax.rem(k, 2)
        greet(to_tm, left)
        greet(to_tm, right)

    x = coarse[...].astype(F32).reshape(256, 256)
    total = jnp.sum(x, axis=0, keepdims=True)
    squares = jnp.sum(x * x, axis=0, keepdims=True)
    st[...] = jnp.zeros((8, 128), F32)
    st[0:1, :] = total[:, :128]
    st[1:2, :] = total[:, 128:]
    st[2:3, :] = squares[:, :128]
    st[3:4, :] = squares[:, 128:]

    def cell(j, f):
        return pl.multiple_of((j * 8 + f) * 48, 8)

    for r in range(4):
        for f in range(8):
            cf[pl.ds(cell(1 + 4 * core + r, f) + 8, 32), :] = cot[f, r].astype(F32)
    for r in range(4):
        base = cell(1 + 4 * core + r, 0)
        ce[0, r] = cf[pl.ds(base + 8, 8, stride=48), :]
        ce[1, r] = cf[pl.ds(base + 39, 8, stride=48), :]
    hc[0, 4 - 3 * core] = jnp.zeros((8, 256), F32)
    hc[1, 4 - 3 * core] = jnp.zeros((8, 256), F32)
    acts[:, 0:2] = jnp.zeros((3, 2, 6, 16, 256), BF16)
    s_buf[:, 8:10] = jnp.zeros((9, 2, 4, 16, 128), BF16)

    pl.semaphore_wait(barrier, 32)

    @pl.loop(1, 8)
    def _(k):
        send(st, st1.at[h], STATS1, tm, lax.rem(h + k, 8))

    @pl.loop(1, 8)
    def _(k):
        to_h = lax.rem(h + k, 8)
        send(
            coarse.at[:, pl.ds(pl.multiple_of(to_h * 16, 16), 16), :],
            xraw.at[h, pl.ds(1 + 2 * core, 2)], BLOCKS, tm, to_h,
        )

    send(cot, cpart, COT_PAIR, pair, h)
    for c2 in range(2):
        send(cot.at[:, pl.ds(3 * core, 1)], cedge.at[1 - core], COT_ROWS, t_off * 2 + c2, h)
    for side, to_h in ((0, left), (1, right)):
        for c2 in range(2):
            send(ce.at[side], ch.at[1 - side, pl.ds(1 + 4 * core, 4)], COT_COLS, 2 * t + c2, to_h)
            send(ce.at[side, pl.ds(3 * core, 1)], ch.at[1 - side, pl.ds(9 - 9 * core, 1)], COT_COLS, t_off * 2 + c2, to_h)

    st1[h] = st[...]
    xraw[h, pl.ds(1 + 2 * core, 2)] = coarse[:, pl.ds(pl.multiple_of(h * 16, 16), 16), :]

    arrived(STATS1, st1.at[pl.ds(0, 7)])
    at[...] = jnp.sum(st1[...], axis=0)

    @pl.loop(1, 16)
    def _(k):
        send(at, st2.at[tm], STATS2, lax.rem(tm + k, 16), h)

    st2[tm] = at[...]

    arrived(BLOCKS, xraw.at[pl.ds(0, 7), pl.ds(0, 2)])
    own = xraw.at[:, pl.ds(1 + 2 * core, 2)]
    send(own, own, X_PAIR, pair, h)
    send(xraw.at[:, pl.ds(1 + 3 * core, 1)], xraw.at[:, pl.ds(5 - 5 * core, 1)], X_ROWS, t_off * 2 + 1 - core, h)
    for r in range(2):
        rows = xraw[:, 1 + 2 * core + r].astype(F32).reshape(128, 256)
        for half in range(2):
            xf[half, :, :] = rows[:, 128 * half : 128 * half + 128]
            for side, column in ((0, 0), (1, 15)):
                xe[side, r, :, 128 * half : 128 * half + 128] = xf.at[half][pl.ds(column, 8, stride=16), :]
    for side, to_h in ((0, left), (1, right)):
        send(xe.at[side], hc.at[1 - side, pl.ds(1 + 2 * core, 2)], X_COLS, tm, to_h)
        send(xe.at[side, pl.ds(1 - core, 1)], hc.at[1 - side, pl.ds(2 + core, 1)], X_COLS, pair, to_h)
        send(xe.at[side, pl.ds(core, 1)], hc.at[1 - side, pl.ds(5 - 5 * core, 1)], X_COLS, t_off * 2 + 1 - core, to_h)

    fetch_w.wait()

    @pl.loop(0, 48)
    def _(step):
        a = step // 16
        rows = pl.ds(pl.multiple_of(lax.rem(step, 16) * 16, 16), 16)
        taps = [[w[a * 9 + b * 3 + e, rows, :].astype(F32) for e in range(3)] for b in range(3)]
        for rc, bs in enumerate(((0,), (1, 2), (0, 1), (2,))):
            line = [taps[bs[0]][e] if len(bs) == 1 else taps[bs[0]][e] + taps[bs[1]][e] for e in range(3)]
            for cc, value in enumerate((line[0], line[1] + line[2], line[0] + line[1], line[2])):
                wc[a, rc, rows, 128 * cc : 128 * cc + 128] = value.astype(BF16)

    arrived(COT_PAIR, cpart)
    arrived(COT_ROWS, cedge)
    arrived(COT_COLS, ch)
    for r in range(4):
        for f in range(8):
            cf[pl.ds(cell(5 - 4 * core + r, f) + 8, 32), :] = cpart[f, r].astype(F32)
    top, bottom = t > 0, t < CHIPS - 1
    for f in range(8):
        cf[pl.ds(cell(0, f) + 8, 32), :] = jnp.where(top, cedge[0, f, 0].astype(F32), 0.0)
        cf[pl.ds(cell(9, f) + 8, 32), :] = jnp.where(bottom, cedge[1, f, 0].astype(F32), 0.0)
    for j in range(10):
        keep = (h > 0, h < HEIGHT - 1)
        if j == 0:
            keep = tuple(jnp.logical_and(k, top) for k in keep)
        if j == 9:
            keep = tuple(jnp.logical_and(k, bottom) for k in keep)
        cf[pl.ds(j * 384 + 7, 8, stride=48), :] = jnp.where(keep[0], ch[0, j], 0.0)
        cf[pl.ds(j * 384 + 40, 8, stride=48), :] = jnp.where(keep[1], ch[1, j], 0.0)

    @pl.loop(0, 8)
    def _(f):
        sums = []
        for j in range(10):
            base = cell(j, f)
            cols = [cf[pl.ds(base + 7 + i, 16, stride=2), :] for i in range(4)]
            sums.append((cols[2] + cols[3], cols[1] + cols[2], cols[0] + cols[1]))
        for b in range(3):
            for e in range(3):
                for row in range(4):
                    s_buf[b * 3 + e, f, row] = (sums[2 * row + 2 - b][e] + sums[2 * row + 3 - b][e]).astype(BF16)

    arrived(STATS2, st2.at[pl.ds(0, 15)])
    stats = group_totals(jnp.sum(st2[...], axis=0)) / NUMBERS
    mean = jnp.concatenate([stats[0:1], stats[1:2]], axis=1)
    square = jnp.concatenate([stats[2:3], stats[3:4]], axis=1)
    inverse = lax.rsqrt(square - mean * mean + EPSILON)
    scale, shift = inverse * gain[...], bias[...]

    def activate(v):
        shifted = (v - mean) * scale + shift
        return shifted * jax.nn.sigmoid(shifted)

    arrived(X_PAIR, xraw.at[:, pl.ds(0, 2)])
    arrived(X_ROWS, xraw.at[:, pl.ds(0, 1)])
    arrived(X_COLS, hc.at[:, pl.ds(0, 4)])

    pads = (pad0, pad1)

    @pl.loop(0, 5)
    def _(k):
        j = core + k
        inside = jnp.logical_and(jnp.logical_or(t > 0, j > 0), jnp.logical_or(t < CHIPS - 1, j < 5))
        act = activate(xraw[:, j].astype(F32).reshape(128, 256))
        act = jnp.where(inside, act, 0.0)
        act_l = jnp.where(jnp.logical_and(inside, h > 0), activate(hc[0, j]), 0.0)
        act_r = jnp.where(jnp.logical_and(inside, h < HEIGHT - 1), activate(hc[1, j]), 0.0)
        acts[1, 2:10, j] = act.astype(BF16).reshape(8, 16, 256)
        for half in range(2):
            lanes = slice(128 * half, 128 * half + 128)
            pad = pads[half]
            for f in range(8):
                pad[32 * f + 8 : 32 * f + 24, :] = act[16 * f : 16 * f + 16, lanes]
            pad[pl.ds(7, 8, stride=32), :] = act_l[:, lanes]
            pad[pl.ds(24, 8, stride=32), :] = act_r[:, lanes]
            for f in range(8):
                acts[0, 2 + f, j, :, lanes] = pad[32 * f + 7 : 32 * f + 23, :].astype(BF16)
                acts[2, 2 + f, j, :, lanes] = pad[32 * f + 9 : 32 * f + 25, :].astype(BF16)

    turned = jnp.transpose(acts[1, 2:10, 1:5].reshape(512, 256))
    a_t[...] = turned.reshape(8, 2, 16, 512)

    def part(to_h):
        lhs = a_t[:, core].reshape(128, 512)
        first = (27 * to_h) // 8
        for two in range(2):
            rhs = []
            for i in range(2):
                tap = first + 2 * two + i
                rhs.append(s_buf[lax.rem(tap, 9), pl.ds(2 - tap // 9, 8)].reshape(512, 128))
            out = jnp.dot(lhs, jnp.concatenate(rhs, axis=1), preferred_element_type=F32)
            for i in range(2):
                g_buf[to_h, :, 2 * two + i] = out[:, 128 * i : 128 * i + 128].astype(BF16).reshape(8, 16, 128)

    def send_part(to_t, to_h):
        send(g_buf.at[to_h, to_t], r_buf.at[t * 8 + h], REDUCE, to_t * 2 + core, to_h)

    @pl.loop(1, 8)
    def _(k):
        to_h = lax.rem(h + k, 8)
        part(to_h)

        @pl.loop(0, 8)
        def _(u):
            send_part(lax.rem(t + u, 8), to_h)

    part(h)

    @pl.loop(1, 8)
    def _(u):
        send_part(lax.rem(t + u, 8), h)

    r_buf[t * 8 + h] = g_buf[h, t]

    grad = jnp.zeros((256, 256), F32)
    for first in range(0, 27, 2):
        taps = range(first, min(first + 2, 27))
        lhs = [s_buf[n % 9, 2 - n // 9 : 10 - n // 9, pl.ds(2 * core, 2)].reshape(256, 128) for n in taps]
        rhs = [w[n] for n in taps]
        if len(lhs) == 2:
            lhs, rhs = [jnp.concatenate(lhs, axis=1)], [jnp.concatenate(rhs, axis=1)]
        grad = grad + lax.dot_general(lhs[0], rhs[0], (((1,), (1,)), ((), ())), preferred_element_type=F32)
    normed = (xraw[:, pl.ds(1 + 2 * core, 2)].astype(F32).reshape(256, 256) - mean) * inverse
    shifted = normed * gain[...] + shift
    sig = jax.nn.sigmoid(shifted)
    grad = grad * sig * (1.0 + shifted * (1.0 - sig))
    d_gain = jnp.sum(grad * normed, axis=0, keepdims=True)
    d_bias = jnp.sum(grad, axis=0, keepdims=True)
    sent(STATS1, st1.at[pl.ds(0, 7)])
    st[0:1, :] = d_gain[:, :128]
    st[1:2, :] = d_gain[:, 128:]
    st[2:3, :] = d_bias[:, :128]
    st[3:4, :] = d_bias[:, 128:]

    @pl.loop(1, 8)
    def _(k):
        send(st, at1.at[h], AFF1, tm, lax.rem(h + k, 8))

    at1[h] = st[...]

    for p in range(2):
        even = jnp.zeros((256, 128), F32)
        odd = jnp.zeros((256, 128), F32)
        for rc, dr in ((0, -1), (1, 0)) if p == 0 else ((2, 0), (3, 1)):
            for a in range(3):
                lhs = [acts[dc, a : a + 8, pl.ds(2 * core + 1 + dr, 2)].reshape(256, 256) for dc in range(3)]
                both = jnp.dot(lhs[1], wc[a, rc, :, 128:384], preferred_element_type=F32)
                even = even + both[:, :128] + jnp.dot(lhs[0], wc[a, rc, :, 0:128], preferred_element_type=F32)
                odd = odd + both[:, 128:] + jnp.dot(lhs[2], wc[a, rc, :, 384:512], preferred_element_type=F32)
        for f in range(8):
            for row in range(2):
                at_row = (f * 4 + 2 * row + p) * 32
                here = (f * 2 + row) * 16
                d_buf[pl.ds(at_row, 16, stride=2), :] = even[here : here + 16]
                d_buf[pl.ds(at_row + 1, 16, stride=2), :] = odd[here : here + 16]
    dec[...] = d_buf[...].astype(BF16).reshape(8, 4, 32, 128)

    arrived(AFF1, at1.at[pl.ds(0, 7)])
    sent(STATS2, st2.at[pl.ds(0, 15)])
    at[...] = jnp.sum(at1[...], axis=0)

    @pl.loop(1, 16)
    def _(k):
        send(at, at2.at[tm], AFF2, lax.rem(tm + k, 16), h)

    at2[tm] = at[...]

    arrived(REDUCE, r_buf.at[pl.ds(0, 63)])
    ag_s[...] = jnp.sum(r_buf[...].astype(F32), axis=0)

    @pl.loop(1, 8)
    def _(k):
        send(ag_s, ag_r.at[h], GATHER, tm, lax.rem(h + k, 8))

    ag_r[h] = ag_s[...]

    arrived(AFF2, at2.at[pl.ds(0, 15)])
    total = jnp.sum(at2[...], axis=0)
    aff[0:1, 0:128] = total[0:1]
    aff[0:1, 128:256] = total[1:2]
    aff[1:2, 0:128] = total[2:3]
    aff[1:2, 128:256] = total[3:4]

    arrived(GATHER, ag_r.at[pl.ds(0, 7)])
    for k in range(8):
        first = (27 * k) // 8
        gw[first : first + 4] = ag_r[k]

    sent(BLOCKS, xraw.at[pl.ds(0, 7), pl.ds(0, 2)])
    sent(COT_PAIR, cpart)
    sent(COT_ROWS, cedge)
    sent(COT_COLS, ch)
    sent(X_PAIR, xraw.at[:, pl.ds(0, 2)])
    sent(X_ROWS, xraw.at[:, pl.ds(0, 1)])
    sent(X_COLS, hc.at[:, pl.ds(0, 4)])
    sent(REDUCE, r_buf.at[pl.ds(0, 63)])
    sent(GATHER, ag_r.at[pl.ds(0, 7)])
    sent(AFF1, at1.at[pl.ds(0, 7)])
    sent(AFF2, at2.at[pl.ds(0, 15)])


def per_device(coarse, gain, bias, weight, cotangent):
    taps = jnp.transpose(weight, (1, 2, 3, 0, 4)).reshape(27, 256, 128)
    vmem = pl.BlockSpec(memory_space=pltpu.VMEM)
    vm = pltpu.VMEM
    decoded, grad_weight, grad_affine = pl.pallas_call(
        kernel,
        out_shape=(
            jax.ShapeDtypeStruct((8, 4, 32, 128), BF16),
            jax.ShapeDtypeStruct((27, 16, 128), F32),
            jax.ShapeDtypeStruct((2, 256), F32),
        ),
        in_specs=[vmem, vmem, vmem, pl.BlockSpec(memory_space=pl.ANY), vmem],
        out_specs=(vmem, vmem, vmem),
        scratch_shapes=[
            vm((27, 256, 128), BF16),
            pltpu.SemaphoreType.DMA,
            vm((3, 4, 256, 512), BF16),
            vm((8, 128), F32),
            vm((8, 8, 128), F32),
            vm((16, 8, 128), F32),
            vm((8, 128), F32),
            vm((8, 8, 128), F32),
            vm((16, 8, 128), F32),
            vm((8, 6, 16, 256), BF16),
            vm((2, 128, 128), F32),
            vm((2, 2, 8, 256), F32),
            vm((2, 6, 8, 256), F32),
            vm((3, 10, 6, 16, 256), BF16),
            vm((256, 128), F32),
            vm((256, 128), F32),
            vm((8, 2, 16, 512), BF16),
            vm((8, 4, 32, 128), BF16),
            vm((2, 8, 1, 32, 128), BF16),
            vm((2, 4, 8, 128), F32),
            vm((2, 10, 8, 128), F32),
            vm((10 * 8 * 48, 128), F32),
            vm((9, 10, 4, 16, 128), BF16),
            vm((8, 8, 4, 16, 128), BF16),
            vm((64, 4, 16, 128), BF16),
            vm((4, 16, 128), F32),
            vm((8, 4, 16, 128), F32),
            vm((1024, 128), F32),
            pltpu.SemaphoreType.DMA((13,)),
            pltpu.SemaphoreType.DMA((13,)),
        ],
        compiler_params=pltpu.CompilerParams(
            collective_id=0, has_side_effects=True, vmem_limit_bytes=48 * 2**20
        ),
        cost_estimate=pl.CostEstimate(flops=2 * 10**9, bytes_accessed=4 * 10**6, transcendentals=300000),
    )(coarse.reshape(2, 128, 256), gain.reshape(1, 256), bias.reshape(1, 256), taps, cotangent)
    grad_weight = jnp.transpose(grad_weight.reshape(3, 3, 3, 16, 128), (3, 0, 1, 2, 4))
    return decoded, grad_weight, grad_affine


def solution(mesh):
    return jax.shard_map(
        per_device,
        mesh=mesh,
        in_specs=(P("height", "tm", None, None), P(), P(), P(), P(None, "tm", "height", None)),
        out_specs=(P(None, "tm", "height", None), P("tm", None, None, None, None), P()),
        check_vma=False,
    )
```

```python
import functools

import jax
import jax.numpy as jnp
from jax import lax
from jax.experimental import pallas as pl
from jax.experimental.pallas import tpu as pltpu
from jax.sharding import PartitionSpec as P

MESH = pl.DeviceIdType.MESH
F32, BF16 = jnp.float32, jnp.bfloat16
EPSILON = 1e-06
NUMBERS = 8 * 32 * 128 * 8
CHIPS, HEIGHT = 8, 8

(STATS1, STATS2, BLOCKS, COT_PAIR, COT_ROWS, COT_COLS, X_PAIR, X_ROWS, X_COLS, REDUCE, GATHER, AFF1, AFF2) = range(13)


def group_totals(tile):
    lane = lax.broadcasted_iota(jnp.int32, tile.shape, 1)
    for step in (1, 2, 4):
        other = jnp.where(
            (lane & step) == 0, pltpu.roll(tile, 128 - step, 1), pltpu.roll(tile, step, 1)
        )
        tile = tile + other
    return tile


def kernel(
    coarse_hbm, gain_hbm, bias_hbm, w_hbm, cot_hbm, dec, gw, aff,
    coarse, gain, bias, w, cot, fetch_sem, wc, st, st1, st2, at, at1, at2,
    xraw, xf, xe, hc, acts, pad0, pad1, a_t,
    cpart, cedge, ce, ch, cf, s_buf, g_buf, r_buf, ag_s, ag_r, d_buf, ssem, rsem,
):
    tm, h = lax.axis_index("tm"), lax.axis_index("height")
    core = lax.rem(tm, 2)
    t = tm // 2
    left, right = lax.rem(h + 7, 8), lax.rem(h + 1, 8)
    t_off = lax.rem(t + 7 + 2 * core, 8)
    pair = tm + 1 - 2 * core

    def send(src, dst, kind, to_tm, to_h):
        pltpu.make_async_remote_copy(
            src_ref=src, dst_ref=dst, send_sem=ssem.at[kind], recv_sem=rsem.at[kind],
            device_id=(to_tm, to_h), device_id_type=MESH,
        ).start()

    def arrived(kind, like):
        pltpu.make_async_copy(like, like, rsem.at[kind]).wait()

    def sent(kind, like):
        pltpu.make_async_copy(like, like, ssem.at[kind]).wait()

    pairs = ((coarse_hbm, coarse), (cot_hbm, cot), (gain_hbm, gain), (bias_hbm, bias), (w_hbm, w))
    fetches = [pltpu.make_async_copy(src, dst, fetch_sem.at[i]) for i, (src, dst) in enumerate(pairs)]
    for fetch in fetches:
        fetch.start()

    barrier = pltpu.get_barrier_semaphore()

    def greet(to_tm, to_h):
        pl.semaphore_signal(barrier, inc=1, device_id=(to_tm, to_h), device_id_type=MESH)

    @pl.loop(1, 8)
    def _(k):
        greet(tm, lax.rem(h + k, 8))

    @pl.loop(1, 16)
    def _(k):
        greet(lax.rem(tm + k, 16), h)

    greet(pair, left)
    greet(pair, right)

    @pl.loop(0, 4)
    def _(k):
        to_tm = lax.rem(t + 7 + 2 * (k // 2), 8) * 2 + lax.rem(k, 2)
        greet(to_tm, left)
        greet(to_tm, right)

    fetches[0].wait()
    x = coarse[...].astype(F32).reshape(256, 256)
    total = jnp.sum(x, axis=0, keepdims=True)
    squares = jnp.sum(x * x, axis=0, keepdims=True)
    st[...] = jnp.zeros((8, 128), F32)
    st[0:1, :] = total[:, :128]
    st[1:2, :] = total[:, 128:]
    st[2:3, :] = squares[:, :128]
    st[3:4, :] = squares[:, 128:]

    def cell(j, f):
        return pl.multiple_of((j * 8 + f) * 48, 8)

    fetches[1].wait()
    for r in range(4):
        for f in range(8):
            cf[pl.ds(cell(1 + 4 * core + r, f) + 8, 32), :] = cot[f, r].astype(F32)
    for r in range(4):
        base = cell(1 + 4 * core + r, 0)
        ce[0, r] = cf[pl.ds(base + 8, 8, stride=48), :]
        ce[1, r] = cf[pl.ds(base + 39, 8, stride=48), :]
    hc[0, 4 - 3 * core] = jnp.zeros((8, 256), F32)
    hc[1, 4 - 3 * core] = jnp.zeros((8, 256), F32)
    acts[:, 0:2] = jnp.zeros((3, 2, 6, 16, 256), BF16)
    s_buf[:, 8:10] = jnp.zeros((9, 2, 4, 16, 128), BF16)

    pl.semaphore_wait(barrier, 32)

    @pl.loop(1, 8)
    def _(k):
        send(st, st1.at[h], STATS1, tm, lax.rem(h + k, 8))

    @pl.loop(1, 8)
    def _(k):
        to_h = lax.rem(h + k, 8)
        send(
            coarse.at[:, pl.ds(pl.multiple_of(to_h * 16, 16), 16), :],
            xraw.at[h, pl.ds(1 + 2 * core, 2)], BLOCKS, tm, to_h,
        )

    send(cot, cpart, COT_PAIR, pair, h)
    for c2 in range(2):
        send(cot.at[:, pl.ds(3 * core, 1)], cedge.at[1 - core], COT_ROWS, t_off * 2 + c2, h)
    for side, to_h in ((0, left), (1, right)):
        for c2 in range(2):
            send(ce.at[side], ch.at[1 - side, pl.ds(1 + 4 * core, 4)], COT_COLS, 2 * t + c2, to_h)
            send(ce.at[side, pl.ds(3 * core, 1)], ch.at[1 - side, pl.ds(9 - 9 * core, 1)], COT_COLS, t_off * 2 + c2, to_h)

    st1[h] = st[...]
    xraw[h, pl.ds(1 + 2 * core, 2)] = coarse[:, pl.ds(pl.multiple_of(h * 16, 16), 16), :]

    arrived(STATS1, st1.at[pl.ds(0, 7)])
    at[...] = jnp.sum(st1[...], axis=0)

    @pl.loop(1, 16)
    def _(k):
        send(at, st2.at[tm], STATS2, lax.rem(tm + k, 16), h)

    st2[tm] = at[...]

    arrived(BLOCKS, xraw.at[pl.ds(0, 7), pl.ds(0, 2)])
    own = xraw.at[:, pl.ds(1 + 2 * core, 2)]
    send(own, own, X_PAIR, pair, h)
    send(xraw.at[:, pl.ds(1 + 3 * core, 1)], xraw.at[:, pl.ds(5 - 5 * core, 1)], X_ROWS, t_off * 2 + 1 - core, h)
    for r in range(2):
        rows = xraw[:, 1 + 2 * core + r].astype(F32).reshape(128, 256)
        for half in range(2):
            xf[half, :, :] = rows[:, 128 * half : 128 * half + 128]
            for side, column in ((0, 0), (1, 15)):
                xe[side, r, :, 128 * half : 128 * half + 128] = xf.at[half][pl.ds(column, 8, stride=16), :]
    for side, to_h in ((0, left), (1, right)):
        send(xe.at[side], hc.at[1 - side, pl.ds(1 + 2 * core, 2)], X_COLS, tm, to_h)
        send(xe.at[side, pl.ds(1 - core, 1)], hc.at[1 - side, pl.ds(2 + core, 1)], X_COLS, pair, to_h)
        send(xe.at[side, pl.ds(core, 1)], hc.at[1 - side, pl.ds(5 - 5 * core, 1)], X_COLS, t_off * 2 + 1 - core, to_h)

    for fetch in fetches[2:]:
        fetch.wait()

    @pl.loop(0, 48)
    def _(step):
        a = step // 16
        rows = pl.ds(pl.multiple_of(lax.rem(step, 16) * 16, 16), 16)
        taps = [[w[a * 9 + b * 3 + e, rows, :].astype(F32) for e in range(3)] for b in range(3)]
        for rc, bs in enumerate(((0,), (1, 2), (0, 1), (2,))):
            line = [taps[bs[0]][e] if len(bs) == 1 else taps[bs[0]][e] + taps[bs[1]][e] for e in range(3)]
            for cc, value in enumerate((line[0], line[1] + line[2], line[0] + line[1], line[2])):
                wc[a, rc, rows, 128 * cc : 128 * cc + 128] = value.astype(BF16)

    arrived(COT_PAIR, cpart)
    arrived(COT_ROWS, cedge)
    arrived(COT_COLS, ch)
    for r in range(4):
        for f in range(8):
            cf[pl.ds(cell(5 - 4 * core + r, f) + 8, 32), :] = cpart[f, r].astype(F32)
    top, bottom = t > 0, t < CHIPS - 1
    for f in range(8):
        cf[pl.ds(cell(0, f) + 8, 32), :] = jnp.where(top, cedge[0, f, 0].astype(F32), 0.0)
        cf[pl.ds(cell(9, f) + 8, 32), :] = jnp.where(bottom, cedge[1, f, 0].astype(F32), 0.0)
    for j in range(10):
        keep = (h > 0, h < HEIGHT - 1)
        if j == 0:
            keep = tuple(jnp.logical_and(k, top) for k in keep)
        if j == 9:
            keep = tuple(jnp.logical_and(k, bottom) for k in keep)
        cf[pl.ds(j * 384 + 7, 8, stride=48), :] = jnp.where(keep[0], ch[0, j], 0.0)
        cf[pl.ds(j * 384 + 40, 8, stride=48), :] = jnp.where(keep[1], ch[1, j], 0.0)

    @pl.loop(0, 8)
    def _(f):
        sums = []
        for j in range(10):
            base = cell(j, f)
            cols = [cf[pl.ds(base + 7 + i, 16, stride=2), :] for i in range(4)]
            sums.append((cols[2] + cols[3], cols[1] + cols[2], cols[0] + cols[1]))
        for b in range(3):
            for e in range(3):
                for row in range(4):
                    s_buf[b * 3 + e, f, row] = (sums[2 * row + 2 - b][e] + sums[2 * row + 3 - b][e]).astype(BF16)

    arrived(STATS2, st2.at[pl.ds(0, 15)])
    stats = group_totals(jnp.sum(st2[...], axis=0)) / NUMBERS
    mean = jnp.concatenate([stats[0:1], stats[1:2]], axis=1)
    square = jnp.concatenate([stats[2:3], stats[3:4]], axis=1)
    inverse = lax.rsqrt(square - mean * mean + EPSILON)
    scale, shift = inverse * gain[...], bias[...]

    def activate(v):
        shifted = (v - mean) * scale + shift
        return shifted * jax.nn.sigmoid(shifted)

    arrived(X_PAIR, xraw.at[:, pl.ds(0, 2)])
    arrived(X_ROWS, xraw.at[:, pl.ds(0, 1)])
    arrived(X_COLS, hc.at[:, pl.ds(0, 4)])

    pads = (pad0, pad1)

    @pl.loop(0, 5)
    def _(k):
        j = core + k
        inside = jnp.logical_and(jnp.logical_or(t > 0, j > 0), jnp.logical_or(t < CHIPS - 1, j < 5))
        act = activate(xraw[:, j].astype(F32).reshape(128, 256))
        act = jnp.where(inside, act, 0.0)
        act_l = jnp.where(jnp.logical_and(inside, h > 0), activate(hc[0, j]), 0.0)
        act_r = jnp.where(jnp.logical_and(inside, h < HEIGHT - 1), activate(hc[1, j]), 0.0)
        acts[1, 2:10, j] = act.astype(BF16).reshape(8, 16, 256)
        for half in range(2):
            lanes = slice(128 * half, 128 * half + 128)
            pad = pads[half]
            for f in range(8):
                pad[32 * f + 8 : 32 * f + 24, :] = act[16 * f : 16 * f + 16, lanes]
            pad[pl.ds(7, 8, stride=32), :] = act_l[:, lanes]
            pad[pl.ds(24, 8, stride=32), :] = act_r[:, lanes]
            for f in range(8):
                acts[0, 2 + f, j, :, lanes] = pad[32 * f + 7 : 32 * f + 23, :].astype(BF16)
                acts[2, 2 + f, j, :, lanes] = pad[32 * f + 9 : 32 * f + 25, :].astype(BF16)

    turned = jnp.transpose(acts[1, 2:10, 1:5].reshape(512, 256))
    a_t[...] = turned.reshape(8, 2, 16, 512)

    def part(to_h):
        lhs = a_t[:, core].reshape(128, 512)
        first = (27 * to_h) // 8
        for two in range(2):
            rhs = []
            for i in range(2):
                tap = first + 2 * two + i
                rhs.append(s_buf[lax.rem(tap, 9), pl.ds(2 - tap // 9, 8)].reshape(512, 128))
            out = jnp.dot(lhs, jnp.concatenate(rhs, axis=1), preferred_element_type=F32)
            for i in range(2):
                g_buf[to_h, :, 2 * two + i] = out[:, 128 * i : 128 * i + 128].astype(BF16).reshape(8, 16, 128)

    def send_part(to_t, to_h):
        send(g_buf.at[to_h, to_t], r_buf.at[t * 8 + h], REDUCE, to_t * 2 + core, to_h)

    @pl.loop(1, 8)
    def _(k):
        to_h = lax.rem(h + k, 8)
        part(to_h)

        @pl.loop(0, 8)
        def _(u):
            send_part(lax.rem(t + u, 8), to_h)

    part(h)

    @pl.loop(1, 8)
    def _(u):
        send_part(lax.rem(t + u, 8), h)

    r_buf[t * 8 + h] = g_buf[h, t]

    grad = jnp.zeros((256, 256), F32)
    for first in range(0, 27, 2):
        taps = range(first, min(first + 2, 27))
        lhs = [s_buf[n % 9, 2 - n // 9 : 10 - n // 9, pl.ds(2 * core, 2)].reshape(256, 128) for n in taps]
        rhs = [w[n] for n in taps]
        if len(lhs) == 2:
            lhs, rhs = [jnp.concatenate(lhs, axis=1)], [jnp.concatenate(rhs, axis=1)]
        grad = grad + lax.dot_general(lhs[0], rhs[0], (((1,), (1,)), ((), ())), preferred_element_type=F32)
    normed = (xraw[:, pl.ds(1 + 2 * core, 2)].astype(F32).reshape(256, 256) - mean) * inverse
    shifted = normed * gain[...] + shift
    sig = jax.nn.sigmoid(shifted)
    grad = grad * sig * (1.0 + shifted * (1.0 - sig))
    d_gain = jnp.sum(grad * normed, axis=0, keepdims=True)
    d_bias = jnp.sum(grad, axis=0, keepdims=True)
    sent(STATS1, st1.at[pl.ds(0, 7)])
    st[0:1, :] = d_gain[:, :128]
    st[1:2, :] = d_gain[:, 128:]
    st[2:3, :] = d_bias[:, :128]
    st[3:4, :] = d_bias[:, 128:]

    @pl.loop(1, 8)
    def _(k):
        send(st, at1.at[h], AFF1, tm, lax.rem(h + k, 8))

    at1[h] = st[...]

    for p in range(2):
        even = jnp.zeros((256, 128), F32)
        odd = jnp.zeros((256, 128), F32)
        for rc, dr in ((0, -1), (1, 0)) if p == 0 else ((2, 0), (3, 1)):
            for a in range(3):
                lhs = [acts[dc, a : a + 8, pl.ds(2 * core + 1 + dr, 2)].reshape(256, 256) for dc in range(3)]
                both = jnp.dot(lhs[1], wc[a, rc, :, 128:384], preferred_element_type=F32)
                even = even + both[:, :128] + jnp.dot(lhs[0], wc[a, rc, :, 0:128], preferred_element_type=F32)
                odd = odd + both[:, 128:] + jnp.dot(lhs[2], wc[a, rc, :, 384:512], preferred_element_type=F32)
        for f in range(8):
            for row in range(2):
                at_row = (f * 4 + 2 * row + p) * 32
                here = (f * 2 + row) * 16
                d_buf[pl.ds(at_row, 16, stride=2), :] = even[here : here + 16]
                d_buf[pl.ds(at_row + 1, 16, stride=2), :] = odd[here : here + 16]
    dec[...] = d_buf[...].astype(BF16).reshape(8, 4, 32, 128)

    arrived(AFF1, at1.at[pl.ds(0, 7)])
    sent(STATS2, st2.at[pl.ds(0, 15)])
    at[...] = jnp.sum(at1[...], axis=0)

    @pl.loop(1, 16)
    def _(k):
        send(at, at2.at[tm], AFF2, lax.rem(tm + k, 16), h)

    at2[tm] = at[...]

    arrived(REDUCE, r_buf.at[pl.ds(0, 63)])
    ag_s[...] = jnp.sum(r_buf[...].astype(F32), axis=0)

    @pl.loop(1, 8)
    def _(k):
        send(ag_s, ag_r.at[h], GATHER, tm, lax.rem(h + k, 8))

    ag_r[h] = ag_s[...]

    arrived(AFF2, at2.at[pl.ds(0, 15)])
    total = jnp.sum(at2[...], axis=0)
    aff[0:1, 0:128] = total[0:1]
    aff[0:1, 128:256] = total[1:2]
    aff[1:2, 0:128] = total[2:3]
    aff[1:2, 128:256] = total[3:4]

    arrived(GATHER, ag_r.at[pl.ds(0, 7)])
    for k in range(8):
        first = (27 * k) // 8
        gw[first : first + 4] = ag_r[k]

    sent(BLOCKS, xraw.at[pl.ds(0, 7), pl.ds(0, 2)])
    sent(COT_PAIR, cpart)
    sent(COT_ROWS, cedge)
    sent(COT_COLS, ch)
    sent(X_PAIR, xraw.at[:, pl.ds(0, 2)])
    sent(X_ROWS, xraw.at[:, pl.ds(0, 1)])
    sent(X_COLS, hc.at[:, pl.ds(0, 4)])
    sent(REDUCE, r_buf.at[pl.ds(0, 63)])
    sent(GATHER, ag_r.at[pl.ds(0, 7)])
    sent(AFF1, at1.at[pl.ds(0, 7)])
    sent(AFF2, at2.at[pl.ds(0, 15)])


def deliver(*refs):
    copies = [pltpu.make_async_copy(refs[i], refs[3 + i], refs[6].at[i]) for i in range(3)]
    for copy in copies:
        copy.start()
    for copy in copies:
        copy.wait()


def per_device(coarse, gain, bias, weight, cotangent):
    taps = jnp.transpose(weight, (1, 2, 3, 0, 4)).reshape(27, 256, 128)
    vmem = pl.BlockSpec(memory_space=pltpu.VMEM)
    vm = pltpu.VMEM
    decoded, grad_weight, grad_affine = pl.pallas_call(
        kernel,
        out_shape=(
            jax.ShapeDtypeStruct((8, 4, 32, 128), BF16),
            jax.ShapeDtypeStruct((27, 16, 128), F32),
            jax.ShapeDtypeStruct((2, 256), F32),
        ),
        in_specs=[pl.BlockSpec(memory_space=pltpu.HBM)] * 5,
        out_specs=(vmem, vmem, vmem),
        scratch_shapes=[
            vm((2, 128, 256), BF16),
            vm((1, 256), F32),
            vm((1, 256), F32),
            vm((27, 256, 128), BF16),
            vm((8, 4, 32, 128), BF16),
            pltpu.SemaphoreType.DMA((5,)),
            vm((3, 4, 256, 512), BF16),
            vm((8, 128), F32),
            vm((8, 8, 128), F32),
            vm((16, 8, 128), F32),
            vm((8, 128), F32),
            vm((8, 8, 128), F32),
            vm((16, 8, 128), F32),
            vm((8, 6, 16, 256), BF16),
            vm((2, 128, 128), F32),
            vm((2, 2, 8, 256), F32),
            vm((2, 6, 8, 256), F32),
            vm((3, 10, 6, 16, 256), BF16),
            vm((256, 128), F32),
            vm((256, 128), F32),
            vm((8, 2, 16, 512), BF16),
            vm((8, 4, 32, 128), BF16),
            vm((2, 8, 1, 32, 128), BF16),
            vm((2, 4, 8, 128), F32),
            vm((2, 10, 8, 128), F32),
            vm((10 * 8 * 48, 128), F32),
            vm((9, 10, 4, 16, 128), BF16),
            vm((8, 8, 4, 16, 128), BF16),
            vm((64, 4, 16, 128), BF16),
            vm((4, 16, 128), F32),
            vm((8, 4, 16, 128), F32),
            vm((1024, 128), F32),
            pltpu.SemaphoreType.DMA((13,)),
            pltpu.SemaphoreType.DMA((13,)),
        ],
        compiler_params=pltpu.CompilerParams(
            collective_id=0, has_side_effects=True, vmem_limit_bytes=48 * 2**20
        ),
        cost_estimate=pl.CostEstimate(flops=2 * 10**9, bytes_accessed=4 * 10**6, transcendentals=300000),
    )(*[
        pltpu.with_memory_space_constraint(x, pltpu.HBM)
        for x in (coarse.reshape(2, 128, 256), gain.reshape(1, 256), bias.reshape(1, 256), taps, cotangent)
    ])
    decoded, grad_weight, grad_affine = pl.pallas_call(
        deliver,
        out_shape=(
            jax.ShapeDtypeStruct((8, 4, 32, 128), BF16),
            jax.ShapeDtypeStruct((27, 16, 128), F32),
            jax.ShapeDtypeStruct((2, 256), F32),
        ),
        in_specs=[pl.BlockSpec(memory_space=pltpu.VMEM)] * 3,
        out_specs=[pl.BlockSpec(memory_space=pl.ANY)] * 3,
        scratch_shapes=[pltpu.SemaphoreType.DMA((3,))],
        compiler_params=pltpu.CompilerParams(vmem_limit_bytes=8 * 2**20),
    )(decoded, grad_weight, grad_affine)
    grad_weight = jnp.transpose(grad_weight.reshape(3, 3, 3, 16, 128), (3, 0, 1, 2, 4))
    return decoded, grad_weight, grad_affine


def solution(mesh):
    return jax.shard_map(
        per_device,
        mesh=mesh,
        in_specs=(P("height", "tm", None, None), P(), P(), P(), P(None, "tm", "height", None)),
        out_specs=(P(None, "tm", "height", None), P("tm", None, None, None, None), P()),
        check_vma=False,
    )
```

```python
import functools

import jax
import jax.numpy as jnp
from jax import lax
from jax.experimental import pallas as pl
from jax.experimental.pallas import tpu as pltpu
from jax.sharding import PartitionSpec as P

MESH = pl.DeviceIdType.MESH
F32, BF16 = jnp.float32, jnp.bfloat16
EPSILON = 1e-06
NUMBERS = 8 * 32 * 128 * 8
CHIPS, HEIGHT = 8, 8
EXTRA = (0, 3, 6)

(STATS1, STATS2, BLOCKS, COT_PAIR, COT_ROWS, COT_COLS, X_PAIR, X_ROWS, X_COLS, ALONG_X, ALONG_Y, ALONG_Z, LAST_X, LAST_Y, LAST_Z, LAST_E, GATHER, AFF1, AFF2) = range(19)


def group_totals(tile):
    lane = lax.broadcasted_iota(jnp.int32, tile.shape, 1)
    for step in (1, 2, 4):
        other = jnp.where(
            (lane & step) == 0, pltpu.roll(tile, 128 - step, 1), pltpu.roll(tile, step, 1)
        )
        tile = tile + other
    return tile


def kernel(
    coarse_hbm, gain_hbm, bias_hbm, w_hbm, cot_hbm, dec, gw, aff,
    coarse, gain, bias, w, cot, fetch_sem, wc, st, sa, st1, st2, af, at, at1, at2,
    xraw, xf, xe, hc, acts, pad0, pad1, a_t,
    cpart, cedge, ce, ch, cf, s_buf,
    gx, gy, gz, rx, ry, rz, px, py, pz, qx, qy, qz, qe, ag_s, ag_r, d_buf, ssem, rsem,
):
    tm, h = lax.axis_index("tm"), lax.axis_index("height")
    core = lax.rem(tm, 2)
    t = tm // 2
    left, right = lax.rem(h + 7, 8), lax.rem(h + 1, 8)
    t_off = lax.rem(t + 7 + 2 * core, 8)
    pair = tm + 1 - 2 * core

    def others_h():
        for dz, dy in ((1, 2), (1, 1), (1, 3), (0, 2), (1, 0), (0, 1), (0, 3)):
            yield lax.rem(h // 4 + dz, 2) * 4 + lax.rem(h + dy, 4)

    def others_tm():
        for dz, dx in ((1, 2), (1, 1), (1, 3), (1, 0), (0, 2), (0, 1), (0, 3)):
            chip = lax.rem(t // 4 + dz, 2) * 4 + lax.rem(t + dx, 4)
            yield 2 * chip + core
            yield 2 * chip + 1 - core
        yield pair

    def send(src, dst, kind, to_tm, to_h):
        pltpu.make_async_remote_copy(
            src_ref=src, dst_ref=dst, send_sem=ssem.at[kind], recv_sem=rsem.at[kind],
            device_id=(to_tm, to_h), device_id_type=MESH,
        ).start()

    def arrived(kind, like):
        pltpu.make_async_copy(like, like, rsem.at[kind]).wait()

    def sent(kind, like):
        pltpu.make_async_copy(like, like, ssem.at[kind]).wait()

    pairs = ((coarse_hbm, coarse), (cot_hbm, cot), (gain_hbm, gain), (bias_hbm, bias), (w_hbm, w))
    fetches = [pltpu.make_async_copy(src, dst, fetch_sem.at[i]) for i, (src, dst) in enumerate(pairs)]
    for fetch in fetches:
        fetch.start()

    barrier = pltpu.get_barrier_semaphore()

    def greet(to_tm, to_h):
        pl.semaphore_signal(barrier, inc=1, device_id=(to_tm, to_h), device_id_type=MESH)

    for to_tm in others_tm():
        greet(to_tm, h)
    for to_h in others_h():
        greet(tm, to_h)

    greet(pair, left)
    greet(pair, right)

    @pl.loop(0, 4)
    def _(k):
        to_tm = lax.rem(t + 7 + 2 * (k // 2), 8) * 2 + lax.rem(k, 2)
        greet(to_tm, left)
        greet(to_tm, right)

    fetches[0].wait()
    x = coarse[...].astype(F32).reshape(256, 256)
    total = jnp.sum(x, axis=0, keepdims=True)
    squares = jnp.sum(x * x, axis=0, keepdims=True)
    quarters = (total[:, :128], total[:, 128:], squares[:, :128], squares[:, 128:])
    quarter = lax.rem(lax.broadcasted_iota(jnp.int32, (4, 128), 1), 4)
    mine = quarter == lax.broadcasted_iota(jnp.int32, (4, 128), 0)
    sums = group_totals(jnp.concatenate(quarters, axis=0))
    st[...] = jnp.sum(jnp.where(mine, sums, 0.0), axis=0, keepdims=True)

    pl.semaphore_wait(barrier, 32)

    for to_h in others_h():
        send(st, st1.at[h], STATS1, tm, to_h)

    for to_h in others_h():
        send(
            coarse.at[:, pl.ds(pl.multiple_of(to_h * 16, 16), 16), :],
            xraw.at[h, pl.ds(1 + 2 * core, 2)], BLOCKS, tm, to_h,
        )

    fetches[1].wait()
    send(cot, cpart, COT_PAIR, pair, h)
    for c2 in range(2):
        send(cot.at[:, pl.ds(3 * core, 1)], cedge.at[1 - core], COT_ROWS, t_off * 2 + c2, h)
    def cell(j, f):
        return pl.multiple_of((j * 8 + f) * 48, 8)

    for r in range(4):
        for f in range(8):
            cf[pl.ds(cell(1 + 4 * core + r, f) + 8, 32), :] = cot[f, r].astype(F32)
    for r in range(4):
        base = cell(1 + 4 * core + r, 0)
        ce[0, r] = cf[pl.ds(base + 8, 8, stride=48), :]
        ce[1, r] = cf[pl.ds(base + 39, 8, stride=48), :]

    for side, to_h in ((0, left), (1, right)):
        for c2 in range(2):
            send(ce.at[side], ch.at[1 - side, pl.ds(1 + 4 * core, 4)], COT_COLS, 2 * t + c2, to_h)
            send(ce.at[side, pl.ds(3 * core, 1)], ch.at[1 - side, pl.ds(9 - 9 * core, 1)], COT_COLS, t_off * 2 + c2, to_h)

    st1[h] = st[...]
    xraw[h, pl.ds(1 + 2 * core, 2)] = coarse[:, pl.ds(pl.multiple_of(h * 16, 16), 16), :]

    arrived(STATS1, st1.at[pl.ds(0, 7)])
    sa[...] = jnp.sum(st1[...], axis=0)

    for to_tm in others_tm():
        send(sa, st2.at[tm], STATS2, to_tm, h)

    st2[tm] = sa[...]

    arrived(BLOCKS, xraw.at[pl.ds(0, 7), pl.ds(0, 2)])
    own = xraw.at[:, pl.ds(1 + 2 * core, 2)]
    send(own, own, X_PAIR, pair, h)
    send(xraw.at[:, pl.ds(1 + 3 * core, 1)], xraw.at[:, pl.ds(5 - 5 * core, 1)], X_ROWS, t_off * 2 + 1 - core, h)

    s_buf[:, 8:10] = jnp.zeros((9, 2, 4, 16, 128), BF16)
    arrived(COT_PAIR, cpart)
    arrived(COT_ROWS, cedge)
    arrived(COT_COLS, ch)
    for r in range(4):
        for f in range(8):
            cf[pl.ds(cell(5 - 4 * core + r, f) + 8, 32), :] = cpart[f, r].astype(F32)
    top, bottom = t > 0, t < CHIPS - 1
    for f in range(8):
        cf[pl.ds(cell(0, f) + 8, 32), :] = jnp.where(top, cedge[0, f, 0].astype(F32), 0.0)
        cf[pl.ds(cell(9, f) + 8, 32), :] = jnp.where(bottom, cedge[1, f, 0].astype(F32), 0.0)
    for j in range(10):
        keep = (h > 0, h < HEIGHT - 1)
        if j == 0:
            keep = tuple(jnp.logical_and(k, top) for k in keep)
        if j == 9:
            keep = tuple(jnp.logical_and(k, bottom) for k in keep)
        cf[pl.ds(j * 384 + 7, 8, stride=48), :] = jnp.where(keep[0], ch[0, j], 0.0)
        cf[pl.ds(j * 384 + 40, 8, stride=48), :] = jnp.where(keep[1], ch[1, j], 0.0)

    @pl.loop(0, 8)
    def _(f):
        sums = []
        for j in range(10):
            base = cell(j, f)
            cols = [cf[pl.ds(base + 7 + i, 16, stride=2), :] for i in range(4)]
            sums.append((cols[2] + cols[3], cols[1] + cols[2], cols[0] + cols[1]))
        for b in range(3):
            for e in range(3):
                for row in range(4):
                    s_buf[b * 3 + e, f, row] = (sums[2 * row + 2 - b][e] + sums[2 * row + 3 - b][e]).astype(BF16)

    for r in range(2):
        rows = xraw[:, 1 + 2 * core + r].astype(F32).reshape(128, 256)
        for half in range(2):
            xf[half, :, :] = rows[:, 128 * half : 128 * half + 128]
            for side, column in ((0, 0), (1, 15)):
                xe[side, r, :, 128 * half : 128 * half + 128] = xf.at[half][pl.ds(column, 8, stride=16), :]
    for side, to_h in ((0, left), (1, right)):
        send(xe.at[side], hc.at[1 - side, pl.ds(1 + 2 * core, 2)], X_COLS, tm, to_h)
        send(xe.at[side, pl.ds(1 - core, 1)], hc.at[1 - side, pl.ds(2 + core, 1)], X_COLS, pair, to_h)
        send(xe.at[side, pl.ds(core, 1)], hc.at[1 - side, pl.ds(5 - 5 * core, 1)], X_COLS, t_off * 2 + 1 - core, to_h)

    fetches[4].wait()
    grad = jnp.zeros((256, 256), F32)
    for first in range(0, 27, 2):
        taps = range(first, min(first + 2, 27))
        lhs = [s_buf[n % 9, 2 - n // 9 : 10 - n // 9, pl.ds(2 * core, 2)].reshape(256, 128) for n in taps]
        rhs = [w[n] for n in taps]
        if len(lhs) == 2:
            lhs, rhs = [jnp.concatenate(lhs, axis=1)], [jnp.concatenate(rhs, axis=1)]
        grad = grad + lax.dot_general(lhs[0], rhs[0], (((1,), (1,)), ((), ())), preferred_element_type=F32)

    fetches[2].wait()
    fetches[3].wait()
    arrived(STATS2, st2.at[pl.ds(0, 15)])
    first_four = lax.rem(lax.broadcasted_iota(jnp.int32, (4, 128), 1), 8) < 4
    sums = jnp.broadcast_to(jnp.sum(st2[...], axis=0), (4, 128))
    stats = group_totals(jnp.where(jnp.logical_and(mine, first_four), sums, 0.0)) / NUMBERS
    mean = jnp.concatenate([stats[0:1], stats[1:2]], axis=1)
    square = jnp.concatenate([stats[2:3], stats[3:4]], axis=1)
    inverse = lax.rsqrt(square - mean * mean + EPSILON)
    scale, shift = inverse * gain[...], bias[...]

    def activate(v):
        shifted = (v - mean) * scale + shift
        return shifted * jax.nn.sigmoid(shifted)

    normed = (xraw[:, pl.ds(1 + 2 * core, 2)].astype(F32).reshape(256, 256) - mean) * inverse
    shifted = normed * gain[...] + shift
    sig = jax.nn.sigmoid(shifted)
    grad = grad * sig * (1.0 + shifted * (1.0 - sig))
    d_gain = jnp.sum(grad * normed, axis=0, keepdims=True)
    d_bias = jnp.sum(grad, axis=0, keepdims=True)
    af[...] = jnp.concatenate([d_gain[:, :128], d_gain[:, 128:], d_bias[:, :128], d_bias[:, 128:]], axis=0)

    for to_h in others_h():
        send(af, at1.at[h], AFF1, tm, to_h)

    at1[h] = af[...]

    arrived(X_PAIR, xraw.at[:, pl.ds(0, 2)])
    for j in range(1, 5):
        act = activate(xraw[:, j].astype(F32).reshape(128, 256))
        acts[1, 2:10, j] = act.astype(BF16).reshape(8, 16, 256)

    turned = jnp.transpose(acts[1, 2:10, 1:5].reshape(512, 256))
    a_t[...] = turned.reshape(8, 2, 16, 512)

    zhi, x_at, zlo, y_at = t // 4, lax.rem(t, 4), h // 4, lax.rem(h, 4)
    z_at = 2 * zhi + zlo

    def products(first, count, keep):
        lhs = a_t[:, core].reshape(128, 512)
        for tap in range(first, first + count, 2):
            taps = range(tap, min(tap + 2, first + count))
            rhs = [s_buf[n % 9, 2 - n // 9 : 10 - n // 9].reshape(512, 128) for n in taps]
            rhs = jnp.concatenate(rhs, axis=1) if len(rhs) == 2 else rhs[0]
            out = jnp.dot(lhs, rhs, preferred_element_type=F32).astype(BF16)
            for i, n in enumerate(taps):
                keep(n - first, out[:, 128 * i : 128 * i + 128].reshape(8, 16, 128))

    def keep_x(n, tiles):
        for z in range(2):
            gx[:, 8 * z + n] = tiles[4 * z : 4 * z + 4]

    def keep_y(n, tiles):
        gy[n % 4, 8 * (n // 4) : 8 * (n // 4) + 8] = tiles

    def keep_z(n, tiles):
        for z in range(2):
            for x in range(4):
                gz[2 * z + n // 4, 4 * x + n % 4] = tiles[4 * z + x]

    def keep_extra(n, tiles):
        for to in range(4):
            if n == 0:
                first, second = to, to + 4
            elif n == 1:
                first, second = (to + 1) % 4, (to + 1) % 4 + 4
            else:
                first = 4 * (to // 2) + 2 * (to // 2 == to % 2)
                second = first + 1
            (gx, gy, gz)[n][to, 16] = tiles[first]
            (gx, gy, gz)[n][to, 17] = tiles[second]

    far = (2, 1, 3)
    products(24, 3, keep_extra)
    products(0, 8, keep_x)
    for k in far:
        to = lax.rem(x_at + k, 4)
        send(gx.at[to], rx.at[x_at], ALONG_X, (zhi * 4 + to) * 2 + core, h)
    products(8, 8, keep_y)
    for k in far:
        to = lax.rem(y_at + k, 4)
        send(gy.at[to], ry.at[y_at], ALONG_Y, tm, zlo * 4 + to)
    products(16, 8, keep_z)
    for k in far:
        to = lax.rem(z_at + k, 4)
        send(gz.at[to], rz.at[z_at], ALONG_Z, (to // 2 * 4 + x_at) * 2 + core, lax.rem(to, 2) * 4 + y_at)
    rx[x_at] = gx[x_at]
    ry[y_at] = gy[y_at]
    rz[z_at] = gz[z_at]

    @pl.loop(0, 48)
    def _(step):
        a = step // 16
        rows = pl.ds(pl.multiple_of(lax.rem(step, 16) * 16, 16), 16)
        taps = [[w[a * 9 + b * 3 + e, rows, :].astype(F32) for e in range(3)] for b in range(3)]
        for rc, bs in enumerate(((0,), (1, 2), (0, 1), (2,))):
            line = [taps[bs[0]][e] if len(bs) == 1 else taps[bs[0]][e] + taps[bs[1]][e] for e in range(3)]
            for cc, value in enumerate((line[0], line[1] + line[2], line[0] + line[1], line[2])):
                wc[a, rc, rows, 128 * cc : 128 * cc + 128] = value.astype(BF16)

    acts[:, 0:2] = jnp.zeros((3, 2, 6, 16, 256), BF16)
    arrived(X_ROWS, xraw.at[:, pl.ds(0, 1)])
    arrived(X_COLS, hc.at[:, pl.ds(0, 4)])
    border = 5 * core
    inside = jnp.where(core == 0, t > 0, t < CHIPS - 1)
    act = jnp.where(inside, activate(xraw[:, border].astype(F32).reshape(128, 256)), 0.0)
    acts[1, 2:10, border] = act.astype(BF16).reshape(8, 16, 256)
    pads = (pad0, pad1)

    @pl.loop(0, 4)
    def _(k):
        j = 2 * core + k
        here = jnp.logical_or(j != border, inside)
        act = acts[1, 2:10, j].astype(F32).reshape(128, 256)
        act_l = jnp.where(jnp.logical_and(here, h > 0), activate(hc[0, j]), 0.0)
        act_r = jnp.where(jnp.logical_and(here, h < HEIGHT - 1), activate(hc[1, j]), 0.0)
        for half in range(2):
            lanes = slice(128 * half, 128 * half + 128)
            pad = pads[half]
            for f in range(8):
                pad[32 * f + 8 : 32 * f + 24, :] = act[16 * f : 16 * f + 16, lanes]
            pad[pl.ds(7, 8, stride=32), :] = act_l[:, lanes]
            pad[pl.ds(24, 8, stride=32), :] = act_r[:, lanes]
            for f in range(8):
                acts[0, 2 + f, j, :, lanes] = pad[32 * f + 7 : 32 * f + 23, :].astype(BF16)
                acts[2, 2 + f, j, :, lanes] = pad[32 * f + 9 : 32 * f + 25, :].astype(BF16)

    def total_of(parts):
        return jnp.sum(parts[...].astype(F32), axis=0).astype(BF16)

    arrived(ALONG_X, rx.at[pl.ds(0, 3)])
    px[...] = total_of(rx)
    for dz in (1, 0):
        for k in (6, 2, 5, 7, 1, 3, 4, 0):
            if dz or k:
                to_z, to_h = lax.rem(zhi + dz, 2), lax.rem(h + k, 8)
                send(px.at[to_z * 8 + to_h], qx.at[zhi * 8 + h], LAST_X, (to_z * 4 + x_at) * 2 + core, to_h)
    arrived(ALONG_Y, ry.at[pl.ds(0, 3)])
    py[...] = total_of(ry)
    for dz in (1, 0):
        for k in (6, 2, 5, 7, 1, 3, 4, 0):
            if dz or k:
                to_z, to_t = lax.rem(zlo + dz, 2), lax.rem(t + k, 8)
                send(py.at[to_z * 8 + to_t], qy.at[zlo * 8 + t], LAST_Y, to_t * 2 + core, to_z * 4 + y_at)
    arrived(ALONG_Z, rz.at[pl.ds(0, 3)])
    pz[...] = total_of(rz)
    for dx in (2, 1, 3, 0):
        for dy in (2, 1, 3, 0):
            if dx or dy:
                to_x, to_y = lax.rem(x_at + dx, 4), lax.rem(y_at + dy, 4)
                send(pz.at[to_x * 4 + to_y], qz.at[x_at * 4 + y_at], LAST_Z, (zhi * 4 + to_x) * 2 + core, zlo * 4 + to_y)

    def extra(tile, at, to_t, to_h):
        here = jnp.logical_and(to_t == t, to_h == h)

        @pl.when(jnp.logical_not(here))
        def _():
            send(tile, qe.at[at], LAST_E, to_t * 2 + core, to_h)

        @pl.when(here)
        def _():
            qe[at] = tile[...]

    for i in range(2):
        to_t = 4 * i + x_at
        extra(px.at[16 + i], zhi * 8 + h, to_t, to_t)
        to_t = 4 * i + lax.rem(y_at + 1, 4)
        extra(py.at[16 + i], zlo * 8 + t, to_t, lax.rem(to_t + EXTRA[1], 8))
        to_t = 4 * zhi + jnp.where(zhi == zlo, 2, 0) + i
        extra(pz.at[16 + i], x_at * 4 + y_at, to_t, lax.rem(to_t + EXTRA[2], 8))
    qx[zhi * 8 + h] = px[zhi * 8 + h]
    qy[zlo * 8 + t] = py[zlo * 8 + t]
    qz[x_at * 4 + y_at] = pz[x_at * 4 + y_at]

    arrived(AFF1, at1.at[pl.ds(0, 7)])
    at[...] = jnp.sum(at1[...], axis=0)

    for to_tm in others_tm():
        send(at, at2.at[tm], AFF2, to_tm, h)

    at2[tm] = at[...]

    for p in range(2):
        even = jnp.zeros((256, 128), F32)
        odd = jnp.zeros((256, 128), F32)
        for rc, dr in ((0, -1), (1, 0)) if p == 0 else ((2, 0), (3, 1)):
            for a in range(3):
                lhs = [acts[dc, a : a + 8, pl.ds(2 * core + 1 + dr, 2)].reshape(256, 256) for dc in range(3)]
                both = jnp.dot(lhs[1], wc[a, rc, :, 128:384], preferred_element_type=F32)
                even = even + both[:, :128] + jnp.dot(lhs[0], wc[a, rc, :, 0:128], preferred_element_type=F32)
                odd = odd + both[:, 128:] + jnp.dot(lhs[2], wc[a, rc, :, 384:512], preferred_element_type=F32)
        for f in range(8):
            for row in range(2):
                at_row = (f * 4 + 2 * row + p) * 32
                here = (f * 2 + row) * 16
                d_buf[pl.ds(at_row, 16, stride=2), :] = even[here : here + 16]
                d_buf[pl.ds(at_row + 1, 16, stride=2), :] = odd[here : here + 16]
    dec[...] = d_buf[...].astype(BF16).reshape(8, 4, 32, 128)

    owners = [lax.rem(t + shift_h, 8) for shift_h in EXTRA]
    has_extra = jnp.logical_or(h == owners[0], jnp.logical_or(h == owners[1], h == owners[2]))
    for i, (kind, parts) in enumerate(((LAST_X, qx), (LAST_Y, qy), (LAST_Z, qz))):
        arrived(kind, parts.at[pl.ds(0, 15)])
        ag_s[i] = total_of(parts)

    @pl.when(has_extra)
    def _():
        arrived(LAST_E, qe.at[pl.ds(0, 15)])
        ag_s[3] = total_of(qe)

    @pl.when(jnp.logical_not(has_extra))
    def _():
        ag_s[3] = jnp.zeros((16, 128), BF16)

    for to_h in others_h():
        send(ag_s, ag_r.at[h], GATHER, tm, to_h)

    ag_r[h] = ag_s[...]

    arrived(AFF2, at2.at[pl.ds(0, 15)])
    total = jnp.sum(at2[...], axis=0)
    aff[0:1, 0:128] = total[0:1]
    aff[0:1, 128:256] = total[1:2]
    aff[1:2, 0:128] = total[2:3]
    aff[1:2, 128:256] = total[3:4]

    arrived(GATHER, ag_r.at[pl.ds(0, 7)])
    for k in range(8):
        for i in range(3):
            gw[8 * i + k] = ag_r[k, i].astype(F32)
    for i in range(3):
        gw[24 + i] = ag_r[owners[i], 3].astype(F32)

    sent(BLOCKS, xraw.at[pl.ds(0, 7), pl.ds(0, 2)])
    sent(COT_PAIR, cpart)
    sent(COT_ROWS, cedge)
    sent(COT_COLS, ch)
    sent(X_PAIR, xraw.at[:, pl.ds(0, 2)])
    sent(X_ROWS, xraw.at[:, pl.ds(0, 1)])
    sent(X_COLS, hc.at[:, pl.ds(0, 4)])
    for kind, parts in ((ALONG_X, rx), (ALONG_Y, ry), (ALONG_Z, rz)):
        sent(kind, parts.at[pl.ds(0, 3)])
    for kind, parts in ((LAST_X, qx), (LAST_Y, qy), (LAST_Z, qz)):
        sent(kind, parts.at[pl.ds(0, 15)])
    sent(LAST_E, qe.at[pl.ds(0, 5)])

    @pl.when(jnp.logical_not(has_extra))
    def _():
        sent(LAST_E, qe.at[0])

    sent(GATHER, ag_r.at[pl.ds(0, 7)])
    sent(STATS1, st1.at[pl.ds(0, 7)])
    sent(STATS2, st2.at[pl.ds(0, 15)])
    sent(AFF1, at1.at[pl.ds(0, 7)])
    sent(AFF2, at2.at[pl.ds(0, 15)])


def deliver(*refs):
    copies = [pltpu.make_async_copy(refs[i], refs[3 + i], refs[6].at[i]) for i in range(3)]
    for copy in copies:
        copy.start()
    for copy in copies:
        copy.wait()


def per_device(coarse, gain, bias, weight, cotangent):
    taps = jnp.transpose(weight, (1, 2, 3, 0, 4)).reshape(27, 256, 128)
    vmem = pl.BlockSpec(memory_space=pltpu.VMEM)
    vm = pltpu.VMEM
    decoded, grad_weight, grad_affine = pl.pallas_call(
        kernel,
        out_shape=(
            jax.ShapeDtypeStruct((8, 4, 32, 128), BF16),
            jax.ShapeDtypeStruct((27, 16, 128), F32),
            jax.ShapeDtypeStruct((2, 256), F32),
        ),
        in_specs=[pl.BlockSpec(memory_space=pltpu.HBM)] * 5,
        out_specs=(vmem, vmem, vmem),
        scratch_shapes=[
            vm((2, 128, 256), BF16),
            vm((1, 256), F32),
            vm((1, 256), F32),
            vm((27, 256, 128), BF16),
            vm((8, 4, 32, 128), BF16),
            pltpu.SemaphoreType.DMA((5,)),
            vm((3, 4, 256, 512), BF16),
            vm((1, 128), F32),
            vm((1, 128), F32),
            vm((8, 1, 128), F32),
            vm((16, 1, 128), F32),
            vm((4, 128), F32),
            vm((4, 128), F32),
            vm((8, 4, 128), F32),
            vm((16, 4, 128), F32),
            vm((8, 6, 16, 256), BF16),
            vm((2, 128, 128), F32),
            vm((2, 2, 8, 256), F32),
            vm((2, 6, 8, 256), F32),
            vm((3, 10, 6, 16, 256), BF16),
            vm((256, 128), F32),
            vm((256, 128), F32),
            vm((8, 2, 16, 512), BF16),
            vm((8, 4, 32, 128), BF16),
            vm((2, 8, 1, 32, 128), BF16),
            vm((2, 4, 8, 128), F32),
            vm((2, 10, 8, 128), F32),
            vm((10 * 8 * 48, 128), F32),
            vm((9, 10, 4, 16, 128), BF16),
            *[vm((4, 18, 16, 128), BF16)] * 6,
            *[vm((18, 16, 128), BF16)] * 3,
            *[vm((16, 16, 128), BF16)] * 4,
            vm((4, 16, 128), BF16),
            vm((8, 4, 16, 128), BF16),
            vm((1024, 128), F32),
            pltpu.SemaphoreType.DMA((19,)),
            pltpu.SemaphoreType.DMA((19,)),
        ],
        compiler_params=pltpu.CompilerParams(
            collective_id=0, has_side_effects=True, vmem_limit_bytes=48 * 2**20
        ),
        cost_estimate=pl.CostEstimate(flops=2 * 10**9, bytes_accessed=4 * 10**6, transcendentals=300000),
    )(*[
        pltpu.with_memory_space_constraint(x, pltpu.HBM)
        for x in (coarse.reshape(2, 128, 256), gain.reshape(1, 256), bias.reshape(1, 256), taps, cotangent)
    ])
    decoded, grad_weight, grad_affine = pl.pallas_call(
        deliver,
        out_shape=(
            jax.ShapeDtypeStruct((8, 4, 32, 128), BF16),
            jax.ShapeDtypeStruct((27, 16, 128), F32),
            jax.ShapeDtypeStruct((2, 256), F32),
        ),
        in_specs=[pl.BlockSpec(memory_space=pltpu.VMEM)] * 3,
        out_specs=[pl.BlockSpec(memory_space=pl.ANY)] * 3,
        scratch_shapes=[pltpu.SemaphoreType.DMA((3,))],
        compiler_params=pltpu.CompilerParams(vmem_limit_bytes=8 * 2**20),
    )(decoded, grad_weight, grad_affine)
    grad_weight = jnp.transpose(grad_weight.reshape(3, 3, 3, 16, 128), (3, 0, 1, 2, 4))
    return decoded, grad_weight, grad_affine


def solution(mesh):
    return jax.shard_map(
        per_device,
        mesh=mesh,
        in_specs=(P("height", "tm", None, None), P(), P(), P(), P(None, "tm", "height", None)),
        out_specs=(P(None, "tm", "height", None), P("tm", None, None, None, None), P()),
        check_vma=False,
    )
```

```python
import functools

import jax
import jax.numpy as jnp
from jax import lax
from jax.experimental import pallas as pl
from jax.experimental.pallas import tpu as pltpu
from jax.sharding import PartitionSpec as P

MESH = pl.DeviceIdType.MESH
F32, BF16 = jnp.float32, jnp.bfloat16
EPSILON = 1e-06
NUMBERS = 8 * 32 * 128 * 8
CHIPS, HEIGHT = 8, 8
EXTRA = (0, 3, 6)

(STATS1, STATS2, BLOCKS, COT_PAIR, COT_ROWS, COT_COLS, X_PAIR, X_ROWS, X_COLS, ALONG_X, ALONG_Y, ALONG_Z, LAST_X, LAST_Y, LAST_Z, LAST_E, GATHER, AFF1, AFF2) = range(19)


def group_totals(tile):
    lane = lax.broadcasted_iota(jnp.int32, tile.shape, 1)
    for step in (1, 2, 4):
        other = jnp.where(
            (lane & step) == 0, pltpu.roll(tile, 128 - step, 1), pltpu.roll(tile, step, 1)
        )
        tile = tile + other
    return tile


def kernel(
    coarse_hbm, gain_hbm, bias_hbm, w_hbm, cot_hbm, dec, gw, aff,
    coarse, gain, bias, w, cot, fetch_sem, wc, st, sa, st1, st2, af, at, at1, at2,
    xraw, xf, xe, hc, acts, pad0, pad1, a_t,
    cpart, cedge, ce, ch, cf, s_buf,
    gx, gy, gz, rx, ry, rz, px, py, pz, qx, qy, qz, qe, ag_s, ag_r, d_buf, ssem, rsem,
):
    tm, h = lax.axis_index("tm"), lax.axis_index("height")
    core = lax.rem(tm, 2)
    t = tm // 2
    left, right = lax.rem(h + 7, 8), lax.rem(h + 1, 8)
    t_off = lax.rem(t + 7 + 2 * core, 8)
    pair = tm + 1 - 2 * core

    def others_h():
        for dz, dy in ((1, 2), (1, 1), (1, 3), (0, 2), (1, 0), (0, 1), (0, 3)):
            yield lax.rem(h // 4 + dz, 2) * 4 + lax.rem(h + dy, 4)

    def others_tm():
        for dz, dx in ((1, 2), (1, 1), (1, 3), (1, 0), (0, 2), (0, 1), (0, 3)):
            chip = lax.rem(t // 4 + dz, 2) * 4 + lax.rem(t + dx, 4)
            yield 2 * chip + core
            yield 2 * chip + 1 - core
        yield pair

    def send(src, dst, kind, to_tm, to_h):
        pltpu.make_async_remote_copy(
            src_ref=src, dst_ref=dst, send_sem=ssem.at[kind], recv_sem=rsem.at[kind],
            device_id=(to_tm, to_h), device_id_type=MESH,
        ).start()

    def arrived(kind, like):
        pltpu.make_async_copy(like, like, rsem.at[kind]).wait()

    def sent(kind, like):
        pltpu.make_async_copy(like, like, ssem.at[kind]).wait()

    pairs = ((coarse_hbm, coarse), (cot_hbm, cot), (gain_hbm, gain), (bias_hbm, bias), (w_hbm, w))
    fetches = [pltpu.make_async_copy(src, dst, fetch_sem.at[i]) for i, (src, dst) in enumerate(pairs)]
    for fetch in fetches:
        fetch.start()

    barrier = pltpu.get_barrier_semaphore()

    def greet(to_tm, to_h):
        pl.semaphore_signal(barrier, inc=1, device_id=(to_tm, to_h), device_id_type=MESH)

    for to_tm in others_tm():
        greet(to_tm, h)
    for to_h in others_h():
        greet(tm, to_h)

    greet(pair, left)
    greet(pair, right)

    @pl.loop(0, 4)
    def _(k):
        to_tm = lax.rem(t + 7 + 2 * (k // 2), 8) * 2 + lax.rem(k, 2)
        greet(to_tm, left)
        greet(to_tm, right)

    fetches[0].wait()
    x = coarse[...].astype(F32).reshape(256, 256)
    total = jnp.sum(x, axis=0, keepdims=True)
    squares = jnp.sum(x * x, axis=0, keepdims=True)
    quarters = (total[:, :128], total[:, 128:], squares[:, :128], squares[:, 128:])
    quarter = lax.rem(lax.broadcasted_iota(jnp.int32, (4, 128), 1), 4)
    mine = quarter == lax.broadcasted_iota(jnp.int32, (4, 128), 0)
    sums = group_totals(jnp.concatenate(quarters, axis=0))
    st[...] = jnp.sum(jnp.where(mine, sums, 0.0), axis=0, keepdims=True)

    pl.semaphore_wait(barrier, 32)

    for to_h in others_h():
        send(st, st1.at[h], STATS1, tm, to_h)

    for to_h in others_h():
        send(
            coarse.at[:, pl.ds(pl.multiple_of(to_h * 16, 16), 16), :],
            xraw.at[h, pl.ds(1 + 2 * core, 2)], BLOCKS, tm, to_h,
        )

    fetches[1].wait()
    send(cot, cpart, COT_PAIR, pair, h)
    for c2 in range(2):
        send(cot.at[:, pl.ds(3 * core, 1)], cedge.at[1 - core], COT_ROWS, t_off * 2 + c2, h)
    def cell(j, f):
        return pl.multiple_of((j * 8 + f) * 48, 8)

    for r in range(4):
        for f in range(8):
            cf[pl.ds(cell(1 + 4 * core + r, f) + 8, 32), :] = cot[f, r].astype(F32)
    for r in range(4):
        base = cell(1 + 4 * core + r, 0)
        ce[0, r] = cf[pl.ds(base + 8, 8, stride=48), :]
        ce[1, r] = cf[pl.ds(base + 39, 8, stride=48), :]

    for side, to_h in ((0, left), (1, right)):
        for c2 in range(2):
            send(ce.at[side], ch.at[1 - side, pl.ds(1 + 4 * core, 4)], COT_COLS, 2 * t + c2, to_h)
            send(ce.at[side, pl.ds(3 * core, 1)], ch.at[1 - side, pl.ds(9 - 9 * core, 1)], COT_COLS, t_off * 2 + c2, to_h)

    st1[h] = st[...]
    xraw[h, pl.ds(1 + 2 * core, 2)] = coarse[:, pl.ds(pl.multiple_of(h * 16, 16), 16), :]

    arrived(STATS1, st1.at[pl.ds(0, 7)])
    sa[...] = jnp.sum(st1[...], axis=0)

    for to_tm in others_tm():
        send(sa, st2.at[tm], STATS2, to_tm, h)

    st2[tm] = sa[...]

    arrived(BLOCKS, xraw.at[pl.ds(0, 7), pl.ds(0, 2)])
    own = xraw.at[:, pl.ds(1 + 2 * core, 2)]
    send(own, own, X_PAIR, pair, h)
    send(xraw.at[:, pl.ds(1 + 3 * core, 1)], xraw.at[:, pl.ds(5 - 5 * core, 1)], X_ROWS, t_off * 2 + 1 - core, h)

    s_buf[:, 8:10] = jnp.zeros((9, 2, 4, 16, 128), BF16)
    arrived(COT_PAIR, cpart)
    arrived(COT_ROWS, cedge)
    arrived(COT_COLS, ch)
    for r in range(4):
        for f in range(8):
            cf[pl.ds(cell(5 - 4 * core + r, f) + 8, 32), :] = cpart[f, r].astype(F32)
    top, bottom = t > 0, t < CHIPS - 1
    for f in range(8):
        cf[pl.ds(cell(0, f) + 8, 32), :] = jnp.where(top, cedge[0, f, 0].astype(F32), 0.0)
        cf[pl.ds(cell(9, f) + 8, 32), :] = jnp.where(bottom, cedge[1, f, 0].astype(F32), 0.0)
    for j in range(10):
        keep = (h > 0, h < HEIGHT - 1)
        if j == 0:
            keep = tuple(jnp.logical_and(k, top) for k in keep)
        if j == 9:
            keep = tuple(jnp.logical_and(k, bottom) for k in keep)
        cf[pl.ds(j * 384 + 7, 8, stride=48), :] = jnp.where(keep[0], ch[0, j], 0.0)
        cf[pl.ds(j * 384 + 40, 8, stride=48), :] = jnp.where(keep[1], ch[1, j], 0.0)

    @pl.loop(0, 8)
    def _(f):
        sums = []
        for j in range(10):
            base = cell(j, f)
            cols = [cf[pl.ds(base + 7 + i, 16, stride=2), :] for i in range(4)]
            sums.append((cols[2] + cols[3], cols[1] + cols[2], cols[0] + cols[1]))
        for b in range(3):
            for e in range(3):
                for row in range(4):
                    s_buf[b * 3 + e, f, row] = (sums[2 * row + 2 - b][e] + sums[2 * row + 3 - b][e]).astype(BF16)

    for r in range(2):
        rows = xraw[:, 1 + 2 * core + r].astype(F32).reshape(128, 256)
        for half in range(2):
            xf[half, 0:128, :] = rows[:, 128 * half : 128 * half + 128]
            for side, column in ((0, 0), (1, 15)):
                xe[side, r, :, 128 * half : 128 * half + 128] = xf.at[half][pl.ds(column, 8, stride=16), :]
    for side, to_h in ((0, left), (1, right)):
        send(xe.at[side], hc.at[1 - side, pl.ds(1 + 2 * core, 2)], X_COLS, tm, to_h)
        send(xe.at[side, pl.ds(1 - core, 1)], hc.at[1 - side, pl.ds(2 + core, 1)], X_COLS, pair, to_h)
        send(xe.at[side, pl.ds(core, 1)], hc.at[1 - side, pl.ds(5 - 5 * core, 1)], X_COLS, t_off * 2 + 1 - core, to_h)

    fetches[2].wait()
    fetches[3].wait()
    arrived(STATS2, st2.at[pl.ds(0, 15)])
    first_four = lax.rem(lax.broadcasted_iota(jnp.int32, (4, 128), 1), 8) < 4
    sums = jnp.broadcast_to(jnp.sum(st2[...], axis=0), (4, 128))
    stats = group_totals(jnp.where(jnp.logical_and(mine, first_four), sums, 0.0)) / NUMBERS
    mean = jnp.concatenate([stats[0:1], stats[1:2]], axis=1)
    square = jnp.concatenate([stats[2:3], stats[3:4]], axis=1)
    inverse = lax.rsqrt(square - mean * mean + EPSILON)
    scale, shift = inverse * gain[...], bias[...]

    def activate(v):
        shifted = (v - mean) * scale + shift
        return shifted * jax.nn.sigmoid(shifted)

    arrived(X_PAIR, xraw.at[:, pl.ds(0, 2)])
    for j in range(1, 5):
        act = activate(xraw[:, j].astype(F32).reshape(128, 256))
        acts[1, 2:10, j] = act.astype(BF16).reshape(8, 16, 256)

    turned = jnp.transpose(acts[1, 2:10, 1:5].reshape(512, 256))
    a_t[...] = turned.reshape(8, 2, 16, 512)

    zhi, x_at, zlo, y_at = t // 4, lax.rem(t, 4), h // 4, lax.rem(h, 4)
    z_at = 2 * zhi + zlo

    def products(first, count, keep):
        lhs = a_t[:, core].reshape(128, 512)
        for tap in range(first, first + count, 2):
            taps = range(tap, min(tap + 2, first + count))
            rhs = [s_buf[n % 9, 2 - n // 9 : 10 - n // 9].reshape(512, 128) for n in taps]
            rhs = jnp.concatenate(rhs, axis=1) if len(rhs) == 2 else rhs[0]
            out = jnp.dot(lhs, rhs, preferred_element_type=F32).astype(BF16)
            for i, n in enumerate(taps):
                keep(n - first, out[:, 128 * i : 128 * i + 128].reshape(8, 16, 128))

    def keep_x(n, tiles):
        for z in range(2):
            gx[:, 8 * z + n] = tiles[4 * z : 4 * z + 4]

    def keep_y(n, tiles):
        gy[n % 4, 8 * (n // 4) : 8 * (n // 4) + 8] = tiles

    def keep_z(n, tiles):
        for z in range(2):
            for x in range(4):
                gz[2 * z + n // 4, 4 * x + n % 4] = tiles[4 * z + x]

    def keep_extra(n, tiles):
        for to in range(4):
            if n == 0:
                first, second = to, to + 4
            elif n == 1:
                first, second = (to + 1) % 4, (to + 1) % 4 + 4
            else:
                first = 4 * (to // 2) + 2 * (to // 2 == to % 2)
                second = first + 1
            (gx, gy, gz)[n][to, 16] = tiles[first]
            (gx, gy, gz)[n][to, 17] = tiles[second]

    far = (2, 1, 3)
    products(24, 3, keep_extra)
    products(0, 8, keep_x)
    for k in far:
        to = lax.rem(x_at + k, 4)
        send(gx.at[to], rx.at[x_at], ALONG_X, (zhi * 4 + to) * 2 + core, h)
    products(8, 8, keep_y)
    for k in far:
        to = lax.rem(y_at + k, 4)
        send(gy.at[to], ry.at[y_at], ALONG_Y, tm, zlo * 4 + to)
    products(16, 8, keep_z)
    for k in far:
        to = lax.rem(z_at + k, 4)
        send(gz.at[to], rz.at[z_at], ALONG_Z, (to // 2 * 4 + x_at) * 2 + core, lax.rem(to, 2) * 4 + y_at)
    rx[x_at] = gx[x_at]
    ry[y_at] = gy[y_at]
    rz[z_at] = gz[z_at]
    fetches[4].wait()
    grad = jnp.zeros((256, 256), F32)
    for first in range(0, 27, 2):
        taps = range(first, min(first + 2, 27))
        lhs = [s_buf[n % 9, 2 - n // 9 : 10 - n // 9, pl.ds(2 * core, 2)].reshape(256, 128) for n in taps]
        rhs = [w[n] for n in taps]
        if len(lhs) == 2:
            lhs, rhs = [jnp.concatenate(lhs, axis=1)], [jnp.concatenate(rhs, axis=1)]
        grad = grad + lax.dot_general(lhs[0], rhs[0], (((1,), (1,)), ((), ())), preferred_element_type=F32)

    normed = (xraw[:, pl.ds(1 + 2 * core, 2)].astype(F32).reshape(256, 256) - mean) * inverse
    shifted = normed * gain[...] + shift
    sig = jax.nn.sigmoid(shifted)
    grad = grad * sig * (1.0 + shifted * (1.0 - sig))
    d_gain = jnp.sum(grad * normed, axis=0, keepdims=True)
    d_bias = jnp.sum(grad, axis=0, keepdims=True)
    af[...] = jnp.concatenate([d_gain[:, :128], d_gain[:, 128:], d_bias[:, :128], d_bias[:, 128:]], axis=0)

    for to_h in others_h():
        send(af, at1.at[h], AFF1, tm, to_h)

    at1[h] = af[...]


    @pl.loop(0, 48)
    def _(step):
        a = step // 16
        rows = pl.ds(pl.multiple_of(lax.rem(step, 16) * 16, 16), 16)
        taps = [[w[a * 9 + b * 3 + e, rows, :].astype(F32) for e in range(3)] for b in range(3)]
        for rc, bs in enumerate(((0,), (1, 2), (0, 1), (2,))):
            line = [taps[bs[0]][e] if len(bs) == 1 else taps[bs[0]][e] + taps[bs[1]][e] for e in range(3)]
            for cc, value in enumerate((line[0], line[1] + line[2], line[0] + line[1], line[2])):
                wc[a, rc, rows, 128 * cc : 128 * cc + 128] = value.astype(BF16)

    acts[:, 0:2] = jnp.zeros((3, 2, 6, 16, 256), BF16)
    arrived(X_ROWS, xraw.at[:, pl.ds(0, 1)])
    arrived(X_COLS, hc.at[:, pl.ds(0, 4)])
    border = 5 * core
    inside = jnp.where(core == 0, t > 0, t < CHIPS - 1)
    act = jnp.where(inside, activate(xraw[:, border].astype(F32).reshape(128, 256)), 0.0)
    acts[1, 2:10, border] = act.astype(BF16).reshape(8, 16, 256)
    pads = (pad0, pad1)

    @pl.loop(0, 4)
    def _(k):
        j = 2 * core + k
        here = jnp.logical_or(j != border, inside)
        act = acts[1, 2:10, j].astype(F32).reshape(128, 256)
        act_l = jnp.where(jnp.logical_and(here, h > 0), activate(hc[0, j]), 0.0)
        act_r = jnp.where(jnp.logical_and(here, h < HEIGHT - 1), activate(hc[1, j]), 0.0)
        for half in range(2):
            lanes = slice(128 * half, 128 * half + 128)
            pad = pads[half]
            for f in range(8):
                pad[32 * f + 8 : 32 * f + 24, :] = act[16 * f : 16 * f + 16, lanes]
            pad[pl.ds(7, 8, stride=32), :] = act_l[:, lanes]
            pad[pl.ds(24, 8, stride=32), :] = act_r[:, lanes]
            for f in range(8):
                acts[0, 2 + f, j, :, lanes] = pad[32 * f + 7 : 32 * f + 23, :].astype(BF16)
                acts[2, 2 + f, j, :, lanes] = pad[32 * f + 9 : 32 * f + 25, :].astype(BF16)

    def total_of(parts):
        return jnp.sum(parts[...].astype(F32), axis=0).astype(BF16)

    arrived(ALONG_X, rx.at[pl.ds(0, 3)])
    px[...] = total_of(rx)
    for dz in (1, 0):
        for k in (6, 2, 5, 7, 1, 3, 4, 0):
            if dz or k:
                to_z, to_h = lax.rem(zhi + dz, 2), lax.rem(h + k, 8)
                send(px.at[to_z * 8 + to_h], qx.at[zhi * 8 + h], LAST_X, (to_z * 4 + x_at) * 2 + core, to_h)
    arrived(ALONG_Y, ry.at[pl.ds(0, 3)])
    py[...] = total_of(ry)
    for dz in (1, 0):
        for k in (6, 2, 5, 7, 1, 3, 4, 0):
            if dz or k:
                to_z, to_t = lax.rem(zlo + dz, 2), lax.rem(t + k, 8)
                send(py.at[to_z * 8 + to_t], qy.at[zlo * 8 + t], LAST_Y, to_t * 2 + core, to_z * 4 + y_at)
    arrived(ALONG_Z, rz.at[pl.ds(0, 3)])
    pz[...] = total_of(rz)
    for dx in (2, 1, 3, 0):
        for dy in (2, 1, 3, 0):
            if dx or dy:
                to_x, to_y = lax.rem(x_at + dx, 4), lax.rem(y_at + dy, 4)
                send(pz.at[to_x * 4 + to_y], qz.at[x_at * 4 + y_at], LAST_Z, (zhi * 4 + to_x) * 2 + core, zlo * 4 + to_y)

    def extra(tile, at, to_t, to_h):
        here = jnp.logical_and(to_t == t, to_h == h)

        @pl.when(jnp.logical_not(here))
        def _():
            send(tile, qe.at[at], LAST_E, to_t * 2 + core, to_h)

        @pl.when(here)
        def _():
            qe[at] = tile[...]

    for i in range(2):
        to_t = 4 * i + x_at
        extra(px.at[16 + i], zhi * 8 + h, to_t, to_t)
        to_t = 4 * i + lax.rem(y_at + 1, 4)
        extra(py.at[16 + i], zlo * 8 + t, to_t, lax.rem(to_t + EXTRA[1], 8))
        to_t = 4 * zhi + jnp.where(zhi == zlo, 2, 0) + i
        extra(pz.at[16 + i], x_at * 4 + y_at, to_t, lax.rem(to_t + EXTRA[2], 8))
    qx[zhi * 8 + h] = px[zhi * 8 + h]
    qy[zlo * 8 + t] = py[zlo * 8 + t]
    qz[x_at * 4 + y_at] = pz[x_at * 4 + y_at]

    arrived(AFF1, at1.at[pl.ds(0, 7)])
    at[...] = jnp.sum(at1[...], axis=0)

    for to_tm in others_tm():
        send(at, at2.at[tm], AFF2, to_tm, h)

    at2[tm] = at[...]

    for p in range(2):
        even = jnp.zeros((256, 128), F32)
        odd = jnp.zeros((256, 128), F32)
        for rc, dr in ((0, -1), (1, 0)) if p == 0 else ((2, 0), (3, 1)):
            for a in range(3):
                lhs = [acts[dc, a : a + 8, pl.ds(2 * core + 1 + dr, 2)].reshape(256, 256) for dc in range(3)]
                both = jnp.dot(lhs[1], wc[a, rc, :, 128:384], preferred_element_type=F32)
                even = even + both[:, :128] + jnp.dot(lhs[0], wc[a, rc, :, 0:128], preferred_element_type=F32)
                odd = odd + both[:, 128:] + jnp.dot(lhs[2], wc[a, rc, :, 384:512], preferred_element_type=F32)
        for f in range(8):
            for row in range(2):
                at_row = (f * 4 + 2 * row + p) * 32
                here = (f * 2 + row) * 16
                d_buf[pl.ds(at_row, 16, stride=2), :] = even[here : here + 16]
                d_buf[pl.ds(at_row + 1, 16, stride=2), :] = odd[here : here + 16]
    dec[...] = d_buf[0:1024, :].astype(BF16).reshape(8, 4, 32, 128)

    owners = [lax.rem(t + shift_h, 8) for shift_h in EXTRA]
    has_extra = jnp.logical_or(h == owners[0], jnp.logical_or(h == owners[1], h == owners[2]))
    for i, (kind, parts) in enumerate(((LAST_X, qx), (LAST_Y, qy), (LAST_Z, qz))):
        arrived(kind, parts.at[pl.ds(0, 15)])
        ag_s[i] = total_of(parts)

    @pl.when(has_extra)
    def _():
        arrived(LAST_E, qe.at[pl.ds(0, 15)])
        ag_s[3] = total_of(qe)

    @pl.when(jnp.logical_not(has_extra))
    def _():
        ag_s[3] = jnp.zeros((16, 128), BF16)

    for to_h in others_h():
        send(ag_s, ag_r.at[h], GATHER, tm, to_h)

    ag_r[h] = ag_s[...]

    arrived(AFF2, at2.at[pl.ds(0, 15)])
    total = jnp.sum(at2[...], axis=0)
    aff[0:1, 0:128] = total[0:1]
    aff[0:1, 128:256] = total[1:2]
    aff[1:2, 0:128] = total[2:3]
    aff[1:2, 128:256] = total[3:4]

    arrived(GATHER, ag_r.at[pl.ds(0, 7)])
    for k in range(8):
        for i in range(3):
            gw[8 * i + k] = ag_r[k, i].astype(F32)
    for i in range(3):
        gw[24 + i] = ag_r[owners[i], 3].astype(F32)

    sent(BLOCKS, xraw.at[pl.ds(0, 7), pl.ds(0, 2)])
    sent(COT_PAIR, cpart)
    sent(COT_ROWS, cedge)
    sent(COT_COLS, ch)
    sent(X_PAIR, xraw.at[:, pl.ds(0, 2)])
    sent(X_ROWS, xraw.at[:, pl.ds(0, 1)])
    sent(X_COLS, hc.at[:, pl.ds(0, 4)])
    for kind, parts in ((ALONG_X, rx), (ALONG_Y, ry), (ALONG_Z, rz)):
        sent(kind, parts.at[pl.ds(0, 3)])
    for kind, parts in ((LAST_X, qx), (LAST_Y, qy), (LAST_Z, qz)):
        sent(kind, parts.at[pl.ds(0, 15)])
    sent(LAST_E, qe.at[pl.ds(0, 5)])

    @pl.when(jnp.logical_not(has_extra))
    def _():
        sent(LAST_E, qe.at[0])

    sent(GATHER, ag_r.at[pl.ds(0, 7)])
    sent(STATS1, st1.at[pl.ds(0, 7)])
    sent(STATS2, st2.at[pl.ds(0, 15)])
    sent(AFF1, at1.at[pl.ds(0, 7)])
    sent(AFF2, at2.at[pl.ds(0, 15)])


def deliver(*refs):
    copies = [pltpu.make_async_copy(refs[i], refs[3 + i], refs[6].at[i]) for i in range(3)]
    for copy in copies:
        copy.start()
    for copy in copies:
        copy.wait()


def per_device(coarse, gain, bias, weight, cotangent):
    taps = jnp.transpose(weight, (1, 2, 3, 0, 4)).reshape(27, 256, 128)
    vmem = pl.BlockSpec(memory_space=pltpu.VMEM)
    vm = pltpu.VMEM
    decoded, grad_weight, grad_affine = pl.pallas_call(
        kernel,
        out_shape=(
            jax.ShapeDtypeStruct((8, 4, 32, 128), BF16),
            jax.ShapeDtypeStruct((27, 16, 128), F32),
            jax.ShapeDtypeStruct((2, 256), F32),
        ),
        in_specs=[pl.BlockSpec(memory_space=pltpu.HBM)] * 5,
        out_specs=(vmem, vmem, vmem),
        scratch_shapes=[
            vm((2, 128, 256), BF16),
            vm((1, 256), F32),
            vm((1, 256), F32),
            vm((27, 256, 128), BF16),
            vm((8, 4, 32, 128), BF16),
            pltpu.SemaphoreType.DMA((5,)),
            vm((3, 4, 256, 512), BF16),
            vm((1, 128), F32),
            vm((1, 128), F32),
            vm((8, 1, 128), F32),
            vm((16, 1, 128), F32),
            vm((4, 128), F32),
            vm((4, 128), F32),
            vm((8, 4, 128), F32),
            vm((16, 4, 128), F32),
            vm((8, 6, 16, 256), BF16),
            vm((2, 144, 128), F32),
            vm((2, 2, 8, 256), F32),
            vm((2, 6, 8, 256), F32),
            vm((3, 10, 6, 16, 256), BF16),
            vm((288, 128), F32),
            vm((288, 128), F32),
            vm((8, 2, 16, 512), BF16),
            vm((8, 4, 32, 128), BF16),
            vm((2, 8, 1, 32, 128), BF16),
            vm((2, 4, 8, 128), F32),
            vm((2, 10, 8, 128), F32),
            vm((10 * 8 * 48 + 64, 128), F32),
            vm((9, 10, 4, 16, 128), BF16),
            *[vm((4, 18, 16, 128), BF16)] * 6,
            *[vm((18, 16, 128), BF16)] * 3,
            *[vm((16, 16, 128), BF16)] * 4,
            vm((4, 16, 128), BF16),
            vm((8, 4, 16, 128), BF16),
            vm((1056, 128), F32),
            pltpu.SemaphoreType.DMA((19,)),
            pltpu.SemaphoreType.DMA((19,)),
        ],
        compiler_params=pltpu.CompilerParams(
            collective_id=0, has_side_effects=True, vmem_limit_bytes=48 * 2**20
        ),
        cost_estimate=pl.CostEstimate(flops=2 * 10**9, bytes_accessed=4 * 10**6, transcendentals=300000),
    )(*[
        pltpu.with_memory_space_constraint(x, pltpu.HBM)
        for x in (coarse.reshape(2, 128, 256), gain.reshape(1, 256), bias.reshape(1, 256), taps, cotangent)
    ])
    decoded, grad_weight, grad_affine = pl.pallas_call(
        deliver,
        out_shape=(
            jax.ShapeDtypeStruct((8, 4, 32, 128), BF16),
            jax.ShapeDtypeStruct((27, 16, 128), F32),
            jax.ShapeDtypeStruct((2, 256), F32),
        ),
        in_specs=[pl.BlockSpec(memory_space=pltpu.VMEM)] * 3,
        out_specs=[pl.BlockSpec(memory_space=pl.ANY)] * 3,
        scratch_shapes=[pltpu.SemaphoreType.DMA((3,))],
        compiler_params=pltpu.CompilerParams(vmem_limit_bytes=8 * 2**20),
    )(decoded, grad_weight, grad_affine)
    grad_weight = jnp.transpose(grad_weight.reshape(3, 3, 3, 16, 128), (3, 0, 1, 2, 4))
    return decoded, grad_weight, grad_affine


def solution(mesh):
    return jax.shard_map(
        per_device,
        mesh=mesh,
        in_specs=(P("height", "tm", None, None), P(), P(), P(), P(None, "tm", "height", None)),
        out_specs=(P(None, "tm", "height", None), P("tm", None, None, None, None), P()),
        check_vma=False,
    )
```

```python
import functools

import jax
import jax.numpy as jnp
from jax import lax
from jax.experimental import pallas as pl
from jax.experimental.pallas import tpu as pltpu
from jax.sharding import PartitionSpec as P

MESH = pl.DeviceIdType.MESH
F32, BF16 = jnp.float32, jnp.bfloat16
EPSILON = 1e-06
NUMBERS = 8 * 32 * 128 * 8
CHIPS, HEIGHT = 8, 8
EXTRA = (0, 3, 6)

(STATS1, STATS2, BLOCKS, COT_PAIR, COT_ROWS, COT_COLS, X_PAIR, X_ROWS, X_COLS, ALONG_X, ALONG_Y, ALONG_Z, LAST_X, LAST_Y, LAST_Z, LAST_E, GATHER, AFF1, AFF2) = range(19)


def group_totals(tile):
    lane = lax.broadcasted_iota(jnp.int32, tile.shape, 1)
    for step in (1, 2, 4):
        other = jnp.where(
            (lane & step) == 0, pltpu.roll(tile, 128 - step, 1), pltpu.roll(tile, step, 1)
        )
        tile = tile + other
    return tile


def kernel(
    coarse_hbm, gain_hbm, bias_hbm, w_hbm, cot_hbm, dec, gw, aff,
    coarse, gain, bias, w, cot, fetch_sem, wc, st, sa, st1, st2, af, at, at1, at2,
    xraw, xf, xe, hc, acts, pad0, pad1, a_t,
    cpart, cedge, ce, ch, cf, s_buf,
    gx, gy, gz, rx, ry, rz, px, py, pz, qx, qy, qz, qe, ag_s, ag_r, d_buf, ssem, rsem,
):
    tm, h = lax.axis_index("tm"), lax.axis_index("height")
    core = lax.rem(tm, 2)
    t = tm // 2
    left, right = lax.rem(h + 7, 8), lax.rem(h + 1, 8)
    t_off = lax.rem(t + 7 + 2 * core, 8)
    pair = tm + 1 - 2 * core

    def others_h():
        for dz, dy in ((1, 2), (1, 1), (1, 3), (0, 2), (1, 0), (0, 1), (0, 3)):
            yield lax.rem(h // 4 + dz, 2) * 4 + lax.rem(h + dy, 4)

    def others_tm():
        for dz, dx in ((1, 2), (1, 1), (1, 3), (1, 0), (0, 2), (0, 1), (0, 3)):
            chip = lax.rem(t // 4 + dz, 2) * 4 + lax.rem(t + dx, 4)
            yield 2 * chip + core
            yield 2 * chip + 1 - core
        yield pair

    def send(src, dst, kind, to_tm, to_h):
        pltpu.make_async_remote_copy(
            src_ref=src, dst_ref=dst, send_sem=ssem.at[kind], recv_sem=rsem.at[kind],
            device_id=(to_tm, to_h), device_id_type=MESH,
        ).start()

    def arrived(kind, like):
        pltpu.make_async_copy(like, like, rsem.at[kind]).wait()

    def sent(kind, like):
        pltpu.make_async_copy(like, like, ssem.at[kind]).wait()

    pairs = ((coarse_hbm, coarse), (cot_hbm, cot), (gain_hbm, gain), (bias_hbm, bias), (w_hbm, w))
    fetches = [pltpu.make_async_copy(src, dst, fetch_sem.at[i]) for i, (src, dst) in enumerate(pairs)]
    for fetch in fetches:
        fetch.start()

    barrier = pltpu.get_barrier_semaphore()

    def greet(to_tm, to_h):
        pl.semaphore_signal(barrier, inc=1, device_id=(to_tm, to_h), device_id_type=MESH)

    for to_tm in others_tm():
        greet(to_tm, h)
    for to_h in others_h():
        greet(tm, to_h)

    greet(pair, left)
    greet(pair, right)

    @pl.loop(0, 4)
    def _(k):
        to_tm = lax.rem(t + 7 + 2 * (k // 2), 8) * 2 + lax.rem(k, 2)
        greet(to_tm, left)
        greet(to_tm, right)

    fetches[0].wait()
    x = coarse[...].astype(F32).reshape(256, 256)
    total = jnp.sum(x, axis=0, keepdims=True)
    squares = jnp.sum(x * x, axis=0, keepdims=True)
    quarters = (total[:, :128], total[:, 128:], squares[:, :128], squares[:, 128:])
    quarter = lax.rem(lax.broadcasted_iota(jnp.int32, (4, 128), 1), 4)
    mine = quarter == lax.broadcasted_iota(jnp.int32, (4, 128), 0)
    sums = group_totals(jnp.concatenate(quarters, axis=0))
    st[...] = jnp.sum(jnp.where(mine, sums, 0.0), axis=0, keepdims=True)

    pl.semaphore_wait(barrier, 32)

    for to_h in others_h():
        send(st, st1.at[h], STATS1, tm, to_h)

    for to_h in others_h():
        send(
            coarse.at[:, pl.ds(pl.multiple_of(to_h * 16, 16), 16), :],
            xraw.at[h, pl.ds(1 + 2 * core, 2)], BLOCKS, tm, to_h,
        )

    fetches[1].wait()
    send(cot, cpart, COT_PAIR, pair, h)
    for c2 in range(2):
        send(cot.at[:, pl.ds(3 * core, 1)], cedge.at[1 - core], COT_ROWS, t_off * 2 + c2, h)
    def cell(j, f):
        return pl.multiple_of((j * 8 + f) * 48, 8)

    for r in range(4):
        for f in range(8):
            cf[pl.ds(cell(1 + 4 * core + r, f) + 8, 32), :] = cot[f, r].astype(F32)
    for r in range(4):
        base = cell(1 + 4 * core + r, 0)
        ce[0, r] = cf[pl.ds(base + 8, 8, stride=48), :]
        ce[1, r] = cf[pl.ds(base + 39, 8, stride=48), :]

    for side, to_h in ((0, left), (1, right)):
        for c2 in range(2):
            send(ce.at[side], ch.at[1 - side, pl.ds(1 + 4 * core, 4)], COT_COLS, 2 * t + c2, to_h)
            send(ce.at[side, pl.ds(3 * core, 1)], ch.at[1 - side, pl.ds(9 - 9 * core, 1)], COT_COLS, t_off * 2 + c2, to_h)

    st1[h] = st[...]
    xraw[h, pl.ds(1 + 2 * core, 2)] = coarse[:, pl.ds(pl.multiple_of(h * 16, 16), 16), :]

    arrived(STATS1, st1.at[pl.ds(0, 7)])
    sa[...] = jnp.sum(st1[...], axis=0)

    for to_tm in others_tm():
        send(sa, st2.at[tm], STATS2, to_tm, h)

    st2[tm] = sa[...]

    arrived(BLOCKS, xraw.at[pl.ds(0, 7), pl.ds(0, 2)])
    own = xraw.at[:, pl.ds(1 + 2 * core, 2)]
    send(own, own, X_PAIR, pair, h)
    send(xraw.at[:, pl.ds(1 + 3 * core, 1)], xraw.at[:, pl.ds(5 - 5 * core, 1)], X_ROWS, t_off * 2 + 1 - core, h)

    s_buf[:, 8:10] = jnp.zeros((9, 2, 4, 16, 128), BF16)
    arrived(COT_PAIR, cpart)
    arrived(COT_ROWS, cedge)
    arrived(COT_COLS, ch)
    for r in range(4):
        for f in range(8):
            cf[pl.ds(cell(5 - 4 * core + r, f) + 8, 32), :] = cpart[f, r].astype(F32)
    top, bottom = t > 0, t < CHIPS - 1
    for f in range(8):
        cf[pl.ds(cell(0, f) + 8, 32), :] = jnp.where(top, cedge[0, f, 0].astype(F32), 0.0)
        cf[pl.ds(cell(9, f) + 8, 32), :] = jnp.where(bottom, cedge[1, f, 0].astype(F32), 0.0)
    for j in range(10):
        keep = (h > 0, h < HEIGHT - 1)
        if j == 0:
            keep = tuple(jnp.logical_and(k, top) for k in keep)
        if j == 9:
            keep = tuple(jnp.logical_and(k, bottom) for k in keep)
        cf[pl.ds(j * 384 + 7, 8, stride=48), :] = jnp.where(keep[0], ch[0, j], 0.0)
        cf[pl.ds(j * 384 + 40, 8, stride=48), :] = jnp.where(keep[1], ch[1, j], 0.0)

    @pl.loop(0, 8)
    def _(f):
        sums = []
        for j in range(10):
            base = cell(j, f)
            cols = [cf[pl.ds(base + 7 + i, 16, stride=2), :] for i in range(4)]
            sums.append((cols[2] + cols[3], cols[1] + cols[2], cols[0] + cols[1]))
        for b in range(3):
            for e in range(3):
                for row in range(4):
                    s_buf[b * 3 + e, f, row] = (sums[2 * row + 2 - b][e] + sums[2 * row + 3 - b][e]).astype(BF16)

    for r in range(2):
        rows = xraw[:, 1 + 2 * core + r].astype(F32).reshape(128, 256)
        for half in range(2):
            xf[half, 0:128, :] = rows[:, 128 * half : 128 * half + 128]
            for side, column in ((0, 0), (1, 15)):
                xe[side, r, :, 128 * half : 128 * half + 128] = xf.at[half][pl.ds(column, 8, stride=16), :]
    for side, to_h in ((0, left), (1, right)):
        send(xe.at[side], hc.at[1 - side, pl.ds(1 + 2 * core, 2)], X_COLS, tm, to_h)
        send(xe.at[side, pl.ds(1 - core, 1)], hc.at[1 - side, pl.ds(2 + core, 1)], X_COLS, pair, to_h)
        send(xe.at[side, pl.ds(core, 1)], hc.at[1 - side, pl.ds(5 - 5 * core, 1)], X_COLS, t_off * 2 + 1 - core, to_h)

    fetches[2].wait()
    fetches[3].wait()
    arrived(STATS2, st2.at[pl.ds(0, 15)])
    first_four = lax.rem(lax.broadcasted_iota(jnp.int32, (4, 128), 1), 8) < 4
    sums = jnp.broadcast_to(jnp.sum(st2[...], axis=0), (4, 128))
    stats = group_totals(jnp.where(jnp.logical_and(mine, first_four), sums, 0.0)) / NUMBERS
    mean = jnp.concatenate([stats[0:1], stats[1:2]], axis=1)
    square = jnp.concatenate([stats[2:3], stats[3:4]], axis=1)
    inverse = lax.rsqrt(square - mean * mean + EPSILON)
    scale, shift = inverse * gain[...], bias[...]

    def activate(v):
        shifted = (v - mean) * scale + shift
        return shifted * jax.nn.sigmoid(shifted)

    arrived(X_PAIR, xraw.at[:, pl.ds(0, 2)])
    for j in range(1, 5):
        act = activate(xraw[:, j].astype(F32).reshape(128, 256))
        acts[1, 2:10, j] = act.astype(BF16).reshape(8, 16, 256)

    turned = jnp.transpose(acts[1, 2:10, 1:5].reshape(512, 256))
    a_t[...] = turned.reshape(8, 2, 16, 512)

    zhi, x_at, zlo, y_at = t // 4, lax.rem(t, 4), h // 4, lax.rem(h, 4)
    z_at = 2 * zhi + zlo

    def products(first, count, keep):
        lhs = a_t[:, core].reshape(128, 512)
        for tap in range(first, first + count, 4):
            taps = range(tap, min(tap + 4, first + count))
            rhs = [s_buf[n % 9, 2 - n // 9 : 10 - n // 9].reshape(512, 128) for n in taps]
            rhs = jnp.concatenate(rhs, axis=1)
            out = jnp.dot(lhs, rhs, preferred_element_type=F32).astype(BF16)
            for i, n in enumerate(taps):
                keep(n - first, out[:, 128 * i : 128 * i + 128].reshape(8, 16, 128))

    def keep_x(n, tiles):
        for z in range(2):
            gx[:, 8 * z + n] = tiles[4 * z : 4 * z + 4]

    def keep_y(n, tiles):
        gy[n % 4, 8 * (n // 4) : 8 * (n // 4) + 8] = tiles

    def keep_z(n, tiles):
        for z in range(2):
            for x in range(4):
                gz[2 * z + n // 4, 4 * x + n % 4] = tiles[4 * z + x]

    def keep_extra(n, tiles):
        for to in range(4):
            if n == 0:
                first, second = to, to + 4
            elif n == 1:
                first, second = (to + 1) % 4, (to + 1) % 4 + 4
            else:
                first = 4 * (to // 2) + 2 * (to // 2 == to % 2)
                second = first + 1
            (gx, gy, gz)[n][to, 16] = tiles[first]
            (gx, gy, gz)[n][to, 17] = tiles[second]

    far = (2, 1, 3)
    products(24, 3, keep_extra)
    products(0, 8, keep_x)
    for k in far:
        to = lax.rem(x_at + k, 4)
        send(gx.at[to], rx.at[x_at], ALONG_X, (zhi * 4 + to) * 2 + core, h)
    products(8, 8, keep_y)
    for k in far:
        to = lax.rem(y_at + k, 4)
        send(gy.at[to], ry.at[y_at], ALONG_Y, tm, zlo * 4 + to)
    products(16, 8, keep_z)
    for k in far:
        to = lax.rem(z_at + k, 4)
        send(gz.at[to], rz.at[z_at], ALONG_Z, (to // 2 * 4 + x_at) * 2 + core, lax.rem(to, 2) * 4 + y_at)
    rx[x_at] = gx[x_at]
    ry[y_at] = gy[y_at]
    rz[z_at] = gz[z_at]
    fetches[4].wait()
    grad = jnp.zeros((256, 256), F32)
    for first in range(0, 27, 2):
        taps = range(first, min(first + 2, 27))
        lhs = [s_buf[n % 9, 2 - n // 9 : 10 - n // 9, pl.ds(2 * core, 2)].reshape(256, 128) for n in taps]
        rhs = [w[n] for n in taps]
        if len(lhs) == 2:
            lhs, rhs = [jnp.concatenate(lhs, axis=1)], [jnp.concatenate(rhs, axis=1)]
        grad = grad + lax.dot_general(lhs[0], rhs[0], (((1,), (1,)), ((), ())), preferred_element_type=F32)

    normed = (xraw[:, pl.ds(1 + 2 * core, 2)].astype(F32).reshape(256, 256) - mean) * inverse
    shifted = normed * gain[...] + shift
    sig = jax.nn.sigmoid(shifted)
    grad = grad * sig * (1.0 + shifted * (1.0 - sig))
    d_gain = jnp.sum(grad * normed, axis=0, keepdims=True)
    d_bias = jnp.sum(grad, axis=0, keepdims=True)
    af[...] = jnp.concatenate([d_gain[:, :128], d_gain[:, 128:], d_bias[:, :128], d_bias[:, 128:]], axis=0)

    for to_h in others_h():
        send(af, at1.at[h], AFF1, tm, to_h)

    at1[h] = af[...]


    @pl.loop(0, 48)
    def _(step):
        a = step // 16
        rows = pl.ds(pl.multiple_of(lax.rem(step, 16) * 16, 16), 16)
        taps = [[w[a * 9 + b * 3 + e, rows, :].astype(F32) for e in range(3)] for b in range(3)]
        for rc, bs in enumerate(((0,), (1, 2), (0, 1), (2,))):
            line = [taps[bs[0]][e] if len(bs) == 1 else taps[bs[0]][e] + taps[bs[1]][e] for e in range(3)]
            for cc, value in enumerate((line[0], line[1] + line[2], line[0] + line[1], line[2])):
                wc[a, rc, rows, 128 * cc : 128 * cc + 128] = value.astype(BF16)

    acts[:, 0:2] = jnp.zeros((3, 2, 6, 16, 256), BF16)
    arrived(X_ROWS, xraw.at[:, pl.ds(0, 1)])
    arrived(X_COLS, hc.at[:, pl.ds(0, 4)])
    border = 5 * core
    inside = jnp.where(core == 0, t > 0, t < CHIPS - 1)
    act = jnp.where(inside, activate(xraw[:, border].astype(F32).reshape(128, 256)), 0.0)
    acts[1, 2:10, border] = act.astype(BF16).reshape(8, 16, 256)
    pads = (pad0, pad1)

    @pl.loop(0, 4)
    def _(k):
        j = 2 * core + k
        here = jnp.logical_or(j != border, inside)
        act = acts[1, 2:10, j].astype(F32).reshape(128, 256)
        act_l = jnp.where(jnp.logical_and(here, h > 0), activate(hc[0, j]), 0.0)
        act_r = jnp.where(jnp.logical_and(here, h < HEIGHT - 1), activate(hc[1, j]), 0.0)
        for half in range(2):
            lanes = slice(128 * half, 128 * half + 128)
            pad = pads[half]
            for f in range(8):
                pad[32 * f + 8 : 32 * f + 24, :] = act[16 * f : 16 * f + 16, lanes]
            pad[pl.ds(7, 8, stride=32), :] = act_l[:, lanes]
            pad[pl.ds(24, 8, stride=32), :] = act_r[:, lanes]
            for f in range(8):
                acts[0, 2 + f, j, :, lanes] = pad[32 * f + 7 : 32 * f + 23, :].astype(BF16)
                acts[2, 2 + f, j, :, lanes] = pad[32 * f + 9 : 32 * f + 25, :].astype(BF16)

    def total_of(parts):
        return jnp.sum(parts[...].astype(F32), axis=0).astype(BF16)

    arrived(ALONG_X, rx.at[pl.ds(0, 3)])
    px[...] = total_of(rx)
    for dz in (1, 0):
        for k in (6, 2, 5, 7, 1, 3, 4, 0):
            if dz or k:
                to_z, to_h = lax.rem(zhi + dz, 2), lax.rem(h + k, 8)
                send(px.at[to_z * 8 + to_h], qx.at[zhi * 8 + h], LAST_X, (to_z * 4 + x_at) * 2 + core, to_h)
    arrived(ALONG_Y, ry.at[pl.ds(0, 3)])
    py[...] = total_of(ry)
    for dz in (1, 0):
        for k in (6, 2, 5, 7, 1, 3, 4, 0):
            if dz or k:
                to_z, to_t = lax.rem(zlo + dz, 2), lax.rem(t + k, 8)
                send(py.at[to_z * 8 + to_t], qy.at[zlo * 8 + t], LAST_Y, to_t * 2 + core, to_z * 4 + y_at)
    arrived(ALONG_Z, rz.at[pl.ds(0, 3)])
    pz[...] = total_of(rz)
    for dx in (2, 1, 3, 0):
        for dy in (2, 1, 3, 0):
            if dx or dy:
                to_x, to_y = lax.rem(x_at + dx, 4), lax.rem(y_at + dy, 4)
                send(pz.at[to_x * 4 + to_y], qz.at[x_at * 4 + y_at], LAST_Z, (zhi * 4 + to_x) * 2 + core, zlo * 4 + to_y)

    def extra(tile, at, to_t, to_h):
        here = jnp.logical_and(to_t == t, to_h == h)

        @pl.when(jnp.logical_not(here))
        def _():
            send(tile, qe.at[at], LAST_E, to_t * 2 + core, to_h)

        @pl.when(here)
        def _():
            qe[at] = tile[...]

    for i in range(2):
        to_t = 4 * i + x_at
        extra(px.at[16 + i], zhi * 8 + h, to_t, to_t)
        to_t = 4 * i + lax.rem(y_at + 1, 4)
        extra(py.at[16 + i], zlo * 8 + t, to_t, lax.rem(to_t + EXTRA[1], 8))
        to_t = 4 * zhi + jnp.where(zhi == zlo, 2, 0) + i
        extra(pz.at[16 + i], x_at * 4 + y_at, to_t, lax.rem(to_t + EXTRA[2], 8))
    qx[zhi * 8 + h] = px[zhi * 8 + h]
    qy[zlo * 8 + t] = py[zlo * 8 + t]
    qz[x_at * 4 + y_at] = pz[x_at * 4 + y_at]

    for p in range(2):
        even = jnp.zeros((256, 128), F32)
        odd = jnp.zeros((256, 128), F32)
        for rc, dr in ((0, -1), (1, 0)) if p == 0 else ((2, 0), (3, 1)):
            for a in range(3):
                lhs = [acts[dc, a : a + 8, pl.ds(2 * core + 1 + dr, 2)].reshape(256, 256) for dc in range(3)]
                both = jnp.dot(lhs[1], wc[a, rc, :, 128:384], preferred_element_type=F32)
                even = even + both[:, :128] + jnp.dot(lhs[0], wc[a, rc, :, 0:128], preferred_element_type=F32)
                odd = odd + both[:, 128:] + jnp.dot(lhs[2], wc[a, rc, :, 384:512], preferred_element_type=F32)
        for f in range(8):
            for row in range(2):
                at_row = (f * 4 + 2 * row + p) * 32
                here = (f * 2 + row) * 16
                d_buf[pl.ds(at_row, 16, stride=2), :] = even[here : here + 16]
                d_buf[pl.ds(at_row + 1, 16, stride=2), :] = odd[here : here + 16]
    dec[...] = d_buf[0:1024, :].astype(BF16).reshape(8, 4, 32, 128)

    arrived(AFF1, at1.at[pl.ds(0, 7)])
    at[...] = jnp.sum(at1[...], axis=0)

    for to_tm in others_tm():
        send(at, at2.at[tm], AFF2, to_tm, h)

    at2[tm] = at[...]

    owners = [lax.rem(t + shift_h, 8) for shift_h in EXTRA]
    has_extra = jnp.logical_or(h == owners[0], jnp.logical_or(h == owners[1], h == owners[2]))
    for i, (kind, parts) in enumerate(((LAST_X, qx), (LAST_Y, qy), (LAST_Z, qz))):
        arrived(kind, parts.at[pl.ds(0, 15)])
        ag_s[i] = total_of(parts)
        if i == 1:
            for to_h in others_h():
                send(ag_s.at[pl.ds(0, 2)], ag_r.at[h, pl.ds(0, 2)], GATHER, tm, to_h)

    @pl.when(has_extra)
    def _():
        arrived(LAST_E, qe.at[pl.ds(0, 15)])
        ag_s[3] = total_of(qe)

    @pl.when(jnp.logical_not(has_extra))
    def _():
        ag_s[3] = jnp.zeros((16, 128), BF16)

    for to_h in others_h():
        send(ag_s.at[pl.ds(2, 2)], ag_r.at[h, pl.ds(2, 2)], GATHER, tm, to_h)

    ag_r[h] = ag_s[...]

    arrived(AFF2, at2.at[pl.ds(0, 15)])
    total = jnp.sum(at2[...], axis=0)
    aff[0:1, 0:128] = total[0:1]
    aff[0:1, 128:256] = total[1:2]
    aff[1:2, 0:128] = total[2:3]
    aff[1:2, 128:256] = total[3:4]

    arrived(GATHER, ag_r.at[pl.ds(0, 7)])
    for k in range(8):
        for i in range(3):
            gw[8 * i + k] = ag_r[k, i].astype(F32)
    for i in range(3):
        gw[24 + i] = ag_r[owners[i], 3].astype(F32)

    sent(BLOCKS, xraw.at[pl.ds(0, 7), pl.ds(0, 2)])
    sent(COT_PAIR, cpart)
    sent(COT_ROWS, cedge)
    sent(COT_COLS, ch)
    sent(X_PAIR, xraw.at[:, pl.ds(0, 2)])
    sent(X_ROWS, xraw.at[:, pl.ds(0, 1)])
    sent(X_COLS, hc.at[:, pl.ds(0, 4)])
    for kind, parts in ((ALONG_X, rx), (ALONG_Y, ry), (ALONG_Z, rz)):
        sent(kind, parts.at[pl.ds(0, 3)])
    for kind, parts in ((LAST_X, qx), (LAST_Y, qy), (LAST_Z, qz)):
        sent(kind, parts.at[pl.ds(0, 15)])
    sent(LAST_E, qe.at[pl.ds(0, 5)])

    @pl.when(jnp.logical_not(has_extra))
    def _():
        sent(LAST_E, qe.at[0])

    sent(GATHER, ag_r.at[pl.ds(0, 7)])
    sent(STATS1, st1.at[pl.ds(0, 7)])
    sent(STATS2, st2.at[pl.ds(0, 15)])
    sent(AFF1, at1.at[pl.ds(0, 7)])
    sent(AFF2, at2.at[pl.ds(0, 15)])


def deliver(*refs):
    copies = [pltpu.make_async_copy(refs[i], refs[3 + i], refs[6].at[i]) for i in range(3)]
    for copy in copies:
        copy.start()
    for copy in copies:
        copy.wait()


def per_device(coarse, gain, bias, weight, cotangent):
    taps = jnp.transpose(weight, (1, 2, 3, 0, 4)).reshape(27, 256, 128)
    vmem = pl.BlockSpec(memory_space=pltpu.VMEM)
    vm = pltpu.VMEM
    decoded, grad_weight, grad_affine = pl.pallas_call(
        kernel,
        out_shape=(
            jax.ShapeDtypeStruct((8, 4, 32, 128), BF16),
            jax.ShapeDtypeStruct((27, 16, 128), F32),
            jax.ShapeDtypeStruct((2, 256), F32),
        ),
        in_specs=[pl.BlockSpec(memory_space=pltpu.HBM)] * 5,
        out_specs=(vmem, vmem, vmem),
        scratch_shapes=[
            vm((2, 128, 256), BF16),
            vm((1, 256), F32),
            vm((1, 256), F32),
            vm((27, 256, 128), BF16),
            vm((8, 4, 32, 128), BF16),
            pltpu.SemaphoreType.DMA((5,)),
            vm((3, 4, 256, 512), BF16),
            vm((1, 128), F32),
            vm((1, 128), F32),
            vm((8, 1, 128), F32),
            vm((16, 1, 128), F32),
            vm((4, 128), F32),
            vm((4, 128), F32),
            vm((8, 4, 128), F32),
            vm((16, 4, 128), F32),
            vm((8, 6, 16, 256), BF16),
            vm((2, 144, 128), F32),
            vm((2, 2, 8, 256), F32),
            vm((2, 6, 8, 256), F32),
            vm((3, 10, 6, 16, 256), BF16),
            vm((288, 128), F32),
            vm((288, 128), F32),
            vm((8, 2, 16, 512), BF16),
            vm((8, 4, 32, 128), BF16),
            vm((2, 8, 1, 32, 128), BF16),
            vm((2, 4, 8, 128), F32),
            vm((2, 10, 8, 128), F32),
            vm((10 * 8 * 48 + 64, 128), F32),
            vm((9, 10, 4, 16, 128), BF16),
            *[vm((4, 18, 16, 128), BF16)] * 6,
            *[vm((18, 16, 128), BF16)] * 3,
            *[vm((16, 16, 128), BF16)] * 4,
            vm((4, 16, 128), BF16),
            vm((8, 4, 16, 128), BF16),
            vm((1056, 128), F32),
            pltpu.SemaphoreType.DMA((19,)),
            pltpu.SemaphoreType.DMA((19,)),
        ],
        compiler_params=pltpu.CompilerParams(
            collective_id=0, has_side_effects=True, vmem_limit_bytes=48 * 2**20
        ),
        cost_estimate=pl.CostEstimate(flops=2 * 10**9, bytes_accessed=4 * 10**6, transcendentals=300000),
    )(*[
        pltpu.with_memory_space_constraint(x, pltpu.HBM)
        for x in (coarse.reshape(2, 128, 256), gain.reshape(1, 256), bias.reshape(1, 256), taps, cotangent)
    ])
    decoded, grad_weight, grad_affine = pl.pallas_call(
        deliver,
        out_shape=(
            jax.ShapeDtypeStruct((8, 4, 32, 128), BF16),
            jax.ShapeDtypeStruct((27, 16, 128), F32),
            jax.ShapeDtypeStruct((2, 256), F32),
        ),
        in_specs=[pl.BlockSpec(memory_space=pltpu.VMEM)] * 3,
        out_specs=[pl.BlockSpec(memory_space=pl.ANY)] * 3,
        scratch_shapes=[pltpu.SemaphoreType.DMA((3,))],
        compiler_params=pltpu.CompilerParams(vmem_limit_bytes=8 * 2**20),
    )(decoded, grad_weight, grad_affine)
    grad_weight = jnp.transpose(grad_weight.reshape(3, 3, 3, 16, 128), (3, 0, 1, 2, 4))
    return decoded, grad_weight, grad_affine


def solution(mesh):
    return jax.shard_map(
        per_device,
        mesh=mesh,
        in_specs=(P("height", "tm", None, None), P(), P(), P(), P(None, "tm", "height", None)),
        out_specs=(P(None, "tm", "height", None), P("tm", None, None, None, None), P()),
        check_vma=False,
    )
```

```python
import functools

import jax
import jax.numpy as jnp
from jax import lax
from jax.experimental import pallas as pl
from jax.experimental.pallas import tpu as pltpu
from jax.sharding import PartitionSpec as P

MESH = pl.DeviceIdType.MESH
F32, BF16 = jnp.float32, jnp.bfloat16
EPSILON = 1e-06
NUMBERS = 8 * 32 * 128 * 8
CHIPS, HEIGHT = 8, 8
EXTRA = (0, 3, 6)

(STATS1, STATS2, BLOCKS, COT_PAIR, COT_ROWS, COT_COLS, X_PAIR, X_ROWS, X_COLS, ALONG_X, ALONG_Y, ALONG_Z, LAST_X, LAST_Y, LAST_Z, LAST_E, GATHER, AFF1, AFF2, ROWS_ON, COLS_ON) = range(21)


def group_totals(tile):
    lane = lax.broadcasted_iota(jnp.int32, tile.shape, 1)
    for step in (1, 2, 4):
        other = jnp.where(
            (lane & step) == 0, pltpu.roll(tile, 128 - step, 1), pltpu.roll(tile, step, 1)
        )
        tile = tile + other
    return tile


def kernel(
    coarse_hbm, gain_hbm, bias_hbm, w_hbm, cot_hbm, dec, gw, aff,
    coarse, gain, bias, w, cot, fetch_sem, wc, st, sa, st1, st2, af, at, at1, at2,
    xraw, xf, xe, hc, acts, pad0, pad1, a_t,
    cpart, cedge, ce, ch, cf, s_buf,
    gx, gy, gz, rx, ry, rz, px, py, pz, qx, qy, qz, qe, ag_s, ag_r, d_buf, ssem, rsem,
):
    tm, h = lax.axis_index("tm"), lax.axis_index("height")
    core = lax.rem(tm, 2)
    t = tm // 2
    left, right = lax.rem(h + 7, 8), lax.rem(h + 1, 8)
    t_off = lax.rem(t + 7 + 2 * core, 8)
    pair = tm + 1 - 2 * core

    def others_h():
        for dz, dy in ((1, 2), (1, 1), (1, 3), (0, 2), (1, 0), (0, 1), (0, 3)):
            yield lax.rem(h // 4 + dz, 2) * 4 + lax.rem(h + dy, 4)

    def others_tm():
        for dz, dx in ((1, 2), (1, 1), (1, 3), (1, 0), (0, 2), (0, 1), (0, 3)):
            chip = lax.rem(t // 4 + dz, 2) * 4 + lax.rem(t + dx, 4)
            yield 2 * chip + core
            yield 2 * chip + 1 - core
        yield pair

    def send(src, dst, kind, to_tm, to_h):
        pltpu.make_async_remote_copy(
            src_ref=src, dst_ref=dst, send_sem=ssem.at[kind], recv_sem=rsem.at[kind],
            device_id=(to_tm, to_h), device_id_type=MESH,
        ).start()

    def arrived(kind, like):
        pltpu.make_async_copy(like, like, rsem.at[kind]).wait()

    def sent(kind, like):
        pltpu.make_async_copy(like, like, ssem.at[kind]).wait()

    pairs = ((coarse_hbm, coarse), (cot_hbm, cot), (gain_hbm, gain), (bias_hbm, bias), (w_hbm, w))
    fetches = [pltpu.make_async_copy(src, dst, fetch_sem.at[i]) for i, (src, dst) in enumerate(pairs)]
    for fetch in fetches:
        fetch.start()

    barrier = pltpu.get_barrier_semaphore()

    def greet(to_tm, to_h):
        pl.semaphore_signal(barrier, inc=1, device_id=(to_tm, to_h), device_id_type=MESH)

    for to_tm in others_tm():
        greet(to_tm, h)
    for to_h in others_h():
        greet(tm, to_h)

    greet(pair, left)
    greet(pair, right)

    @pl.loop(0, 4)
    def _(k):
        to_tm = lax.rem(t + 7 + 2 * (k // 2), 8) * 2 + lax.rem(k, 2)
        greet(to_tm, left)
        greet(to_tm, right)

    fetches[0].wait()
    x = coarse[...].astype(F32).reshape(256, 256)
    total = jnp.sum(x, axis=0, keepdims=True)
    squares = jnp.sum(x * x, axis=0, keepdims=True)
    quarters = (total[:, :128], total[:, 128:], squares[:, :128], squares[:, 128:])
    quarter = lax.rem(lax.broadcasted_iota(jnp.int32, (4, 128), 1), 4)
    mine = quarter == lax.broadcasted_iota(jnp.int32, (4, 128), 0)
    sums = group_totals(jnp.concatenate(quarters, axis=0))
    st[...] = jnp.sum(jnp.where(mine, sums, 0.0), axis=0, keepdims=True)

    pl.semaphore_wait(barrier, 32)

    for to_h in others_h():
        send(st, st1.at[h], STATS1, tm, to_h)

    for to_h in others_h():
        send(
            coarse.at[:, pl.ds(pl.multiple_of(to_h * 16, 16), 16), :],
            xraw.at[h, pl.ds(1 + 2 * core, 2)], BLOCKS, tm, to_h,
        )

    fetches[1].wait()
    send(cot, cpart, COT_PAIR, pair, h)
    send(cot.at[:, pl.ds(3 * core, 1)], cedge.at[1 - core], COT_ROWS, t_off * 2 + 1 - core, h)
    def cell(j, f):
        return pl.multiple_of((j * 8 + f) * 48, 8)

    for r in range(4):
        for f in range(8):
            cf[pl.ds(cell(1 + 4 * core + r, f) + 8, 32), :] = cot[f, r].astype(F32)
    for r in range(4):
        base = cell(1 + 4 * core + r, 0)
        ce[0, r] = cf[pl.ds(base + 8, 8, stride=48), :]
        ce[1, r] = cf[pl.ds(base + 39, 8, stride=48), :]

    for side, to_h in ((0, left), (1, right)):
        send(ce.at[side], ch.at[1 - side, pl.ds(1 + 4 * core, 4)], COT_COLS, tm, to_h)
        send(ce.at[side, pl.ds(3 * core, 1)], ch.at[1 - side, pl.ds(9 - 9 * core, 1)], COT_COLS, t_off * 2 + 1 - core, to_h)

    st1[h] = st[...]
    xraw[h, pl.ds(1 + 2 * core, 2)] = coarse[:, pl.ds(pl.multiple_of(h * 16, 16), 16), :]

    arrived(STATS1, st1.at[pl.ds(0, 7)])
    sa[...] = jnp.sum(st1[...], axis=0)

    for to_tm in others_tm():
        send(sa, st2.at[tm], STATS2, to_tm, h)

    st2[tm] = sa[...]

    arrived(BLOCKS, xraw.at[pl.ds(0, 7), pl.ds(0, 2)])
    own = xraw.at[:, pl.ds(1 + 2 * core, 2)]
    send(own, own, X_PAIR, pair, h)
    send(xraw.at[:, pl.ds(1 + 3 * core, 1)], xraw.at[:, pl.ds(5 - 5 * core, 1)], X_ROWS, t_off * 2 + 1 - core, h)

    s_buf[:, 8:10] = jnp.zeros((9, 2, 4, 16, 128), BF16)
    half_rows = ch.at[:, pl.ds(5 * core, 5)]
    arrived(COT_ROWS, cedge.at[0])
    send(cedge.at[core], cedge.at[core], ROWS_ON, pair, h)
    arrived(COT_COLS, ch.at[:, pl.ds(0, 5)])
    send(half_rows, half_rows, COLS_ON, pair, h)
    arrived(COT_PAIR, cpart)
    for r in range(4):
        for f in range(8):
            cf[pl.ds(cell(5 - 4 * core + r, f) + 8, 32), :] = cpart[f, r].astype(F32)
    arrived(ROWS_ON, cedge.at[0])
    arrived(COLS_ON, ch.at[:, pl.ds(0, 5)])
    top, bottom = t > 0, t < CHIPS - 1
    for f in range(8):
        cf[pl.ds(cell(0, f) + 8, 32), :] = jnp.where(top, cedge[0, f, 0].astype(F32), 0.0)
        cf[pl.ds(cell(9, f) + 8, 32), :] = jnp.where(bottom, cedge[1, f, 0].astype(F32), 0.0)
    for j in range(10):
        keep = (h > 0, h < HEIGHT - 1)
        if j == 0:
            keep = tuple(jnp.logical_and(k, top) for k in keep)
        if j == 9:
            keep = tuple(jnp.logical_and(k, bottom) for k in keep)
        cf[pl.ds(j * 384 + 7, 8, stride=48), :] = jnp.where(keep[0], ch[0, j], 0.0)
        cf[pl.ds(j * 384 + 40, 8, stride=48), :] = jnp.where(keep[1], ch[1, j], 0.0)

    @pl.loop(0, 8)
    def _(f):
        sums = []
        for j in range(10):
            base = cell(j, f)
            cols = [cf[pl.ds(base + 7 + i, 16, stride=2), :] for i in range(4)]
            sums.append((cols[2] + cols[3], cols[1] + cols[2], cols[0] + cols[1]))
        for b in range(3):
            for e in range(3):
                for row in range(4):
                    s_buf[b * 3 + e, f, row] = (sums[2 * row + 2 - b][e] + sums[2 * row + 3 - b][e]).astype(BF16)

    for r in range(2):
        rows = xraw[:, 1 + 2 * core + r].astype(F32).reshape(128, 256)
        for half in range(2):
            xf[half, 0:128, :] = rows[:, 128 * half : 128 * half + 128]
            for side, column in ((0, 0), (1, 15)):
                xe[side, r, :, 128 * half : 128 * half + 128] = xf.at[half][pl.ds(column, 8, stride=16), :]
    for side, to_h in ((0, left), (1, right)):
        send(xe.at[side], hc.at[1 - side, pl.ds(1 + 2 * core, 2)], X_COLS, tm, to_h)
        send(xe.at[side, pl.ds(1 - core, 1)], hc.at[1 - side, pl.ds(2 + core, 1)], X_COLS, pair, to_h)
        send(xe.at[side, pl.ds(core, 1)], hc.at[1 - side, pl.ds(5 - 5 * core, 1)], X_COLS, t_off * 2 + 1 - core, to_h)

    fetches[2].wait()
    fetches[3].wait()
    arrived(STATS2, st2.at[pl.ds(0, 15)])
    first_four = lax.rem(lax.broadcasted_iota(jnp.int32, (4, 128), 1), 8) < 4
    sums = jnp.broadcast_to(jnp.sum(st2[...], axis=0), (4, 128))
    stats = group_totals(jnp.where(jnp.logical_and(mine, first_four), sums, 0.0)) / NUMBERS
    mean = jnp.concatenate([stats[0:1], stats[1:2]], axis=1)
    square = jnp.concatenate([stats[2:3], stats[3:4]], axis=1)
    inverse = lax.rsqrt(square - mean * mean + EPSILON)
    scale, shift = inverse * gain[...], bias[...]

    def activate(v):
        shifted = (v - mean) * scale + shift
        return shifted * jax.nn.sigmoid(shifted)

    arrived(X_PAIR, xraw.at[:, pl.ds(0, 2)])
    for j in range(1, 5):
        act = activate(xraw[:, j].astype(F32).reshape(128, 256))
        acts[1, 2:10, j] = act.astype(BF16).reshape(8, 16, 256)

    turned = jnp.transpose(acts[1, 2:10, 1:5].reshape(512, 256))
    a_t[...] = turned.reshape(8, 2, 16, 512)

    zhi, x_at, zlo, y_at = t // 4, lax.rem(t, 4), h // 4, lax.rem(h, 4)
    z_at = 2 * zhi + zlo

    def products(first, count, keep):
        lhs = a_t[:, core].reshape(128, 512)
        for tap in range(first, first + count, 2):
            taps = range(tap, min(tap + 2, first + count))
            rhs = [s_buf[n % 9, 2 - n // 9 : 10 - n // 9].reshape(512, 128) for n in taps]
            rhs = jnp.concatenate(rhs, axis=1) if len(rhs) == 2 else rhs[0]
            out = jnp.dot(lhs, rhs, preferred_element_type=F32).astype(BF16)
            for i, n in enumerate(taps):
                keep(n - first, out[:, 128 * i : 128 * i + 128].reshape(8, 16, 128))

    def keep_x(n, tiles):
        for z in range(2):
            gx[:, 8 * z + n] = tiles[4 * z : 4 * z + 4]

    def keep_y(n, tiles):
        gy[n % 4, 8 * (n // 4) : 8 * (n // 4) + 8] = tiles

    def keep_z(n, tiles):
        for z in range(2):
            for x in range(4):
                gz[2 * z + n // 4, 4 * x + n % 4] = tiles[4 * z + x]

    def keep_extra(n, tiles):
        for to in range(4):
            if n == 0:
                first, second = to, to + 4
            elif n == 1:
                first, second = (to + 1) % 4, (to + 1) % 4 + 4
            else:
                first = 4 * (to // 2) + 2 * (to // 2 == to % 2)
                second = first + 1
            (gx, gy, gz)[n][to, 16] = tiles[first]
            (gx, gy, gz)[n][to, 17] = tiles[second]

    far = (2, 1, 3)
    products(24, 3, keep_extra)
    products(0, 8, keep_x)
    for k in far:
        to = lax.rem(x_at + k, 4)
        send(gx.at[to], rx.at[x_at], ALONG_X, (zhi * 4 + to) * 2 + core, h)
    products(8, 8, keep_y)
    for k in far:
        to = lax.rem(y_at + k, 4)
        send(gy.at[to], ry.at[y_at], ALONG_Y, tm, zlo * 4 + to)
    products(16, 8, keep_z)
    for k in far:
        to = lax.rem(z_at + k, 4)
        send(gz.at[to], rz.at[z_at], ALONG_Z, (to // 2 * 4 + x_at) * 2 + core, lax.rem(to, 2) * 4 + y_at)
    rx[x_at] = gx[x_at]
    ry[y_at] = gy[y_at]
    rz[z_at] = gz[z_at]
    fetches[4].wait()
    grad = jnp.zeros((256, 256), F32)
    for first in range(0, 27, 2):
        taps = range(first, min(first + 2, 27))
        lhs = [s_buf[n % 9, 2 - n // 9 : 10 - n // 9, pl.ds(2 * core, 2)].reshape(256, 128) for n in taps]
        rhs = [w[n] for n in taps]
        if len(lhs) == 2:
            lhs, rhs = [jnp.concatenate(lhs, axis=1)], [jnp.concatenate(rhs, axis=1)]
        grad = grad + lax.dot_general(lhs[0], rhs[0], (((1,), (1,)), ((), ())), preferred_element_type=F32)

    normed = (xraw[:, pl.ds(1 + 2 * core, 2)].astype(F32).reshape(256, 256) - mean) * inverse
    shifted = normed * gain[...] + shift
    sig = jax.nn.sigmoid(shifted)
    grad = grad * sig * (1.0 + shifted * (1.0 - sig))
    d_gain = jnp.sum(grad * normed, axis=0, keepdims=True)
    d_bias = jnp.sum(grad, axis=0, keepdims=True)
    af[...] = jnp.concatenate([d_gain[:, :128], d_gain[:, 128:], d_bias[:, :128], d_bias[:, 128:]], axis=0)

    for to_h in others_h():
        send(af, at1.at[h], AFF1, tm, to_h)

    at1[h] = af[...]


    @pl.loop(0, 48)
    def _(step):
        a = step // 16
        rows = pl.ds(pl.multiple_of(lax.rem(step, 16) * 16, 16), 16)
        taps = [[w[a * 9 + b * 3 + e, rows, :].astype(F32) for e in range(3)] for b in range(3)]
        for rc, bs in enumerate(((0,), (1, 2), (0, 1), (2,))):
            line = [taps[bs[0]][e] if len(bs) == 1 else taps[bs[0]][e] + taps[bs[1]][e] for e in range(3)]
            for cc, value in enumerate((line[0], line[1] + line[2], line[0] + line[1], line[2])):
                wc[a, rc, rows, 128 * cc : 128 * cc + 128] = value.astype(BF16)

    acts[:, 0:2] = jnp.zeros((3, 2, 6, 16, 256), BF16)
    arrived(X_ROWS, xraw.at[:, pl.ds(0, 1)])
    arrived(X_COLS, hc.at[:, pl.ds(0, 4)])
    border = 5 * core
    inside = jnp.where(core == 0, t > 0, t < CHIPS - 1)
    act = jnp.where(inside, activate(xraw[:, border].astype(F32).reshape(128, 256)), 0.0)
    acts[1, 2:10, border] = act.astype(BF16).reshape(8, 16, 256)
    pads = (pad0, pad1)

    @pl.loop(0, 4)
    def _(k):
        j = 2 * core + k
        here = jnp.logical_or(j != border, inside)
        act = acts[1, 2:10, j].astype(F32).reshape(128, 256)
        act_l = jnp.where(jnp.logical_and(here, h > 0), activate(hc[0, j]), 0.0)
        act_r = jnp.where(jnp.logical_and(here, h < HEIGHT - 1), activate(hc[1, j]), 0.0)
        for half in range(2):
            lanes = slice(128 * half, 128 * half + 128)
            pad = pads[half]
            for f in range(8):
                pad[32 * f + 8 : 32 * f + 24, :] = act[16 * f : 16 * f + 16, lanes]
            pad[pl.ds(7, 8, stride=32), :] = act_l[:, lanes]
            pad[pl.ds(24, 8, stride=32), :] = act_r[:, lanes]
            for f in range(8):
                acts[0, 2 + f, j, :, lanes] = pad[32 * f + 7 : 32 * f + 23, :].astype(BF16)
                acts[2, 2 + f, j, :, lanes] = pad[32 * f + 9 : 32 * f + 25, :].astype(BF16)

    def total_of(parts):
        return jnp.sum(parts[...].astype(F32), axis=0).astype(BF16)

    arrived(ALONG_X, rx.at[pl.ds(0, 3)])
    px[...] = total_of(rx)
    for dz in (1, 0):
        for k in (6, 2, 5, 7, 1, 3, 4, 0):
            if dz or k:
                to_z, to_h = lax.rem(zhi + dz, 2), lax.rem(h + k, 8)
                send(px.at[to_z * 8 + to_h], qx.at[zhi * 8 + h], LAST_X, (to_z * 4 + x_at) * 2 + core, to_h)
    arrived(ALONG_Y, ry.at[pl.ds(0, 3)])
    py[...] = total_of(ry)
    for dz in (1, 0):
        for k in (6, 2, 5, 7, 1, 3, 4, 0):
            if dz or k:
                to_z, to_t = lax.rem(zlo + dz, 2), lax.rem(t + k, 8)
                send(py.at[to_z * 8 + to_t], qy.at[zlo * 8 + t], LAST_Y, to_t * 2 + core, to_z * 4 + y_at)
    arrived(ALONG_Z, rz.at[pl.ds(0, 3)])
    pz[...] = total_of(rz)
    for dx in (2, 1, 3, 0):
        for dy in (2, 1, 3, 0):
            if dx or dy:
                to_x, to_y = lax.rem(x_at + dx, 4), lax.rem(y_at + dy, 4)
                send(pz.at[to_x * 4 + to_y], qz.at[x_at * 4 + y_at], LAST_Z, (zhi * 4 + to_x) * 2 + core, zlo * 4 + to_y)

    def extra(tile, at, to_t, to_h):
        here = jnp.logical_and(to_t == t, to_h == h)

        @pl.when(jnp.logical_not(here))
        def _():
            send(tile, qe.at[at], LAST_E, to_t * 2 + core, to_h)

        @pl.when(here)
        def _():
            qe[at] = tile[...]

    for i in range(2):
        to_t = 4 * i + x_at
        extra(px.at[16 + i], zhi * 8 + h, to_t, to_t)
        to_t = 4 * i + lax.rem(y_at + 1, 4)
        extra(py.at[16 + i], zlo * 8 + t, to_t, lax.rem(to_t + EXTRA[1], 8))
        to_t = 4 * zhi + jnp.where(zhi == zlo, 2, 0) + i
        extra(pz.at[16 + i], x_at * 4 + y_at, to_t, lax.rem(to_t + EXTRA[2], 8))
    qx[zhi * 8 + h] = px[zhi * 8 + h]
    qy[zlo * 8 + t] = py[zlo * 8 + t]
    qz[x_at * 4 + y_at] = pz[x_at * 4 + y_at]

    arrived(AFF1, at1.at[pl.ds(0, 7)])
    at[...] = jnp.sum(at1[...], axis=0)

    for to_tm in others_tm():
        send(at, at2.at[tm], AFF2, to_tm, h)

    at2[tm] = at[...]

    for p in range(2):
        even = jnp.zeros((256, 128), F32)
        odd = jnp.zeros((256, 128), F32)
        for rc, dr in ((0, -1), (1, 0)) if p == 0 else ((2, 0), (3, 1)):
            for a in range(3):
                lhs = [acts[dc, a : a + 8, pl.ds(2 * core + 1 + dr, 2)].reshape(256, 256) for dc in range(3)]
                both = jnp.dot(lhs[1], wc[a, rc, :, 128:384], preferred_element_type=F32)
                even = even + both[:, :128] + jnp.dot(lhs[0], wc[a, rc, :, 0:128], preferred_element_type=F32)
                odd = odd + both[:, 128:] + jnp.dot(lhs[2], wc[a, rc, :, 384:512], preferred_element_type=F32)
        for f in range(8):
            for row in range(2):
                at_row = (f * 4 + 2 * row + p) * 32
                here = (f * 2 + row) * 16
                d_buf[pl.ds(at_row, 16, stride=2), :] = even[here : here + 16]
                d_buf[pl.ds(at_row + 1, 16, stride=2), :] = odd[here : here + 16]
    dec[...] = d_buf[0:1024, :].astype(BF16).reshape(8, 4, 32, 128)

    owners = [lax.rem(t + shift_h, 8) for shift_h in EXTRA]
    has_extra = jnp.logical_or(h == owners[0], jnp.logical_or(h == owners[1], h == owners[2]))
    for i, (kind, parts) in enumerate(((LAST_X, qx), (LAST_Y, qy), (LAST_Z, qz))):
        arrived(kind, parts.at[pl.ds(0, 15)])
        ag_s[i] = total_of(parts)

    @pl.when(has_extra)
    def _():
        arrived(LAST_E, qe.at[pl.ds(0, 15)])
        ag_s[3] = total_of(qe)

    @pl.when(jnp.logical_not(has_extra))
    def _():
        ag_s[3] = jnp.zeros((16, 128), BF16)

    for to_h in others_h():
        send(ag_s, ag_r.at[h], GATHER, tm, to_h)

    ag_r[h] = ag_s[...]

    arrived(AFF2, at2.at[pl.ds(0, 15)])
    total = jnp.sum(at2[...], axis=0)
    aff[0:1, 0:128] = total[0:1]
    aff[0:1, 128:256] = total[1:2]
    aff[1:2, 0:128] = total[2:3]
    aff[1:2, 128:256] = total[3:4]

    arrived(GATHER, ag_r.at[pl.ds(0, 7)])
    for k in range(8):
        for i in range(3):
            gw[8 * i + k] = ag_r[k, i].astype(F32)
    for i in range(3):
        gw[24 + i] = ag_r[owners[i], 3].astype(F32)

    sent(BLOCKS, xraw.at[pl.ds(0, 7), pl.ds(0, 2)])
    sent(COT_PAIR, cpart)
    sent(COT_ROWS, cedge.at[0])
    sent(COT_COLS, ch.at[:, pl.ds(0, 5)])
    sent(ROWS_ON, cedge.at[0])
    sent(COLS_ON, ch.at[:, pl.ds(0, 5)])
    sent(X_PAIR, xraw.at[:, pl.ds(0, 2)])
    sent(X_ROWS, xraw.at[:, pl.ds(0, 1)])
    sent(X_COLS, hc.at[:, pl.ds(0, 4)])
    for kind, parts in ((ALONG_X, rx), (ALONG_Y, ry), (ALONG_Z, rz)):
        sent(kind, parts.at[pl.ds(0, 3)])
    for kind, parts in ((LAST_X, qx), (LAST_Y, qy), (LAST_Z, qz)):
        sent(kind, parts.at[pl.ds(0, 15)])
    sent(LAST_E, qe.at[pl.ds(0, 5)])

    @pl.when(jnp.logical_not(has_extra))
    def _():
        sent(LAST_E, qe.at[0])

    sent(GATHER, ag_r.at[pl.ds(0, 7)])
    sent(STATS1, st1.at[pl.ds(0, 7)])
    sent(STATS2, st2.at[pl.ds(0, 15)])
    sent(AFF1, at1.at[pl.ds(0, 7)])
    sent(AFF2, at2.at[pl.ds(0, 15)])


def deliver(*refs):
    copies = [pltpu.make_async_copy(refs[i], refs[3 + i], refs[6].at[i]) for i in range(3)]
    for copy in copies:
        copy.start()
    for copy in copies:
        copy.wait()


def per_device(coarse, gain, bias, weight, cotangent):
    taps = jnp.transpose(weight, (1, 2, 3, 0, 4)).reshape(27, 256, 128)
    vmem = pl.BlockSpec(memory_space=pltpu.VMEM)
    vm = pltpu.VMEM
    decoded, grad_weight, grad_affine = pl.pallas_call(
        kernel,
        out_shape=(
            jax.ShapeDtypeStruct((8, 4, 32, 128), BF16),
            jax.ShapeDtypeStruct((27, 16, 128), F32),
            jax.ShapeDtypeStruct((2, 256), F32),
        ),
        in_specs=[pl.BlockSpec(memory_space=pltpu.HBM)] * 5,
        out_specs=(vmem, vmem, vmem),
        scratch_shapes=[
            vm((2, 128, 256), BF16),
            vm((1, 256), F32),
            vm((1, 256), F32),
            vm((27, 256, 128), BF16),
            vm((8, 4, 32, 128), BF16),
            pltpu.SemaphoreType.DMA((5,)),
            vm((3, 4, 256, 512), BF16),
            vm((1, 128), F32),
            vm((1, 128), F32),
            vm((8, 1, 128), F32),
            vm((16, 1, 128), F32),
            vm((4, 128), F32),
            vm((4, 128), F32),
            vm((8, 4, 128), F32),
            vm((16, 4, 128), F32),
            vm((8, 6, 16, 256), BF16),
            vm((2, 144, 128), F32),
            vm((2, 2, 8, 256), F32),
            vm((2, 6, 8, 256), F32),
            vm((3, 10, 6, 16, 256), BF16),
            vm((288, 128), F32),
            vm((288, 128), F32),
            vm((8, 2, 16, 512), BF16),
            vm((8, 4, 32, 128), BF16),
            vm((2, 8, 1, 32, 128), BF16),
            vm((2, 4, 8, 128), F32),
            vm((2, 10, 8, 128), F32),
            vm((10 * 8 * 48 + 64, 128), F32),
            vm((9, 10, 4, 16, 128), BF16),
            *[vm((4, 18, 16, 128), BF16)] * 6,
            *[vm((18, 16, 128), BF16)] * 3,
            *[vm((16, 16, 128), BF16)] * 4,
            vm((4, 16, 128), BF16),
            vm((8, 4, 16, 128), BF16),
            vm((1056, 128), F32),
            pltpu.SemaphoreType.DMA((21,)),
            pltpu.SemaphoreType.DMA((21,)),
        ],
        compiler_params=pltpu.CompilerParams(
            collective_id=0, has_side_effects=True, vmem_limit_bytes=48 * 2**20
        ),
        cost_estimate=pl.CostEstimate(flops=2 * 10**9, bytes_accessed=4 * 10**6, transcendentals=300000),
    )(*[
        pltpu.with_memory_space_constraint(x, pltpu.HBM)
        for x in (coarse.reshape(2, 128, 256), gain.reshape(1, 256), bias.reshape(1, 256), taps, cotangent)
    ])
    decoded, grad_weight, grad_affine = pl.pallas_call(
        deliver,
        out_shape=(
            jax.ShapeDtypeStruct((8, 4, 32, 128), BF16),
            jax.ShapeDtypeStruct((27, 16, 128), F32),
            jax.ShapeDtypeStruct((2, 256), F32),
        ),
        in_specs=[pl.BlockSpec(memory_space=pltpu.VMEM)] * 3,
        out_specs=[pl.BlockSpec(memory_space=pl.ANY)] * 3,
        scratch_shapes=[pltpu.SemaphoreType.DMA((3,))],
        compiler_params=pltpu.CompilerParams(vmem_limit_bytes=8 * 2**20),
    )(decoded, grad_weight, grad_affine)
    grad_weight = jnp.transpose(grad_weight.reshape(3, 3, 3, 16, 128), (3, 0, 1, 2, 4))
    return decoded, grad_weight, grad_affine


def solution(mesh):
    return jax.shard_map(
        per_device,
        mesh=mesh,
        in_specs=(P("height", "tm", None, None), P(), P(), P(), P(None, "tm", "height", None)),
        out_specs=(P(None, "tm", "height", None), P("tm", None, None, None, None), P()),
        check_vma=False,
    )
```

```python
import functools

import jax
import jax.numpy as jnp
from jax import lax
from jax.experimental import pallas as pl
from jax.experimental.pallas import tpu as pltpu
from jax.sharding import PartitionSpec as P

MESH = pl.DeviceIdType.MESH
F32, BF16 = jnp.float32, jnp.bfloat16
EPSILON = 1e-06
NUMBERS = 8 * 32 * 128 * 8
CHIPS, HEIGHT = 8, 8
EXTRA = (0, 3, 6)

(STATS1, STATS2, BLOCKS, COT_PAIR, COT_ROWS, COT_COLS, X_PAIR, X_ROWS, X_COLS, ALONG_X, ALONG_Y, ALONG_Z, LAST_X, LAST_Y, LAST_Z, LAST_E, GATHER, AFF1, AFF2, ROWS_ON, COLS_ON, X_COLS_ON) = range(22)


def group_totals(tile):
    lane = lax.broadcasted_iota(jnp.int32, tile.shape, 1)
    for step in (1, 2, 4):
        other = jnp.where(
            (lane & step) == 0, pltpu.roll(tile, 128 - step, 1), pltpu.roll(tile, step, 1)
        )
        tile = tile + other
    return tile


def kernel(
    coarse_hbm, gain_hbm, bias_hbm, w_hbm, cot_hbm, dec, gw, aff,
    coarse, gain, bias, w, cot, fetch_sem, wc, st, sa, st1, st2, af, at, at1, at2,
    xraw, xf, xe, hc, acts, pad0, pad1, a_t,
    cpart, cedge, ce, ch, cf, s_buf,
    gx, gy, gz, rx, ry, rz, px, py, pz, qx, qy, qz, qe, ag_s, ag_r, d_buf, ssem, rsem,
):
    tm, h = lax.axis_index("tm"), lax.axis_index("height")
    core = lax.rem(tm, 2)
    t = tm // 2
    left, right = lax.rem(h + 7, 8), lax.rem(h + 1, 8)
    t_off = lax.rem(t + 7 + 2 * core, 8)
    pair = tm + 1 - 2 * core

    def others_h():
        for dz, dy in ((1, 2), (1, 1), (1, 3), (0, 2), (1, 0), (0, 1), (0, 3)):
            yield lax.rem(h // 4 + dz, 2) * 4 + lax.rem(h + dy, 4)

    def others_tm():
        for dz, dx in ((1, 2), (1, 1), (1, 3), (1, 0), (0, 2), (0, 1), (0, 3)):
            chip = lax.rem(t // 4 + dz, 2) * 4 + lax.rem(t + dx, 4)
            yield 2 * chip + core
            yield 2 * chip + 1 - core
        yield pair

    def send(src, dst, kind, to_tm, to_h):
        pltpu.make_async_remote_copy(
            src_ref=src, dst_ref=dst, send_sem=ssem.at[kind], recv_sem=rsem.at[kind],
            device_id=(to_tm, to_h), device_id_type=MESH,
        ).start()

    def arrived(kind, like):
        pltpu.make_async_copy(like, like, rsem.at[kind]).wait()

    def sent(kind, like):
        pltpu.make_async_copy(like, like, ssem.at[kind]).wait()

    pairs = ((coarse_hbm, coarse), (cot_hbm, cot), (gain_hbm, gain), (bias_hbm, bias), (w_hbm, w))
    fetches = [pltpu.make_async_copy(src, dst, fetch_sem.at[i]) for i, (src, dst) in enumerate(pairs)]
    for fetch in fetches:
        fetch.start()

    barrier = pltpu.get_barrier_semaphore()

    def greet(to_tm, to_h):
        pl.semaphore_signal(barrier, inc=1, device_id=(to_tm, to_h), device_id_type=MESH)

    for to_tm in others_tm():
        greet(to_tm, h)
    for to_h in others_h():
        greet(tm, to_h)

    for to_h in (left, right):
        greet(t_off * 2 + 1 - core, to_h)

    fetches[0].wait()
    x = coarse[...].astype(F32).reshape(256, 256)
    total = jnp.sum(x, axis=0, keepdims=True)
    squares = jnp.sum(x * x, axis=0, keepdims=True)
    quarters = (total[:, :128], total[:, 128:], squares[:, :128], squares[:, 128:])
    quarter = lax.rem(lax.broadcasted_iota(jnp.int32, (4, 128), 1), 4)
    mine = quarter == lax.broadcasted_iota(jnp.int32, (4, 128), 0)
    sums = group_totals(jnp.concatenate(quarters, axis=0))
    st[...] = jnp.sum(jnp.where(mine, sums, 0.0), axis=0, keepdims=True)

    pl.semaphore_wait(barrier, 24)

    for to_h in others_h():
        send(st, st1.at[h], STATS1, tm, to_h)

    for to_h in others_h():
        send(
            coarse.at[:, pl.ds(pl.multiple_of(to_h * 16, 16), 16), :],
            xraw.at[h, pl.ds(1 + 2 * core, 2)], BLOCKS, tm, to_h,
        )

    fetches[1].wait()
    send(cot, cpart, COT_PAIR, pair, h)
    send(cot.at[:, pl.ds(3 * core, 1)], cedge.at[1 - core], COT_ROWS, t_off * 2 + 1 - core, h)
    def cell(j, f):
        return pl.multiple_of((j * 8 + f) * 48, 8)

    for r in range(4):
        for f in range(8):
            cf[pl.ds(cell(1 + 4 * core + r, f) + 8, 32), :] = cot[f, r].astype(F32)
    for r in range(4):
        base = cell(1 + 4 * core + r, 0)
        ce[0, r] = cf[pl.ds(base + 8, 8, stride=48), :]
        ce[1, r] = cf[pl.ds(base + 39, 8, stride=48), :]

    for side, to_h in ((0, left), (1, right)):
        send(ce.at[side], ch.at[1 - side, pl.ds(1 + 4 * core, 4)], COT_COLS, tm, to_h)
        send(ce.at[side, pl.ds(3 * core, 1)], ch.at[1 - side, pl.ds(9 - 9 * core, 1)], COT_COLS, t_off * 2 + 1 - core, to_h)

    st1[h] = st[...]
    xraw[h, pl.ds(1 + 2 * core, 2)] = coarse[:, pl.ds(pl.multiple_of(h * 16, 16), 16), :]

    arrived(STATS1, st1.at[pl.ds(0, 7)])
    sa[...] = jnp.sum(st1[...], axis=0)

    for to_tm in others_tm():
        send(sa, st2.at[tm], STATS2, to_tm, h)

    st2[tm] = sa[...]

    arrived(BLOCKS, xraw.at[pl.ds(0, 7), pl.ds(0, 2)])
    own = xraw.at[:, pl.ds(1 + 2 * core, 2)]
    send(own, own, X_PAIR, pair, h)
    send(xraw.at[:, pl.ds(1 + 3 * core, 1)], xraw.at[:, pl.ds(5 - 5 * core, 1)], X_ROWS, t_off * 2 + 1 - core, h)

    s_buf[:, 8:10] = jnp.zeros((9, 2, 4, 16, 128), BF16)
    half_rows = ch.at[:, pl.ds(5 * core, 5)]
    arrived(COT_ROWS, cedge.at[0])
    send(cedge.at[core], cedge.at[core], ROWS_ON, pair, h)
    arrived(COT_COLS, ch.at[:, pl.ds(0, 5)])
    send(half_rows, half_rows, COLS_ON, pair, h)
    arrived(COT_PAIR, cpart)
    for r in range(4):
        for f in range(8):
            cf[pl.ds(cell(5 - 4 * core + r, f) + 8, 32), :] = cpart[f, r].astype(F32)
    arrived(ROWS_ON, cedge.at[0])
    arrived(COLS_ON, ch.at[:, pl.ds(0, 5)])
    top, bottom = t > 0, t < CHIPS - 1
    for f in range(8):
        cf[pl.ds(cell(0, f) + 8, 32), :] = jnp.where(top, cedge[0, f, 0].astype(F32), 0.0)
        cf[pl.ds(cell(9, f) + 8, 32), :] = jnp.where(bottom, cedge[1, f, 0].astype(F32), 0.0)
    for j in range(10):
        keep = (h > 0, h < HEIGHT - 1)
        if j == 0:
            keep = tuple(jnp.logical_and(k, top) for k in keep)
        if j == 9:
            keep = tuple(jnp.logical_and(k, bottom) for k in keep)
        cf[pl.ds(j * 384 + 7, 8, stride=48), :] = jnp.where(keep[0], ch[0, j], 0.0)
        cf[pl.ds(j * 384 + 40, 8, stride=48), :] = jnp.where(keep[1], ch[1, j], 0.0)

    @pl.loop(0, 8)
    def _(f):
        sums = []
        for j in range(10):
            base = cell(j, f)
            cols = [cf[pl.ds(base + 7 + i, 16, stride=2), :] for i in range(4)]
            sums.append((cols[2] + cols[3], cols[1] + cols[2], cols[0] + cols[1]))
        for b in range(3):
            for e in range(3):
                for row in range(4):
                    s_buf[b * 3 + e, f, row] = (sums[2 * row + 2 - b][e] + sums[2 * row + 3 - b][e]).astype(BF16)

    for r in range(2):
        rows = xraw[:, 1 + 2 * core + r].astype(F32).reshape(128, 256)
        for half in range(2):
            xf[half, 0:128, :] = rows[:, 128 * half : 128 * half + 128]
            for side, column in ((0, 0), (1, 15)):
                xe[side, r, :, 128 * half : 128 * half + 128] = xf.at[half][pl.ds(column, 8, stride=16), :]
    for side, to_h in ((0, left), (1, right)):
        send(xe.at[side], hc.at[1 - side, pl.ds(1 + 2 * core, 2)], X_COLS, tm, to_h)
        send(xe.at[side, pl.ds(core, 1)], hc.at[1 - side, pl.ds(5 - 5 * core, 1)], X_COLS, t_off * 2 + 1 - core, to_h)

    fetches[2].wait()
    fetches[3].wait()
    arrived(STATS2, st2.at[pl.ds(0, 15)])
    first_four = lax.rem(lax.broadcasted_iota(jnp.int32, (4, 128), 1), 8) < 4
    sums = jnp.broadcast_to(jnp.sum(st2[...], axis=0), (4, 128))
    stats = group_totals(jnp.where(jnp.logical_and(mine, first_four), sums, 0.0)) / NUMBERS
    mean = jnp.concatenate([stats[0:1], stats[1:2]], axis=1)
    square = jnp.concatenate([stats[2:3], stats[3:4]], axis=1)
    inverse = lax.rsqrt(square - mean * mean + EPSILON)
    scale, shift = inverse * gain[...], bias[...]

    def activate(v):
        shifted = (v - mean) * scale + shift
        return shifted * jax.nn.sigmoid(shifted)

    arrived(X_PAIR, xraw.at[:, pl.ds(0, 2)])
    for j in range(1, 5):
        act = activate(xraw[:, j].astype(F32).reshape(128, 256))
        acts[1, 2:10, j] = act.astype(BF16).reshape(8, 16, 256)

    turned = jnp.transpose(acts[1, 2:10, 1:5].reshape(512, 256))
    a_t[...] = turned.reshape(8, 2, 16, 512)

    zhi, x_at, zlo, y_at = t // 4, lax.rem(t, 4), h // 4, lax.rem(h, 4)
    z_at = 2 * zhi + zlo

    def products(first, count, keep):
        lhs = a_t[:, core].reshape(128, 512)
        for tap in range(first, first + count, 2):
            taps = range(tap, min(tap + 2, first + count))
            rhs = [s_buf[n % 9, 2 - n // 9 : 10 - n // 9].reshape(512, 128) for n in taps]
            rhs = jnp.concatenate(rhs, axis=1) if len(rhs) == 2 else rhs[0]
            out = jnp.dot(lhs, rhs, preferred_element_type=F32).astype(BF16)
            for i, n in enumerate(taps):
                keep(n - first, out[:, 128 * i : 128 * i + 128].reshape(8, 16, 128))

    def keep_x(n, tiles):
        for z in range(2):
            gx[:, 8 * z + n] = tiles[4 * z : 4 * z + 4]

    def keep_y(n, tiles):
        gy[n % 4, 8 * (n // 4) : 8 * (n // 4) + 8] = tiles

    def keep_z(n, tiles):
        for z in range(2):
            for x in range(4):
                gz[2 * z + n // 4, 4 * x + n % 4] = tiles[4 * z + x]

    def keep_extra(n, tiles):
        for to in range(4):
            if n == 0:
                first, second = to, to + 4
            elif n == 1:
                first, second = (to + 1) % 4, (to + 1) % 4 + 4
            else:
                first = 4 * (to // 2) + 2 * (to // 2 == to % 2)
                second = first + 1
            (gx, gy, gz)[n][to, 16] = tiles[first]
            (gx, gy, gz)[n][to, 17] = tiles[second]

    far = (2, 1, 3)
    products(24, 3, keep_extra)
    products(0, 8, keep_x)
    for k in far:
        to = lax.rem(x_at + k, 4)
        send(gx.at[to], rx.at[x_at], ALONG_X, (zhi * 4 + to) * 2 + core, h)
    products(8, 8, keep_y)
    for k in far:
        to = lax.rem(y_at + k, 4)
        send(gy.at[to], ry.at[y_at], ALONG_Y, tm, zlo * 4 + to)
    products(16, 8, keep_z)
    for k in far:
        to = lax.rem(z_at + k, 4)
        send(gz.at[to], rz.at[z_at], ALONG_Z, (to // 2 * 4 + x_at) * 2 + core, lax.rem(to, 2) * 4 + y_at)
    rx[x_at] = gx[x_at]
    ry[y_at] = gy[y_at]
    rz[z_at] = gz[z_at]
    fetches[4].wait()
    grad = jnp.zeros((256, 256), F32)
    for first in range(0, 27, 2):
        taps = range(first, min(first + 2, 27))
        lhs = [s_buf[n % 9, 2 - n // 9 : 10 - n // 9, pl.ds(2 * core, 2)].reshape(256, 128) for n in taps]
        rhs = [w[n] for n in taps]
        if len(lhs) == 2:
            lhs, rhs = [jnp.concatenate(lhs, axis=1)], [jnp.concatenate(rhs, axis=1)]
        grad = grad + lax.dot_general(lhs[0], rhs[0], (((1,), (1,)), ((), ())), preferred_element_type=F32)

    normed = (xraw[:, pl.ds(1 + 2 * core, 2)].astype(F32).reshape(256, 256) - mean) * inverse
    shifted = normed * gain[...] + shift
    sig = jax.nn.sigmoid(shifted)
    grad = grad * sig * (1.0 + shifted * (1.0 - sig))
    d_gain = jnp.sum(grad * normed, axis=0, keepdims=True)
    d_bias = jnp.sum(grad, axis=0, keepdims=True)
    af[...] = jnp.concatenate([d_gain[:, :128], d_gain[:, 128:], d_bias[:, :128], d_bias[:, 128:]], axis=0)

    for to_h in others_h():
        send(af, at1.at[h], AFF1, tm, to_h)

    at1[h] = af[...]

    arrived(X_COLS, hc.at[:, pl.ds(0, 3)])
    next_to_pair = hc.at[:, pl.ds(2 + core, 1)]
    send(next_to_pair, next_to_pair, X_COLS_ON, pair, h)


    @pl.loop(0, 48)
    def _(step):
        a = step // 16
        rows = pl.ds(pl.multiple_of(lax.rem(step, 16) * 16, 16), 16)
        taps = [[w[a * 9 + b * 3 + e, rows, :].astype(F32) for e in range(3)] for b in range(3)]
        for rc, bs in enumerate(((0,), (1, 2), (0, 1), (2,))):
            line = [taps[bs[0]][e] if len(bs) == 1 else taps[bs[0]][e] + taps[bs[1]][e] for e in range(3)]
            for cc, value in enumerate((line[0], line[1] + line[2], line[0] + line[1], line[2])):
                wc[a, rc, rows, 128 * cc : 128 * cc + 128] = value.astype(BF16)

    acts[:, 0:2] = jnp.zeros((3, 2, 6, 16, 256), BF16)
    arrived(X_ROWS, xraw.at[:, pl.ds(0, 1)])
    arrived(X_COLS_ON, hc.at[:, pl.ds(0, 1)])
    border = 5 * core
    inside = jnp.where(core == 0, t > 0, t < CHIPS - 1)
    act = jnp.where(inside, activate(xraw[:, border].astype(F32).reshape(128, 256)), 0.0)
    acts[1, 2:10, border] = act.astype(BF16).reshape(8, 16, 256)
    pads = (pad0, pad1)

    @pl.loop(0, 4)
    def _(k):
        j = 2 * core + k
        here = jnp.logical_or(j != border, inside)
        act = acts[1, 2:10, j].astype(F32).reshape(128, 256)
        act_l = jnp.where(jnp.logical_and(here, h > 0), activate(hc[0, j]), 0.0)
        act_r = jnp.where(jnp.logical_and(here, h < HEIGHT - 1), activate(hc[1, j]), 0.0)
        for half in range(2):
            lanes = slice(128 * half, 128 * half + 128)
            pad = pads[half]
            for f in range(8):
                pad[32 * f + 8 : 32 * f + 24, :] = act[16 * f : 16 * f + 16, lanes]
            pad[pl.ds(7, 8, stride=32), :] = act_l[:, lanes]
            pad[pl.ds(24, 8, stride=32), :] = act_r[:, lanes]
            for f in range(8):
                acts[0, 2 + f, j, :, lanes] = pad[32 * f + 7 : 32 * f + 23, :].astype(BF16)
                acts[2, 2 + f, j, :, lanes] = pad[32 * f + 9 : 32 * f + 25, :].astype(BF16)

    def total_of(parts):
        return jnp.sum(parts[...].astype(F32), axis=0).astype(BF16)

    arrived(ALONG_X, rx.at[pl.ds(0, 3)])
    px[...] = total_of(rx)
    for dz in (1, 0):
        for k in (6, 2, 5, 7, 1, 3, 4, 0):
            if dz or k:
                to_z, to_h = lax.rem(zhi + dz, 2), lax.rem(h + k, 8)
                send(px.at[to_z * 8 + to_h], qx.at[zhi * 8 + h], LAST_X, (to_z * 4 + x_at) * 2 + core, to_h)
    arrived(ALONG_Y, ry.at[pl.ds(0, 3)])
    py[...] = total_of(ry)
    for dz in (1, 0):
        for k in (6, 2, 5, 7, 1, 3, 4, 0):
            if dz or k:
                to_z, to_t = lax.rem(zlo + dz, 2), lax.rem(t + k, 8)
                send(py.at[to_z * 8 + to_t], qy.at[zlo * 8 + t], LAST_Y, to_t * 2 + core, to_z * 4 + y_at)
    arrived(ALONG_Z, rz.at[pl.ds(0, 3)])
    pz[...] = total_of(rz)
    for dx in (2, 1, 3, 0):
        for dy in (2, 1, 3, 0):
            if dx or dy:
                to_x, to_y = lax.rem(x_at + dx, 4), lax.rem(y_at + dy, 4)
                send(pz.at[to_x * 4 + to_y], qz.at[x_at * 4 + y_at], LAST_Z, (zhi * 4 + to_x) * 2 + core, zlo * 4 + to_y)

    def extra(tile, at, to_t, to_h):
        here = jnp.logical_and(to_t == t, to_h == h)

        @pl.when(jnp.logical_not(here))
        def _():
            send(tile, qe.at[at], LAST_E, to_t * 2 + core, to_h)

        @pl.when(here)
        def _():
            qe[at] = tile[...]

    for i in range(2):
        to_t = 4 * i + x_at
        extra(px.at[16 + i], zhi * 8 + h, to_t, to_t)
        to_t = 4 * i + lax.rem(y_at + 1, 4)
        extra(py.at[16 + i], zlo * 8 + t, to_t, lax.rem(to_t + EXTRA[1], 8))
        to_t = 4 * zhi + jnp.where(zhi == zlo, 2, 0) + i
        extra(pz.at[16 + i], x_at * 4 + y_at, to_t, lax.rem(to_t + EXTRA[2], 8))
    qx[zhi * 8 + h] = px[zhi * 8 + h]
    qy[zlo * 8 + t] = py[zlo * 8 + t]
    qz[x_at * 4 + y_at] = pz[x_at * 4 + y_at]

    arrived(AFF1, at1.at[pl.ds(0, 7)])
    at[...] = jnp.sum(at1[...], axis=0)

    for to_tm in others_tm():
        send(at, at2.at[tm], AFF2, to_tm, h)

    at2[tm] = at[...]

    for p in range(2):
        even = jnp.zeros((256, 128), F32)
        odd = jnp.zeros((256, 128), F32)
        for rc, dr in ((0, -1), (1, 0)) if p == 0 else ((2, 0), (3, 1)):
            for a in range(3):
                lhs = [acts[dc, a : a + 8, pl.ds(2 * core + 1 + dr, 2)].reshape(256, 256) for dc in range(3)]
                both = jnp.dot(lhs[1], wc[a, rc, :, 128:384], preferred_element_type=F32)
                even = even + both[:, :128] + jnp.dot(lhs[0], wc[a, rc, :, 0:128], preferred_element_type=F32)
                odd = odd + both[:, 128:] + jnp.dot(lhs[2], wc[a, rc, :, 384:512], preferred_element_type=F32)
        for f in range(8):
            for row in range(2):
                at_row = (f * 4 + 2 * row + p) * 32
                here = (f * 2 + row) * 16
                d_buf[pl.ds(at_row, 16, stride=2), :] = even[here : here + 16]
                d_buf[pl.ds(at_row + 1, 16, stride=2), :] = odd[here : here + 16]
    dec[...] = d_buf[0:1024, :].astype(BF16).reshape(8, 4, 32, 128)

    owners = [lax.rem(t + shift_h, 8) for shift_h in EXTRA]
    has_extra = jnp.logical_or(h == owners[0], jnp.logical_or(h == owners[1], h == owners[2]))
    for i, (kind, parts) in enumerate(((LAST_X, qx), (LAST_Y, qy), (LAST_Z, qz))):
        arrived(kind, parts.at[pl.ds(0, 15)])
        ag_s[i] = total_of(parts)

    @pl.when(has_extra)
    def _():
        arrived(LAST_E, qe.at[pl.ds(0, 15)])
        ag_s[3] = total_of(qe)

    @pl.when(jnp.logical_not(has_extra))
    def _():
        ag_s[3] = jnp.zeros((16, 128), BF16)

    for to_h in others_h():
        send(ag_s, ag_r.at[h], GATHER, tm, to_h)

    ag_r[h] = ag_s[...]

    arrived(AFF2, at2.at[pl.ds(0, 15)])
    total = jnp.sum(at2[...], axis=0)
    aff[0:1, 0:128] = total[0:1]
    aff[0:1, 128:256] = total[1:2]
    aff[1:2, 0:128] = total[2:3]
    aff[1:2, 128:256] = total[3:4]

    arrived(GATHER, ag_r.at[pl.ds(0, 7)])
    for k in range(8):
        for i in range(3):
            gw[8 * i + k] = ag_r[k, i].astype(F32)
    for i in range(3):
        gw[24 + i] = ag_r[owners[i], 3].astype(F32)

    sent(BLOCKS, xraw.at[pl.ds(0, 7), pl.ds(0, 2)])
    sent(COT_PAIR, cpart)
    sent(COT_ROWS, cedge.at[0])
    sent(COT_COLS, ch.at[:, pl.ds(0, 5)])
    sent(ROWS_ON, cedge.at[0])
    sent(COLS_ON, ch.at[:, pl.ds(0, 5)])
    sent(X_PAIR, xraw.at[:, pl.ds(0, 2)])
    sent(X_ROWS, xraw.at[:, pl.ds(0, 1)])
    sent(X_COLS, hc.at[:, pl.ds(0, 3)])
    sent(X_COLS_ON, hc.at[:, pl.ds(0, 1)])
    for kind, parts in ((ALONG_X, rx), (ALONG_Y, ry), (ALONG_Z, rz)):
        sent(kind, parts.at[pl.ds(0, 3)])
    for kind, parts in ((LAST_X, qx), (LAST_Y, qy), (LAST_Z, qz)):
        sent(kind, parts.at[pl.ds(0, 15)])
    sent(LAST_E, qe.at[pl.ds(0, 5)])

    @pl.when(jnp.logical_not(has_extra))
    def _():
        sent(LAST_E, qe.at[0])

    sent(GATHER, ag_r.at[pl.ds(0, 7)])
    sent(STATS1, st1.at[pl.ds(0, 7)])
    sent(STATS2, st2.at[pl.ds(0, 15)])
    sent(AFF1, at1.at[pl.ds(0, 7)])
    sent(AFF2, at2.at[pl.ds(0, 15)])


def deliver(*refs):
    copies = [pltpu.make_async_copy(refs[i], refs[3 + i], refs[6].at[i]) for i in range(3)]
    for copy in copies:
        copy.start()
    for copy in copies:
        copy.wait()


def per_device(coarse, gain, bias, weight, cotangent):
    taps = jnp.transpose(weight, (1, 2, 3, 0, 4)).reshape(27, 256, 128)
    vmem = pl.BlockSpec(memory_space=pltpu.VMEM)
    vm = pltpu.VMEM
    decoded, grad_weight, grad_affine = pl.pallas_call(
        kernel,
        out_shape=(
            jax.ShapeDtypeStruct((8, 4, 32, 128), BF16),
            jax.ShapeDtypeStruct((27, 16, 128), F32),
            jax.ShapeDtypeStruct((2, 256), F32),
        ),
        in_specs=[pl.BlockSpec(memory_space=pltpu.HBM)] * 5,
        out_specs=(vmem, vmem, vmem),
        scratch_shapes=[
            vm((2, 128, 256), BF16),
            vm((1, 256), F32),
            vm((1, 256), F32),
            vm((27, 256, 128), BF16),
            vm((8, 4, 32, 128), BF16),
            pltpu.SemaphoreType.DMA((5,)),
            vm((3, 4, 256, 512), BF16),
            vm((1, 128), F32),
            vm((1, 128), F32),
            vm((8, 1, 128), F32),
            vm((16, 1, 128), F32),
            vm((4, 128), F32),
            vm((4, 128), F32),
            vm((8, 4, 128), F32),
            vm((16, 4, 128), F32),
            vm((8, 6, 16, 256), BF16),
            vm((2, 144, 128), F32),
            vm((2, 2, 8, 256), F32),
            vm((2, 6, 8, 256), F32),
            vm((3, 10, 6, 16, 256), BF16),
            vm((288, 128), F32),
            vm((288, 128), F32),
            vm((8, 2, 16, 512), BF16),
            vm((8, 4, 32, 128), BF16),
            vm((2, 8, 1, 32, 128), BF16),
            vm((2, 4, 8, 128), F32),
            vm((2, 10, 8, 128), F32),
            vm((10 * 8 * 48 + 64, 128), F32),
            vm((9, 10, 4, 16, 128), BF16),
            *[vm((4, 18, 16, 128), BF16)] * 6,
            *[vm((18, 16, 128), BF16)] * 3,
            *[vm((16, 16, 128), BF16)] * 4,
            vm((4, 16, 128), BF16),
            vm((8, 4, 16, 128), BF16),
            vm((1056, 128), F32),
            pltpu.SemaphoreType.DMA((22,)),
            pltpu.SemaphoreType.DMA((22,)),
        ],
        compiler_params=pltpu.CompilerParams(
            collective_id=0, has_side_effects=True, vmem_limit_bytes=48 * 2**20
        ),
        cost_estimate=pl.CostEstimate(flops=2 * 10**9, bytes_accessed=4 * 10**6, transcendentals=300000),
    )(*[
        pltpu.with_memory_space_constraint(x, pltpu.HBM)
        for x in (coarse.reshape(2, 128, 256), gain.reshape(1, 256), bias.reshape(1, 256), taps, cotangent)
    ])
    decoded, grad_weight, grad_affine = pl.pallas_call(
        deliver,
        out_shape=(
            jax.ShapeDtypeStruct((8, 4, 32, 128), BF16),
            jax.ShapeDtypeStruct((27, 16, 128), F32),
            jax.ShapeDtypeStruct((2, 256), F32),
        ),
        in_specs=[pl.BlockSpec(memory_space=pltpu.VMEM)] * 3,
        out_specs=[pl.BlockSpec(memory_space=pl.ANY)] * 3,
        scratch_shapes=[pltpu.SemaphoreType.DMA((3,))],
        compiler_params=pltpu.CompilerParams(vmem_limit_bytes=8 * 2**20),
    )(decoded, grad_weight, grad_affine)
    grad_weight = jnp.transpose(grad_weight.reshape(3, 3, 3, 16, 128), (3, 0, 1, 2, 4))
    return decoded, grad_weight, grad_affine


def solution(mesh):
    return jax.shard_map(
        per_device,
        mesh=mesh,
        in_specs=(P("height", "tm", None, None), P(), P(), P(), P(None, "tm", "height", None)),
        out_specs=(P(None, "tm", "height", None), P("tm", None, None, None, None), P()),
        check_vma=False,
    )
```

```python
import functools

import jax
import jax.numpy as jnp
from jax import lax
from jax.experimental import pallas as pl
from jax.experimental.pallas import tpu as pltpu
from jax.sharding import PartitionSpec as P

MESH = pl.DeviceIdType.MESH
F32, BF16 = jnp.float32, jnp.bfloat16
EPSILON = 1e-06
NUMBERS = 8 * 32 * 128 * 8
CHIPS, HEIGHT = 8, 8
EXTRA = (0, 3, 6)

(STATS1, STATS2, BLOCKS, COT_PAIR, COT_ROWS, COT_COLS, X_PAIR, X_ROWS, X_COLS, ALONG_X, ALONG_Y, ALONG_Z, LAST_X, LAST_Y, LAST_Z, LAST_E, GATHER, AFF1, AFF2, ROWS_ON, COLS_ON, X_COLS_ON) = range(22)


def group_totals(tile):
    lane = lax.broadcasted_iota(jnp.int32, tile.shape, 1)
    for step in (1, 2, 4):
        other = jnp.where(
            (lane & step) == 0, pltpu.roll(tile, 128 - step, 1), pltpu.roll(tile, step, 1)
        )
        tile = tile + other
    return tile


def kernel(
    coarse_hbm, gain_hbm, bias_hbm, w_hbm, cot_hbm, dec, gw, aff,
    coarse, gain, bias, w, cot, fetch_sem, wc, st, sa, st1, st2, af, at, at1, at2,
    xraw, xf, xe, hc, acts, pad0, pad1, a_t,
    cpart, cedge, ce, ch, cf, s_buf,
    gx, gy, gz, rx, ry, rz, px, py, pz, qx, qy, qz, qe, ag_s, ag_r, d_buf, ssem, rsem,
):
    tm, h = lax.axis_index("tm"), lax.axis_index("height")
    core = lax.rem(tm, 2)
    t = tm // 2
    left, right = lax.rem(h + 7, 8), lax.rem(h + 1, 8)
    t_off = lax.rem(t + 7 + 2 * core, 8)
    pair = tm + 1 - 2 * core

    def others_h():
        for dz, dy in ((1, 2), (1, 1), (1, 3), (0, 2), (1, 0), (0, 1), (0, 3)):
            yield lax.rem(h // 4 + dz, 2) * 4 + lax.rem(h + dy, 4)

    def others_tm():
        for dz, dx in ((1, 2), (1, 1), (1, 3), (1, 0), (0, 2), (0, 1), (0, 3)):
            chip = lax.rem(t // 4 + dz, 2) * 4 + lax.rem(t + dx, 4)
            yield 2 * chip + core
            yield 2 * chip + 1 - core
        yield pair

    def send(src, dst, kind, to_tm, to_h):
        pltpu.make_async_remote_copy(
            src_ref=src, dst_ref=dst, send_sem=ssem.at[kind], recv_sem=rsem.at[kind],
            device_id=(to_tm, to_h), device_id_type=MESH,
        ).start()

    def arrived(kind, like):
        pltpu.make_async_copy(like, like, rsem.at[kind]).wait()

    def sent(kind, like):
        pltpu.make_async_copy(like, like, ssem.at[kind]).wait()

    pairs = ((coarse_hbm, coarse), (cot_hbm, cot), (gain_hbm, gain), (bias_hbm, bias), (w_hbm, w))
    fetches = [pltpu.make_async_copy(src, dst, fetch_sem.at[i]) for i, (src, dst) in enumerate(pairs)]
    for fetch in fetches:
        fetch.start()

    barrier = pltpu.get_barrier_semaphore()

    def greet(to_tm, to_h):
        pl.semaphore_signal(barrier, inc=1, device_id=(to_tm, to_h), device_id_type=MESH)

    for to_h in (left, right):
        greet(t_off * 2 + 1 - core, to_h)
    for to_tm in others_tm():
        greet(to_tm, h)
    for to_h in others_h():
        greet(tm, to_h)


    fetches[0].wait()
    x = coarse[...].astype(F32).reshape(256, 256)
    total = jnp.sum(x, axis=0, keepdims=True)
    squares = jnp.sum(x * x, axis=0, keepdims=True)
    quarters = (total[:, :128], total[:, 128:], squares[:, :128], squares[:, 128:])
    quarter = lax.rem(lax.broadcasted_iota(jnp.int32, (4, 128), 1), 4)
    mine = quarter == lax.broadcasted_iota(jnp.int32, (4, 128), 0)
    sums = group_totals(jnp.concatenate(quarters, axis=0))
    st[...] = jnp.sum(jnp.where(mine, sums, 0.0), axis=0, keepdims=True)

    pl.semaphore_wait(barrier, 24)

    for to_h in others_h():
        send(st, st1.at[h], STATS1, tm, to_h)

    for to_h in others_h():
        send(
            coarse.at[:, pl.ds(pl.multiple_of(to_h * 16, 16), 16), :],
            xraw.at[h, pl.ds(1 + 2 * core, 2)], BLOCKS, tm, to_h,
        )

    fetches[1].wait()
    send(cot, cpart, COT_PAIR, pair, h)
    send(cot.at[:, pl.ds(3 * core, 1)], cedge.at[1 - core], COT_ROWS, t_off * 2 + 1 - core, h)
    def cell(j, f):
        return pl.multiple_of((j * 8 + f) * 48, 8)

    for r in range(4):
        for f in range(8):
            cf[pl.ds(cell(1 + 4 * core + r, f) + 8, 32), :] = cot[f, r].astype(F32)
    for r in range(4):
        base = cell(1 + 4 * core + r, 0)
        ce[0, r] = cf[pl.ds(base + 8, 8, stride=48), :]
        ce[1, r] = cf[pl.ds(base + 39, 8, stride=48), :]

    for side, to_h in ((0, left), (1, right)):
        send(ce.at[side], ch.at[1 - side, pl.ds(1 + 4 * core, 4)], COT_COLS, tm, to_h)
        send(ce.at[side, pl.ds(3 * core, 1)], ch.at[1 - side, pl.ds(9 - 9 * core, 1)], COT_COLS, t_off * 2 + 1 - core, to_h)

    st1[h] = st[...]
    xraw[h, pl.ds(1 + 2 * core, 2)] = coarse[:, pl.ds(pl.multiple_of(h * 16, 16), 16), :]

    arrived(STATS1, st1.at[pl.ds(0, 7)])
    sa[...] = jnp.sum(st1[...], axis=0)

    for to_tm in others_tm():
        send(sa, st2.at[tm], STATS2, to_tm, h)

    st2[tm] = sa[...]

    arrived(BLOCKS, xraw.at[pl.ds(0, 7), pl.ds(0, 2)])
    own = xraw.at[:, pl.ds(1 + 2 * core, 2)]
    send(own, own, X_PAIR, pair, h)
    send(xraw.at[:, pl.ds(1 + 3 * core, 1)], xraw.at[:, pl.ds(5 - 5 * core, 1)], X_ROWS, t_off * 2 + 1 - core, h)

    s_buf[:, 8:10] = jnp.zeros((9, 2, 4, 16, 128), BF16)
    half_rows = ch.at[:, pl.ds(5 * core, 5)]
    arrived(COT_ROWS, cedge.at[0])
    send(cedge.at[core], cedge.at[core], ROWS_ON, pair, h)
    arrived(COT_COLS, ch.at[:, pl.ds(0, 5)])
    send(half_rows, half_rows, COLS_ON, pair, h)
    arrived(COT_PAIR, cpart)
    for r in range(4):
        for f in range(8):
            cf[pl.ds(cell(5 - 4 * core + r, f) + 8, 32), :] = cpart[f, r].astype(F32)
    arrived(ROWS_ON, cedge.at[0])
    arrived(COLS_ON, ch.at[:, pl.ds(0, 5)])
    top, bottom = t > 0, t < CHIPS - 1
    for f in range(8):
        cf[pl.ds(cell(0, f) + 8, 32), :] = jnp.where(top, cedge[0, f, 0].astype(F32), 0.0)
        cf[pl.ds(cell(9, f) + 8, 32), :] = jnp.where(bottom, cedge[1, f, 0].astype(F32), 0.0)
    for j in range(10):
        keep = (h > 0, h < HEIGHT - 1)
        if j == 0:
            keep = tuple(jnp.logical_and(k, top) for k in keep)
        if j == 9:
            keep = tuple(jnp.logical_and(k, bottom) for k in keep)
        cf[pl.ds(j * 384 + 7, 8, stride=48), :] = jnp.where(keep[0], ch[0, j], 0.0)
        cf[pl.ds(j * 384 + 40, 8, stride=48), :] = jnp.where(keep[1], ch[1, j], 0.0)

    @pl.loop(0, 8)
    def _(f):
        sums = []
        for j in range(10):
            base = cell(j, f)
            cols = [cf[pl.ds(base + 7 + i, 16, stride=2), :] for i in range(4)]
            sums.append((cols[2] + cols[3], cols[1] + cols[2], cols[0] + cols[1]))
        for b in range(3):
            for e in range(3):
                for row in range(4):
                    s_buf[b * 3 + e, f, row] = (sums[2 * row + 2 - b][e] + sums[2 * row + 3 - b][e]).astype(BF16)

    for r in range(2):
        rows = xraw[:, 1 + 2 * core + r].astype(F32).reshape(128, 256)
        for half in range(2):
            xf[half, 0:128, :] = rows[:, 128 * half : 128 * half + 128]
            for side, column in ((0, 0), (1, 15)):
                xe[side, r, :, 128 * half : 128 * half + 128] = xf.at[half][pl.ds(column, 8, stride=16), :]
    for side, to_h in ((0, left), (1, right)):
        send(xe.at[side], hc.at[1 - side, pl.ds(1 + 2 * core, 2)], X_COLS, tm, to_h)
        send(xe.at[side, pl.ds(core, 1)], hc.at[1 - side, pl.ds(5 - 5 * core, 1)], X_COLS, t_off * 2 + 1 - core, to_h)

    fetches[2].wait()
    fetches[3].wait()
    arrived(STATS2, st2.at[pl.ds(0, 15)])
    first_four = lax.rem(lax.broadcasted_iota(jnp.int32, (4, 128), 1), 8) < 4
    sums = jnp.broadcast_to(jnp.sum(st2[...], axis=0), (4, 128))
    stats = group_totals(jnp.where(jnp.logical_and(mine, first_four), sums, 0.0)) / NUMBERS
    mean = jnp.concatenate([stats[0:1], stats[1:2]], axis=1)
    square = jnp.concatenate([stats[2:3], stats[3:4]], axis=1)
    inverse = lax.rsqrt(square - mean * mean + EPSILON)
    scale, shift = inverse * gain[...], bias[...]

    def activate(v):
        shifted = (v - mean) * scale + shift
        return shifted * jax.nn.sigmoid(shifted)

    arrived(X_PAIR, xraw.at[:, pl.ds(0, 2)])
    for j in range(1, 5):
        act = activate(xraw[:, j].astype(F32).reshape(128, 256))
        acts[1, 2:10, j] = act.astype(BF16).reshape(8, 16, 256)

    turned = jnp.transpose(acts[1, 2:10, 1:5].reshape(512, 256))
    a_t[...] = turned.reshape(8, 2, 16, 512)

    zhi, x_at, zlo, y_at = t // 4, lax.rem(t, 4), h // 4, lax.rem(h, 4)
    z_at = 2 * zhi + zlo

    def products(first, count, keep):
        lhs = a_t[:, core].reshape(128, 512)
        for tap in range(first, first + count, 2):
            taps = range(tap, min(tap + 2, first + count))
            rhs = [s_buf[n % 9, 2 - n // 9 : 10 - n // 9].reshape(512, 128) for n in taps]
            rhs = jnp.concatenate(rhs, axis=1) if len(rhs) == 2 else rhs[0]
            out = jnp.dot(lhs, rhs, preferred_element_type=F32).astype(BF16)
            for i, n in enumerate(taps):
                keep(n - first, out[:, 128 * i : 128 * i + 128].reshape(8, 16, 128))

    def keep_x(n, tiles):
        for z in range(2):
            gx[:, 8 * z + n] = tiles[4 * z : 4 * z + 4]

    def keep_y(n, tiles):
        gy[n % 4, 8 * (n // 4) : 8 * (n // 4) + 8] = tiles

    def keep_z(n, tiles):
        for z in range(2):
            for x in range(4):
                gz[2 * z + n // 4, 4 * x + n % 4] = tiles[4 * z + x]

    def keep_extra(n, tiles):
        for to in range(4):
            if n == 0:
                first, second = to, to + 4
            elif n == 1:
                first, second = (to + 1) % 4, (to + 1) % 4 + 4
            else:
                first = 4 * (to // 2) + 2 * (to // 2 == to % 2)
                second = first + 1
            (gx, gy, gz)[n][to, 16] = tiles[first]
            (gx, gy, gz)[n][to, 17] = tiles[second]

    far = (2, 1, 3)
    products(24, 3, keep_extra)
    products(0, 8, keep_x)
    for k in far:
        to = lax.rem(x_at + k, 4)
        send(gx.at[to], rx.at[x_at], ALONG_X, (zhi * 4 + to) * 2 + core, h)
    products(8, 8, keep_y)
    for k in far:
        to = lax.rem(y_at + k, 4)
        send(gy.at[to], ry.at[y_at], ALONG_Y, tm, zlo * 4 + to)
    products(16, 8, keep_z)
    for k in far:
        to = lax.rem(z_at + k, 4)
        send(gz.at[to], rz.at[z_at], ALONG_Z, (to // 2 * 4 + x_at) * 2 + core, lax.rem(to, 2) * 4 + y_at)
    rx[x_at] = gx[x_at]
    ry[y_at] = gy[y_at]
    rz[z_at] = gz[z_at]
    fetches[4].wait()
    grad = jnp.zeros((256, 256), F32)
    for first in range(0, 27, 2):
        taps = range(first, min(first + 2, 27))
        lhs = [s_buf[n % 9, 2 - n // 9 : 10 - n // 9, pl.ds(2 * core, 2)].reshape(256, 128) for n in taps]
        rhs = [w[n] for n in taps]
        if len(lhs) == 2:
            lhs, rhs = [jnp.concatenate(lhs, axis=1)], [jnp.concatenate(rhs, axis=1)]
        grad = grad + lax.dot_general(lhs[0], rhs[0], (((1,), (1,)), ((), ())), preferred_element_type=F32)

    normed = (xraw[:, pl.ds(1 + 2 * core, 2)].astype(F32).reshape(256, 256) - mean) * inverse
    shifted = normed * gain[...] + shift
    sig = jax.nn.sigmoid(shifted)
    grad = grad * sig * (1.0 + shifted * (1.0 - sig))
    d_gain = jnp.sum(grad * normed, axis=0, keepdims=True)
    d_bias = jnp.sum(grad, axis=0, keepdims=True)
    af[...] = jnp.concatenate([d_gain[:, :128], d_gain[:, 128:], d_bias[:, :128], d_bias[:, 128:]], axis=0)

    for to_h in others_h():
        send(af, at1.at[h], AFF1, tm, to_h)

    at1[h] = af[...]

    arrived(X_COLS, hc.at[:, pl.ds(0, 3)])
    next_to_pair = hc.at[:, pl.ds(2 + core, 1)]
    send(next_to_pair, next_to_pair, X_COLS_ON, pair, h)


    @pl.loop(0, 48)
    def _(step):
        a = step // 16
        rows = pl.ds(pl.multiple_of(lax.rem(step, 16) * 16, 16), 16)
        taps = [[w[a * 9 + b * 3 + e, rows, :].astype(F32) for e in range(3)] for b in range(3)]
        for rc, bs in enumerate(((0,), (1, 2), (0, 1), (2,))):
            line = [taps[bs[0]][e] if len(bs) == 1 else taps[bs[0]][e] + taps[bs[1]][e] for e in range(3)]
            for cc, value in enumerate((line[0], line[1] + line[2], line[0] + line[1], line[2])):
                wc[a, rc, rows, 128 * cc : 128 * cc + 128] = value.astype(BF16)

    acts[:, 0:2] = jnp.zeros((3, 2, 6, 16, 256), BF16)
    arrived(X_ROWS, xraw.at[:, pl.ds(0, 1)])
    arrived(X_COLS_ON, hc.at[:, pl.ds(0, 1)])
    border = 5 * core
    inside = jnp.where(core == 0, t > 0, t < CHIPS - 1)
    act = jnp.where(inside, activate(xraw[:, border].astype(F32).reshape(128, 256)), 0.0)
    acts[1, 2:10, border] = act.astype(BF16).reshape(8, 16, 256)
    pads = (pad0, pad1)

    @pl.loop(0, 4)
    def _(k):
        j = 2 * core + k
        here = jnp.logical_or(j != border, inside)
        act = acts[1, 2:10, j].astype(F32).reshape(128, 256)
        act_l = jnp.where(jnp.logical_and(here, h > 0), activate(hc[0, j]), 0.0)
        act_r = jnp.where(jnp.logical_and(here, h < HEIGHT - 1), activate(hc[1, j]), 0.0)
        for half in range(2):
            lanes = slice(128 * half, 128 * half + 128)
            pad = pads[half]
            for f in range(8):
                pad[32 * f + 8 : 32 * f + 24, :] = act[16 * f : 16 * f + 16, lanes]
            pad[pl.ds(7, 8, stride=32), :] = act_l[:, lanes]
            pad[pl.ds(24, 8, stride=32), :] = act_r[:, lanes]
            for f in range(8):
                acts[0, 2 + f, j, :, lanes] = pad[32 * f + 7 : 32 * f + 23, :].astype(BF16)
                acts[2, 2 + f, j, :, lanes] = pad[32 * f + 9 : 32 * f + 25, :].astype(BF16)

    def total_of(parts):
        return jnp.sum(parts[...].astype(F32), axis=0).astype(BF16)

    arrived(ALONG_X, rx.at[pl.ds(0, 3)])
    px[...] = total_of(rx)
    for dz in (1, 0):
        for k in (6, 2, 5, 7, 1, 3, 4, 0):
            if dz or k:
                to_z, to_h = lax.rem(zhi + dz, 2), lax.rem(h + k, 8)
                send(px.at[to_z * 8 + to_h], qx.at[zhi * 8 + h], LAST_X, (to_z * 4 + x_at) * 2 + core, to_h)
    arrived(ALONG_Y, ry.at[pl.ds(0, 3)])
    py[...] = total_of(ry)
    for dz in (1, 0):
        for k in (6, 2, 5, 7, 1, 3, 4, 0):
            if dz or k:
                to_z, to_t = lax.rem(zlo + dz, 2), lax.rem(t + k, 8)
                send(py.at[to_z * 8 + to_t], qy.at[zlo * 8 + t], LAST_Y, to_t * 2 + core, to_z * 4 + y_at)
    arrived(ALONG_Z, rz.at[pl.ds(0, 3)])
    pz[...] = total_of(rz)
    for dx in (2, 1, 3, 0):
        for dy in (2, 1, 3, 0):
            if dx or dy:
                to_x, to_y = lax.rem(x_at + dx, 4), lax.rem(y_at + dy, 4)
                send(pz.at[to_x * 4 + to_y], qz.at[x_at * 4 + y_at], LAST_Z, (zhi * 4 + to_x) * 2 + core, zlo * 4 + to_y)

    def extra(tile, at, to_t, to_h):
        here = jnp.logical_and(to_t == t, to_h == h)

        @pl.when(jnp.logical_not(here))
        def _():
            send(tile, qe.at[at], LAST_E, to_t * 2 + core, to_h)

        @pl.when(here)
        def _():
            qe[at] = tile[...]

    for i in range(2):
        to_t = 4 * i + x_at
        extra(px.at[16 + i], zhi * 8 + h, to_t, to_t)
        to_t = 4 * i + lax.rem(y_at + 1, 4)
        extra(py.at[16 + i], zlo * 8 + t, to_t, lax.rem(to_t + EXTRA[1], 8))
        to_t = 4 * zhi + jnp.where(zhi == zlo, 2, 0) + i
        extra(pz.at[16 + i], x_at * 4 + y_at, to_t, lax.rem(to_t + EXTRA[2], 8))
    qx[zhi * 8 + h] = px[zhi * 8 + h]
    qy[zlo * 8 + t] = py[zlo * 8 + t]
    qz[x_at * 4 + y_at] = pz[x_at * 4 + y_at]

    arrived(AFF1, at1.at[pl.ds(0, 7)])
    at[...] = jnp.sum(at1[...], axis=0)

    for to_tm in others_tm():
        send(at, at2.at[tm], AFF2, to_tm, h)

    at2[tm] = at[...]

    for p in range(2):
        even = jnp.zeros((256, 128), F32)
        odd = jnp.zeros((256, 128), F32)
        for rc, dr in ((0, -1), (1, 0)) if p == 0 else ((2, 0), (3, 1)):
            for a in range(3):
                lhs = [acts[dc, a : a + 8, pl.ds(2 * core + 1 + dr, 2)].reshape(256, 256) for dc in range(3)]
                both = jnp.dot(lhs[1], wc[a, rc, :, 128:384], preferred_element_type=F32)
                even = even + both[:, :128] + jnp.dot(lhs[0], wc[a, rc, :, 0:128], preferred_element_type=F32)
                odd = odd + both[:, 128:] + jnp.dot(lhs[2], wc[a, rc, :, 384:512], preferred_element_type=F32)
        for f in range(8):
            for row in range(2):
                at_row = (f * 4 + 2 * row + p) * 32
                here = (f * 2 + row) * 16
                d_buf[pl.ds(at_row, 16, stride=2), :] = even[here : here + 16]
                d_buf[pl.ds(at_row + 1, 16, stride=2), :] = odd[here : here + 16]
    dec[...] = d_buf[0:1024, :].astype(BF16).reshape(8, 4, 32, 128)

    owners = [lax.rem(t + shift_h, 8) for shift_h in EXTRA]
    has_extra = jnp.logical_or(h == owners[0], jnp.logical_or(h == owners[1], h == owners[2]))
    for i, (kind, parts) in enumerate(((LAST_X, qx), (LAST_Y, qy), (LAST_Z, qz))):
        arrived(kind, parts.at[pl.ds(0, 15)])
        ag_s[i] = total_of(parts)

    @pl.when(has_extra)
    def _():
        arrived(LAST_E, qe.at[pl.ds(0, 15)])
        ag_s[3] = total_of(qe)

    @pl.when(jnp.logical_not(has_extra))
    def _():
        ag_s[3] = jnp.zeros((16, 128), BF16)

    for to_h in others_h():
        send(ag_s, ag_r.at[h], GATHER, tm, to_h)

    ag_r[h] = ag_s[...]

    arrived(AFF2, at2.at[pl.ds(0, 15)])
    total = jnp.sum(at2[...], axis=0)
    aff[0:1, 0:128] = total[0:1]
    aff[0:1, 128:256] = total[1:2]
    aff[1:2, 0:128] = total[2:3]
    aff[1:2, 128:256] = total[3:4]

    arrived(GATHER, ag_r.at[pl.ds(0, 7)])
    for k in range(8):
        for i in range(3):
            gw[8 * i + k] = ag_r[k, i].astype(F32)
    for i in range(3):
        gw[24 + i] = ag_r[owners[i], 3].astype(F32)

    sent(BLOCKS, xraw.at[pl.ds(0, 7), pl.ds(0, 2)])
    sent(COT_PAIR, cpart)
    sent(COT_ROWS, cedge.at[0])
    sent(COT_COLS, ch.at[:, pl.ds(0, 5)])
    sent(ROWS_ON, cedge.at[0])
    sent(COLS_ON, ch.at[:, pl.ds(0, 5)])
    sent(X_PAIR, xraw.at[:, pl.ds(0, 2)])
    sent(X_ROWS, xraw.at[:, pl.ds(0, 1)])
    sent(X_COLS, hc.at[:, pl.ds(0, 3)])
    sent(X_COLS_ON, hc.at[:, pl.ds(0, 1)])
    for kind, parts in ((ALONG_X, rx), (ALONG_Y, ry), (ALONG_Z, rz)):
        sent(kind, parts.at[pl.ds(0, 3)])
    for kind, parts in ((LAST_X, qx), (LAST_Y, qy), (LAST_Z, qz)):
        sent(kind, parts.at[pl.ds(0, 15)])
    sent(LAST_E, qe.at[pl.ds(0, 5)])

    @pl.when(jnp.logical_not(has_extra))
    def _():
        sent(LAST_E, qe.at[0])

    sent(GATHER, ag_r.at[pl.ds(0, 7)])
    sent(STATS1, st1.at[pl.ds(0, 7)])
    sent(STATS2, st2.at[pl.ds(0, 15)])
    sent(AFF1, at1.at[pl.ds(0, 7)])
    sent(AFF2, at2.at[pl.ds(0, 15)])


def deliver(*refs):
    copies = [pltpu.make_async_copy(refs[i], refs[3 + i], refs[6].at[i]) for i in range(3)]
    for copy in copies:
        copy.start()
    for copy in copies:
        copy.wait()


def per_device(coarse, gain, bias, weight, cotangent):
    taps = jnp.transpose(weight, (1, 2, 3, 0, 4)).reshape(27, 256, 128)
    vmem = pl.BlockSpec(memory_space=pltpu.VMEM)
    vm = pltpu.VMEM
    decoded, grad_weight, grad_affine = pl.pallas_call(
        kernel,
        out_shape=(
            jax.ShapeDtypeStruct((8, 4, 32, 128), BF16),
            jax.ShapeDtypeStruct((27, 16, 128), F32),
            jax.ShapeDtypeStruct((2, 256), F32),
        ),
        in_specs=[pl.BlockSpec(memory_space=pltpu.HBM)] * 5,
        out_specs=(vmem, vmem, vmem),
        scratch_shapes=[
            vm((2, 128, 256), BF16),
            vm((1, 256), F32),
            vm((1, 256), F32),
            vm((27, 256, 128), BF16),
            vm((8, 4, 32, 128), BF16),
            pltpu.SemaphoreType.DMA((5,)),
            vm((3, 4, 256, 512), BF16),
            vm((1, 128), F32),
            vm((1, 128), F32),
            vm((8, 1, 128), F32),
            vm((16, 1, 128), F32),
            vm((4, 128), F32),
            vm((4, 128), F32),
            vm((8, 4, 128), F32),
            vm((16, 4, 128), F32),
            vm((8, 6, 16, 256), BF16),
            vm((2, 144, 128), F32),
            vm((2, 2, 8, 256), F32),
            vm((2, 6, 8, 256), F32),
            vm((3, 10, 6, 16, 256), BF16),
            vm((288, 128), F32),
            vm((288, 128), F32),
            vm((8, 2, 16, 512), BF16),
            vm((8, 4, 32, 128), BF16),
            vm((2, 8, 1, 32, 128), BF16),
            vm((2, 4, 8, 128), F32),
            vm((2, 10, 8, 128), F32),
            vm((10 * 8 * 48 + 64, 128), F32),
            vm((9, 10, 4, 16, 128), BF16),
            *[vm((4, 18, 16, 128), BF16)] * 6,
            *[vm((18, 16, 128), BF16)] * 3,
            *[vm((16, 16, 128), BF16)] * 4,
            vm((4, 16, 128), BF16),
            vm((8, 4, 16, 128), BF16),
            vm((1056, 128), F32),
            pltpu.SemaphoreType.DMA((22,)),
            pltpu.SemaphoreType.DMA((22,)),
        ],
        compiler_params=pltpu.CompilerParams(
            collective_id=0, has_side_effects=True, vmem_limit_bytes=48 * 2**20
        ),
        cost_estimate=pl.CostEstimate(flops=2 * 10**9, bytes_accessed=4 * 10**6, transcendentals=300000),
    )(*[
        pltpu.with_memory_space_constraint(x, pltpu.HBM)
        for x in (coarse.reshape(2, 128, 256), gain.reshape(1, 256), bias.reshape(1, 256), taps, cotangent)
    ])
    decoded, grad_weight, grad_affine = pl.pallas_call(
        deliver,
        out_shape=(
            jax.ShapeDtypeStruct((8, 4, 32, 128), BF16),
            jax.ShapeDtypeStruct((27, 16, 128), F32),
            jax.ShapeDtypeStruct((2, 256), F32),
        ),
        in_specs=[pl.BlockSpec(memory_space=pltpu.VMEM)] * 3,
        out_specs=[pl.BlockSpec(memory_space=pl.ANY)] * 3,
        scratch_shapes=[pltpu.SemaphoreType.DMA((3,))],
        compiler_params=pltpu.CompilerParams(vmem_limit_bytes=8 * 2**20),
    )(decoded, grad_weight, grad_affine)
    grad_weight = jnp.transpose(grad_weight.reshape(3, 3, 3, 16, 128), (3, 0, 1, 2, 4))
    return decoded, grad_weight, grad_affine


def solution(mesh):
    return jax.shard_map(
        per_device,
        mesh=mesh,
        in_specs=(P("height", "tm", None, None), P(), P(), P(), P(None, "tm", "height", None)),
        out_specs=(P(None, "tm", "height", None), P("tm", None, None, None, None), P()),
        check_vma=False,
    )
```

```python
import functools

import jax
import jax.numpy as jnp
from jax import lax
from jax.experimental import pallas as pl
from jax.experimental.pallas import tpu as pltpu
from jax.sharding import PartitionSpec as P

MESH = pl.DeviceIdType.MESH
F32, BF16 = jnp.float32, jnp.bfloat16
EPSILON = 1e-06
NUMBERS = 8 * 32 * 128 * 8
CHIPS, HEIGHT = 8, 8
EXTRA = (0, 3, 6)

(STATS1, STATS2, BLOCKS, COT_PAIR, COT_ROWS, COT_COLS, X_PAIR, X_ROWS, X_COLS, ALONG_X, ALONG_Y, ALONG_Z, LAST_X, LAST_Y, LAST_Z, LAST_E, GATHER, AFF1, AFF2, ROWS_ON, COLS_ON, X_COLS_ON) = range(22)


def group_totals(tile):
    lane = lax.broadcasted_iota(jnp.int32, tile.shape, 1)
    for step in (1, 2, 4):
        other = jnp.where(
            (lane & step) == 0, pltpu.roll(tile, 128 - step, 1), pltpu.roll(tile, step, 1)
        )
        tile = tile + other
    return tile


def kernel(
    coarse_hbm, gain_hbm, bias_hbm, w_hbm, cot_hbm, dec, gw, aff,
    coarse, gain, bias, w, cot, fetch_sem, wc, st, sa, st1, st2, af, at, at1, at2,
    xraw, xf, xe, hc, acts, pad0, pad1, a_t,
    cpart, cedge, ce, ch, cf, s_buf,
    gx, gy, gz, rx, ry, rz, px, py, pz, qx, qy, qz, qe, ag_s, ag_r, d_buf, ssem, rsem,
):
    tm, h = lax.axis_index("tm"), lax.axis_index("height")
    core = lax.rem(tm, 2)
    t = tm // 2
    left, right = lax.rem(h + 7, 8), lax.rem(h + 1, 8)
    t_off = lax.rem(t + 7 + 2 * core, 8)
    pair = tm + 1 - 2 * core

    def others_h():
        for dz, dy in ((1, 2), (1, 1), (1, 3), (0, 2), (1, 0), (0, 1), (0, 3)):
            yield lax.rem(h // 4 + dz, 2) * 4 + lax.rem(h + dy, 4)

    def others_tm():
        for dz, dx in ((1, 2), (1, 1), (1, 3), (1, 0), (0, 2), (0, 1), (0, 3)):
            chip = lax.rem(t // 4 + dz, 2) * 4 + lax.rem(t + dx, 4)
            yield 2 * chip + core
            yield 2 * chip + 1 - core
        yield pair

    def send(src, dst, kind, to_tm, to_h):
        pltpu.make_async_remote_copy(
            src_ref=src, dst_ref=dst, send_sem=ssem.at[kind], recv_sem=rsem.at[kind],
            device_id=(to_tm, to_h), device_id_type=MESH,
        ).start()

    def arrived(kind, like):
        pltpu.make_async_copy(like, like, rsem.at[kind]).wait()

    def sent(kind, like):
        pltpu.make_async_copy(like, like, ssem.at[kind]).wait()

    pairs = ((coarse_hbm, coarse), (cot_hbm, cot), (gain_hbm, gain), (bias_hbm, bias), (w_hbm, w))
    fetches = [pltpu.make_async_copy(src, dst, fetch_sem.at[i]) for i, (src, dst) in enumerate(pairs)]
    for fetch in fetches:
        fetch.start()

    barrier = pltpu.get_barrier_semaphore()

    def greet(to_tm, to_h):
        pl.semaphore_signal(barrier, inc=1, device_id=(to_tm, to_h), device_id_type=MESH)

    for to_h in (left, right):
        greet(t_off * 2 + 1 - core, to_h)
    for to_tm in others_tm():
        greet(to_tm, h)
    for to_h in others_h():
        greet(tm, to_h)


    fetches[0].wait()
    x = coarse[...].astype(F32).reshape(256, 256)
    total = jnp.sum(x, axis=0, keepdims=True)
    squares = jnp.sum(x * x, axis=0, keepdims=True)
    quarters = (total[:, :128], total[:, 128:], squares[:, :128], squares[:, 128:])
    quarter = lax.rem(lax.broadcasted_iota(jnp.int32, (4, 128), 1), 4)
    mine = quarter == lax.broadcasted_iota(jnp.int32, (4, 128), 0)
    sums = group_totals(jnp.concatenate(quarters, axis=0))
    st[...] = jnp.sum(jnp.where(mine, sums, 0.0), axis=0, keepdims=True)

    pl.semaphore_wait(barrier, 24)

    for to_h in others_h():
        send(st, st1.at[h], STATS1, tm, to_h)

    fetches[1].wait()
    send(cot, cpart, COT_PAIR, pair, h)
    send(cot.at[:, pl.ds(3 * core, 1)], cedge.at[1 - core], COT_ROWS, t_off * 2 + 1 - core, h)
    def cell(j, f):
        return pl.multiple_of((j * 8 + f) * 48, 8)

    for r in range(4):
        for f in range(8):
            cf[pl.ds(cell(1 + 4 * core + r, f) + 8, 32), :] = cot[f, r].astype(F32)
    for r in range(4):
        base = cell(1 + 4 * core + r, 0)
        ce[0, r] = cf[pl.ds(base + 8, 8, stride=48), :]
        ce[1, r] = cf[pl.ds(base + 39, 8, stride=48), :]

    for side, to_h in ((0, left), (1, right)):
        send(ce.at[side], ch.at[1 - side, pl.ds(1 + 4 * core, 4)], COT_COLS, tm, to_h)
        send(ce.at[side, pl.ds(3 * core, 1)], ch.at[1 - side, pl.ds(9 - 9 * core, 1)], COT_COLS, t_off * 2 + 1 - core, to_h)

    for to_h in others_h():
        send(
            coarse.at[:, pl.ds(pl.multiple_of(to_h * 16, 16), 16), :],
            xraw.at[h, pl.ds(1 + 2 * core, 2)], BLOCKS, tm, to_h,
        )

    st1[h] = st[...]
    xraw[h, pl.ds(1 + 2 * core, 2)] = coarse[:, pl.ds(pl.multiple_of(h * 16, 16), 16), :]

    arrived(STATS1, st1.at[pl.ds(0, 7)])
    sa[...] = jnp.sum(st1[...], axis=0)

    for to_tm in others_tm():
        send(sa, st2.at[tm], STATS2, to_tm, h)

    st2[tm] = sa[...]

    arrived(BLOCKS, xraw.at[pl.ds(0, 7), pl.ds(0, 2)])
    own = xraw.at[:, pl.ds(1 + 2 * core, 2)]
    send(own, own, X_PAIR, pair, h)
    send(xraw.at[:, pl.ds(1 + 3 * core, 1)], xraw.at[:, pl.ds(5 - 5 * core, 1)], X_ROWS, t_off * 2 + 1 - core, h)

    s_buf[:, 8:10] = jnp.zeros((9, 2, 4, 16, 128), BF16)
    half_rows = ch.at[:, pl.ds(5 * core, 5)]
    arrived(COT_ROWS, cedge.at[0])
    send(cedge.at[core], cedge.at[core], ROWS_ON, pair, h)
    arrived(COT_COLS, ch.at[:, pl.ds(0, 5)])
    send(half_rows, half_rows, COLS_ON, pair, h)
    arrived(COT_PAIR, cpart)
    for r in range(4):
        for f in range(8):
            cf[pl.ds(cell(5 - 4 * core + r, f) + 8, 32), :] = cpart[f, r].astype(F32)
    arrived(ROWS_ON, cedge.at[0])
    arrived(COLS_ON, ch.at[:, pl.ds(0, 5)])
    top, bottom = t > 0, t < CHIPS - 1
    for f in range(8):
        cf[pl.ds(cell(0, f) + 8, 32), :] = jnp.where(top, cedge[0, f, 0].astype(F32), 0.0)
        cf[pl.ds(cell(9, f) + 8, 32), :] = jnp.where(bottom, cedge[1, f, 0].astype(F32), 0.0)
    for j in range(10):
        keep = (h > 0, h < HEIGHT - 1)
        if j == 0:
            keep = tuple(jnp.logical_and(k, top) for k in keep)
        if j == 9:
            keep = tuple(jnp.logical_and(k, bottom) for k in keep)
        cf[pl.ds(j * 384 + 7, 8, stride=48), :] = jnp.where(keep[0], ch[0, j], 0.0)
        cf[pl.ds(j * 384 + 40, 8, stride=48), :] = jnp.where(keep[1], ch[1, j], 0.0)

    @pl.loop(0, 8)
    def _(f):
        sums = []
        for j in range(10):
            base = cell(j, f)
            cols = [cf[pl.ds(base + 7 + i, 16, stride=2), :] for i in range(4)]
            sums.append((cols[2] + cols[3], cols[1] + cols[2], cols[0] + cols[1]))
        for b in range(3):
            for e in range(3):
                for row in range(4):
                    s_buf[b * 3 + e, f, row] = (sums[2 * row + 2 - b][e] + sums[2 * row + 3 - b][e]).astype(BF16)

    for r in range(2):
        rows = xraw[:, 1 + 2 * core + r].astype(F32).reshape(128, 256)
        for half in range(2):
            xf[half, 0:128, :] = rows[:, 128 * half : 128 * half + 128]
            for side, column in ((0, 0), (1, 15)):
                xe[side, r, :, 128 * half : 128 * half + 128] = xf.at[half][pl.ds(column, 8, stride=16), :]
    for side, to_h in ((0, left), (1, right)):
        send(xe.at[side], hc.at[1 - side, pl.ds(1 + 2 * core, 2)], X_COLS, tm, to_h)
        send(xe.at[side, pl.ds(core, 1)], hc.at[1 - side, pl.ds(5 - 5 * core, 1)], X_COLS, t_off * 2 + 1 - core, to_h)

    fetches[2].wait()
    fetches[3].wait()
    arrived(STATS2, st2.at[pl.ds(0, 15)])
    first_four = lax.rem(lax.broadcasted_iota(jnp.int32, (4, 128), 1), 8) < 4
    sums = jnp.broadcast_to(jnp.sum(st2[...], axis=0), (4, 128))
    stats = group_totals(jnp.where(jnp.logical_and(mine, first_four), sums, 0.0)) / NUMBERS
    mean = jnp.concatenate([stats[0:1], stats[1:2]], axis=1)
    square = jnp.concatenate([stats[2:3], stats[3:4]], axis=1)
    inverse = lax.rsqrt(square - mean * mean + EPSILON)
    scale, shift = inverse * gain[...], bias[...]

    def activate(v):
        shifted = (v - mean) * scale + shift
        return shifted * jax.nn.sigmoid(shifted)

    arrived(X_PAIR, xraw.at[:, pl.ds(0, 2)])
    for j in range(1, 5):
        act = activate(xraw[:, j].astype(F32).reshape(128, 256))
        acts[1, 2:10, j] = act.astype(BF16).reshape(8, 16, 256)

    turned = jnp.transpose(acts[1, 2:10, 1:5].reshape(512, 256))
    a_t[...] = turned.reshape(8, 2, 16, 512)

    zhi, x_at, zlo, y_at = t // 4, lax.rem(t, 4), h // 4, lax.rem(h, 4)
    z_at = 2 * zhi + zlo

    def products(first, count, keep):
        lhs = a_t[:, core].reshape(128, 512)
        for tap in range(first, first + count, 2):
            taps = range(tap, min(tap + 2, first + count))
            rhs = [s_buf[n % 9, 2 - n // 9 : 10 - n // 9].reshape(512, 128) for n in taps]
            rhs = jnp.concatenate(rhs, axis=1) if len(rhs) == 2 else rhs[0]
            out = jnp.dot(lhs, rhs, preferred_element_type=F32).astype(BF16)
            for i, n in enumerate(taps):
                keep(n - first, out[:, 128 * i : 128 * i + 128].reshape(8, 16, 128))

    def keep_x(n, tiles):
        for z in range(2):
            gx[:, 8 * z + n] = tiles[4 * z : 4 * z + 4]

    def keep_y(n, tiles):
        gy[n % 4, 8 * (n // 4) : 8 * (n // 4) + 8] = tiles

    def keep_z(n, tiles):
        for z in range(2):
            for x in range(4):
                gz[2 * z + n // 4, 4 * x + n % 4] = tiles[4 * z + x]

    def keep_extra(n, tiles):
        for to in range(4):
            if n == 0:
                first, second = to, to + 4
            elif n == 1:
                first, second = (to + 1) % 4, (to + 1) % 4 + 4
            else:
                first = 4 * (to // 2) + 2 * (to // 2 == to % 2)
                second = first + 1
            (gx, gy, gz)[n][to, 16] = tiles[first]
            (gx, gy, gz)[n][to, 17] = tiles[second]

    far = (2, 1, 3)
    products(24, 3, keep_extra)
    products(0, 8, keep_x)
    for k in far:
        to = lax.rem(x_at + k, 4)
        send(gx.at[to], rx.at[x_at], ALONG_X, (zhi * 4 + to) * 2 + core, h)
    products(8, 8, keep_y)
    for k in far:
        to = lax.rem(y_at + k, 4)
        send(gy.at[to], ry.at[y_at], ALONG_Y, tm, zlo * 4 + to)
    products(16, 8, keep_z)
    for k in far:
        to = lax.rem(z_at + k, 4)
        send(gz.at[to], rz.at[z_at], ALONG_Z, (to // 2 * 4 + x_at) * 2 + core, lax.rem(to, 2) * 4 + y_at)
    rx[x_at] = gx[x_at]
    ry[y_at] = gy[y_at]
    rz[z_at] = gz[z_at]
    fetches[4].wait()
    grad = jnp.zeros((256, 256), F32)
    for first in range(0, 27, 2):
        taps = range(first, min(first + 2, 27))
        lhs = [s_buf[n % 9, 2 - n // 9 : 10 - n // 9, pl.ds(2 * core, 2)].reshape(256, 128) for n in taps]
        rhs = [w[n] for n in taps]
        if len(lhs) == 2:
            lhs, rhs = [jnp.concatenate(lhs, axis=1)], [jnp.concatenate(rhs, axis=1)]
        grad = grad + lax.dot_general(lhs[0], rhs[0], (((1,), (1,)), ((), ())), preferred_element_type=F32)

    normed = (xraw[:, pl.ds(1 + 2 * core, 2)].astype(F32).reshape(256, 256) - mean) * inverse
    shifted = normed * gain[...] + shift
    sig = jax.nn.sigmoid(shifted)
    grad = grad * sig * (1.0 + shifted * (1.0 - sig))
    d_gain = jnp.sum(grad * normed, axis=0, keepdims=True)
    d_bias = jnp.sum(grad, axis=0, keepdims=True)
    af[...] = jnp.concatenate([d_gain[:, :128], d_gain[:, 128:], d_bias[:, :128], d_bias[:, 128:]], axis=0)

    for to_h in others_h():
        send(af, at1.at[h], AFF1, tm, to_h)

    at1[h] = af[...]

    arrived(X_COLS, hc.at[:, pl.ds(0, 3)])
    next_to_pair = hc.at[:, pl.ds(2 + core, 1)]
    send(next_to_pair, next_to_pair, X_COLS_ON, pair, h)


    @pl.loop(0, 48)
    def _(step):
        a = step // 16
        rows = pl.ds(pl.multiple_of(lax.rem(step, 16) * 16, 16), 16)
        taps = [[w[a * 9 + b * 3 + e, rows, :].astype(F32) for e in range(3)] for b in range(3)]
        for rc, bs in enumerate(((0,), (1, 2), (0, 1), (2,))):
            line = [taps[bs[0]][e] if len(bs) == 1 else taps[bs[0]][e] + taps[bs[1]][e] for e in range(3)]
            for cc, value in enumerate((line[0], line[1] + line[2], line[0] + line[1], line[2])):
                wc[a, rc, rows, 128 * cc : 128 * cc + 128] = value.astype(BF16)

    acts[:, 0:2] = jnp.zeros((3, 2, 6, 16, 256), BF16)
    arrived(X_ROWS, xraw.at[:, pl.ds(0, 1)])
    arrived(X_COLS_ON, hc.at[:, pl.ds(0, 1)])
    border = 5 * core
    inside = jnp.where(core == 0, t > 0, t < CHIPS - 1)
    act = jnp.where(inside, activate(xraw[:, border].astype(F32).reshape(128, 256)), 0.0)
    acts[1, 2:10, border] = act.astype(BF16).reshape(8, 16, 256)
    pads = (pad0, pad1)

    @pl.loop(0, 4)
    def _(k):
        j = 2 * core + k
        here = jnp.logical_or(j != border, inside)
        act = acts[1, 2:10, j].astype(F32).reshape(128, 256)
        act_l = jnp.where(jnp.logical_and(here, h > 0), activate(hc[0, j]), 0.0)
        act_r = jnp.where(jnp.logical_and(here, h < HEIGHT - 1), activate(hc[1, j]), 0.0)
        for half in range(2):
            lanes = slice(128 * half, 128 * half + 128)
            pad = pads[half]
            for f in range(8):
                pad[32 * f + 8 : 32 * f + 24, :] = act[16 * f : 16 * f + 16, lanes]
            pad[pl.ds(7, 8, stride=32), :] = act_l[:, lanes]
            pad[pl.ds(24, 8, stride=32), :] = act_r[:, lanes]
            for f in range(8):
                acts[0, 2 + f, j, :, lanes] = pad[32 * f + 7 : 32 * f + 23, :].astype(BF16)
                acts[2, 2 + f, j, :, lanes] = pad[32 * f + 9 : 32 * f + 25, :].astype(BF16)

    def total_of(parts):
        return jnp.sum(parts[...].astype(F32), axis=0).astype(BF16)

    arrived(ALONG_X, rx.at[pl.ds(0, 3)])
    px[...] = total_of(rx)
    for dz in (1, 0):
        for k in (6, 2, 5, 7, 1, 3, 4, 0):
            if dz or k:
                to_z, to_h = lax.rem(zhi + dz, 2), lax.rem(h + k, 8)
                send(px.at[to_z * 8 + to_h], qx.at[zhi * 8 + h], LAST_X, (to_z * 4 + x_at) * 2 + core, to_h)
    arrived(ALONG_Y, ry.at[pl.ds(0, 3)])
    py[...] = total_of(ry)
    for dz in (1, 0):
        for k in (6, 2, 5, 7, 1, 3, 4, 0):
            if dz or k:
                to_z, to_t = lax.rem(zlo + dz, 2), lax.rem(t + k, 8)
                send(py.at[to_z * 8 + to_t], qy.at[zlo * 8 + t], LAST_Y, to_t * 2 + core, to_z * 4 + y_at)
    arrived(ALONG_Z, rz.at[pl.ds(0, 3)])
    pz[...] = total_of(rz)
    for dx in (2, 1, 3, 0):
        for dy in (2, 1, 3, 0):
            if dx or dy:
                to_x, to_y = lax.rem(x_at + dx, 4), lax.rem(y_at + dy, 4)
                send(pz.at[to_x * 4 + to_y], qz.at[x_at * 4 + y_at], LAST_Z, (zhi * 4 + to_x) * 2 + core, zlo * 4 + to_y)

    def extra(tile, at, to_t, to_h):
        here = jnp.logical_and(to_t == t, to_h == h)

        @pl.when(jnp.logical_not(here))
        def _():
            send(tile, qe.at[at], LAST_E, to_t * 2 + core, to_h)

        @pl.when(here)
        def _():
            qe[at] = tile[...]

    for i in range(2):
        to_t = 4 * i + x_at
        extra(px.at[16 + i], zhi * 8 + h, to_t, to_t)
        to_t = 4 * i + lax.rem(y_at + 1, 4)
        extra(py.at[16 + i], zlo * 8 + t, to_t, lax.rem(to_t + EXTRA[1], 8))
        to_t = 4 * zhi + jnp.where(zhi == zlo, 2, 0) + i
        extra(pz.at[16 + i], x_at * 4 + y_at, to_t, lax.rem(to_t + EXTRA[2], 8))
    qx[zhi * 8 + h] = px[zhi * 8 + h]
    qy[zlo * 8 + t] = py[zlo * 8 + t]
    qz[x_at * 4 + y_at] = pz[x_at * 4 + y_at]

    arrived(AFF1, at1.at[pl.ds(0, 7)])
    at[...] = jnp.sum(at1[...], axis=0)

    for to_tm in others_tm():
        send(at, at2.at[tm], AFF2, to_tm, h)

    at2[tm] = at[...]

    for p in range(2):
        even = jnp.zeros((256, 128), F32)
        odd = jnp.zeros((256, 128), F32)
        for rc, dr in ((0, -1), (1, 0)) if p == 0 else ((2, 0), (3, 1)):
            for a in range(3):
                lhs = [acts[dc, a : a + 8, pl.ds(2 * core + 1 + dr, 2)].reshape(256, 256) for dc in range(3)]
                both = jnp.dot(lhs[1], wc[a, rc, :, 128:384], preferred_element_type=F32)
                even = even + both[:, :128] + jnp.dot(lhs[0], wc[a, rc, :, 0:128], preferred_element_type=F32)
                odd = odd + both[:, 128:] + jnp.dot(lhs[2], wc[a, rc, :, 384:512], preferred_element_type=F32)
        for f in range(8):
            for row in range(2):
                at_row = (f * 4 + 2 * row + p) * 32
                here = (f * 2 + row) * 16
                d_buf[pl.ds(at_row, 16, stride=2), :] = even[here : here + 16]
                d_buf[pl.ds(at_row + 1, 16, stride=2), :] = odd[here : here + 16]
    dec[...] = d_buf[0:1024, :].astype(BF16).reshape(8, 4, 32, 128)

    owners = [lax.rem(t + shift_h, 8) for shift_h in EXTRA]
    has_extra = jnp.logical_or(h == owners[0], jnp.logical_or(h == owners[1], h == owners[2]))
    for i, (kind, parts) in enumerate(((LAST_X, qx), (LAST_Y, qy), (LAST_Z, qz))):
        arrived(kind, parts.at[pl.ds(0, 15)])
        ag_s[i] = total_of(parts)

    @pl.when(has_extra)
    def _():
        arrived(LAST_E, qe.at[pl.ds(0, 15)])
        ag_s[3] = total_of(qe)

    @pl.when(jnp.logical_not(has_extra))
    def _():
        ag_s[3] = jnp.zeros((16, 128), BF16)

    for to_h in others_h():
        send(ag_s, ag_r.at[h], GATHER, tm, to_h)

    ag_r[h] = ag_s[...]

    arrived(AFF2, at2.at[pl.ds(0, 15)])
    total = jnp.sum(at2[...], axis=0)
    aff[0:1, 0:128] = total[0:1]
    aff[0:1, 128:256] = total[1:2]
    aff[1:2, 0:128] = total[2:3]
    aff[1:2, 128:256] = total[3:4]

    arrived(GATHER, ag_r.at[pl.ds(0, 7)])
    for k in range(8):
        for i in range(3):
            gw[8 * i + k] = ag_r[k, i].astype(F32)
    for i in range(3):
        gw[24 + i] = ag_r[owners[i], 3].astype(F32)

    sent(BLOCKS, xraw.at[pl.ds(0, 7), pl.ds(0, 2)])
    sent(COT_PAIR, cpart)
    sent(COT_ROWS, cedge.at[0])
    sent(COT_COLS, ch.at[:, pl.ds(0, 5)])
    sent(ROWS_ON, cedge.at[0])
    sent(COLS_ON, ch.at[:, pl.ds(0, 5)])
    sent(X_PAIR, xraw.at[:, pl.ds(0, 2)])
    sent(X_ROWS, xraw.at[:, pl.ds(0, 1)])
    sent(X_COLS, hc.at[:, pl.ds(0, 3)])
    sent(X_COLS_ON, hc.at[:, pl.ds(0, 1)])
    for kind, parts in ((ALONG_X, rx), (ALONG_Y, ry), (ALONG_Z, rz)):
        sent(kind, parts.at[pl.ds(0, 3)])
    for kind, parts in ((LAST_X, qx), (LAST_Y, qy), (LAST_Z, qz)):
        sent(kind, parts.at[pl.ds(0, 15)])
    sent(LAST_E, qe.at[pl.ds(0, 5)])

    @pl.when(jnp.logical_not(has_extra))
    def _():
        sent(LAST_E, qe.at[0])

    sent(GATHER, ag_r.at[pl.ds(0, 7)])
    sent(STATS1, st1.at[pl.ds(0, 7)])
    sent(STATS2, st2.at[pl.ds(0, 15)])
    sent(AFF1, at1.at[pl.ds(0, 7)])
    sent(AFF2, at2.at[pl.ds(0, 15)])


def deliver(*refs):
    copies = [pltpu.make_async_copy(refs[i], refs[3 + i], refs[6].at[i]) for i in range(3)]
    for copy in copies:
        copy.start()
    for copy in copies:
        copy.wait()


def per_device(coarse, gain, bias, weight, cotangent):
    taps = jnp.transpose(weight, (1, 2, 3, 0, 4)).reshape(27, 256, 128)
    vmem = pl.BlockSpec(memory_space=pltpu.VMEM)
    vm = pltpu.VMEM
    decoded, grad_weight, grad_affine = pl.pallas_call(
        kernel,
        out_shape=(
            jax.ShapeDtypeStruct((8, 4, 32, 128), BF16),
            jax.ShapeDtypeStruct((27, 16, 128), F32),
            jax.ShapeDtypeStruct((2, 256), F32),
        ),
        in_specs=[pl.BlockSpec(memory_space=pltpu.HBM)] * 5,
        out_specs=(vmem, vmem, vmem),
        scratch_shapes=[
            vm((2, 128, 256), BF16),
            vm((1, 256), F32),
            vm((1, 256), F32),
            vm((27, 256, 128), BF16),
            vm((8, 4, 32, 128), BF16),
            pltpu.SemaphoreType.DMA((5,)),
            vm((3, 4, 256, 512), BF16),
            vm((1, 128), F32),
            vm((1, 128), F32),
            vm((8, 1, 128), F32),
            vm((16, 1, 128), F32),
            vm((4, 128), F32),
            vm((4, 128), F32),
            vm((8, 4, 128), F32),
            vm((16, 4, 128), F32),
            vm((8, 6, 16, 256), BF16),
            vm((2, 144, 128), F32),
            vm((2, 2, 8, 256), F32),
            vm((2, 6, 8, 256), F32),
            vm((3, 10, 6, 16, 256), BF16),
            vm((288, 128), F32),
            vm((288, 128), F32),
            vm((8, 2, 16, 512), BF16),
            vm((8, 4, 32, 128), BF16),
            vm((2, 8, 1, 32, 128), BF16),
            vm((2, 4, 8, 128), F32),
            vm((2, 10, 8, 128), F32),
            vm((10 * 8 * 48 + 64, 128), F32),
            vm((9, 10, 4, 16, 128), BF16),
            *[vm((4, 18, 16, 128), BF16)] * 6,
            *[vm((18, 16, 128), BF16)] * 3,
            *[vm((16, 16, 128), BF16)] * 4,
            vm((4, 16, 128), BF16),
            vm((8, 4, 16, 128), BF16),
            vm((1056, 128), F32),
            pltpu.SemaphoreType.DMA((22,)),
            pltpu.SemaphoreType.DMA((22,)),
        ],
        compiler_params=pltpu.CompilerParams(
            collective_id=0, has_side_effects=True, vmem_limit_bytes=48 * 2**20
        ),
        cost_estimate=pl.CostEstimate(flops=2 * 10**9, bytes_accessed=4 * 10**6, transcendentals=300000),
    )(*[
        pltpu.with_memory_space_constraint(x, pltpu.HBM)
        for x in (coarse.reshape(2, 128, 256), gain.reshape(1, 256), bias.reshape(1, 256), taps, cotangent)
    ])
    decoded, grad_weight, grad_affine = pl.pallas_call(
        deliver,
        out_shape=(
            jax.ShapeDtypeStruct((8, 4, 32, 128), BF16),
            jax.ShapeDtypeStruct((27, 16, 128), F32),
            jax.ShapeDtypeStruct((2, 256), F32),
        ),
        in_specs=[pl.BlockSpec(memory_space=pltpu.VMEM)] * 3,
        out_specs=[pl.BlockSpec(memory_space=pl.ANY)] * 3,
        scratch_shapes=[pltpu.SemaphoreType.DMA((3,))],
        compiler_params=pltpu.CompilerParams(vmem_limit_bytes=8 * 2**20),
    )(decoded, grad_weight, grad_affine)
    grad_weight = jnp.transpose(grad_weight.reshape(3, 3, 3, 16, 128), (3, 0, 1, 2, 4))
    return decoded, grad_weight, grad_affine


def solution(mesh):
    return jax.shard_map(
        per_device,
        mesh=mesh,
        in_specs=(P("height", "tm", None, None), P(), P(), P(), P(None, "tm", "height", None)),
        out_specs=(P(None, "tm", "height", None), P("tm", None, None, None, None), P()),
        check_vma=False,
    )
```
